32 devices in a mesh: dp: 8 (over z, x), mp: 4 (over y, core).
Axes of the slice: x: 2, y: 2, z: 4, core: 2. Of those that a mesh axis runs over, the one named last changes fastest.
Arguments:
- lap_vectors: float32 [8, 1024, 16], P('dp'), may hold values from -3 to 3
- eig_index: int32 [8, 1024, 2], P('dp'), may hold values from 0 to 1023, as said below
- type_ids: int32 [8, 1024], P('dp'), may hold values from 0 to 191
- seg_ids: int32 [8, 1024], P('dp'), may hold values from 0 to 24, as said below
- targets: float32 [8, 24], P('dp'), may hold values from 3 to 7
- layer_weights: float32 [768, 4608], P('dp', 'mp')
- left_stats: float32 [768, 24, 96], P('dp', 'mp')
- right_stats: float32 [8, 24, 192, 192], P('dp', 'mp')
- left_roots: float32 [768, 24, 96], P('dp', 'mp')
- right_roots: float32 [8, 24, 192, 192], P('dp', 'mp')
- tables: float32 [224, 768], replicated, may hold values from -2.4 to 2.4
- tables_m: float32 [224, 768], replicated
- tables_v: float32 [224, 768], replicated
- head_weight: float32 [768, 768], replicated, may hold values from -0.21875 to 0.21875
- head_m: float32 [768, 768], replicated
- head_v: float32 [768, 768], replicated
- vectors: float32 [11, 768], replicated
- vectors_m: float32 [11, 768], replicated
- vectors_v: float32 [11, 768], replicated
Outputs:
- loss_sum: float32 [], replicated
- count: float32 [], replicated
- grad_norm: float32 [], replicated
- layer_grad: float32 [768, 4608], P('dp', 'mp')
- layer_new: float32 [768, 4608], P('dp', 'mp')
- left_new: float32 [768, 24, 96], P('dp', 'mp')
- right_new: float32 [8, 24, 192, 192], P('dp', 'mp')
- tables_m_new: float32 [224, 768], replicated
- tables_v_new: float32 [224, 768], replicated
- tables_new: float32 [224, 768], replicated
- head_m_new: float32 [768, 768], replicated
- head_v_new: float32 [768, 768], replicated
- head_new: float32 [768, 768], replicated
- vectors_m_new: float32 [11, 768], replicated
- vectors_v_new: float32 [11, 768], replicated
- vectors_new: float32 [11, 768], replicated
The draws below stay inside these ranges and needn't reach their ends.
Inputs may be any that keep to these rules, and one draw needn't show every extreme that they name: `seg_ids`: each row holds 1 to 24 molecules of 16 to 40 positions, laid end to end from position 0 and numbered 0, 1, ... in order, then padding; the last row holds exactly 24 molecules. `eig_index`: both entries equal the position itself except at a molecule's edge positions (those past its first 1 + (length - 1) // 2 positions), where they name node positions of the same molecule.
All inputs are finite; a program needn't handle non-finite values.
Results may differ from the reference program's by a relative error of at most 0.02.
Values may be sent and summed in bfloat16 or wider, within the bound.
No kernel may reach another device: no remote copies, remote signals or barrier semaphores. Data moves between devices by JAX's collectives and lax.ppermute only.
A program may use at most 192 MiB of HBM per device.

```python
import math
import jax
import jax.numpy as jnp
from jax import lax

D = 768
HEADS = 32
HEAD_DIM = 24
LAP = 16
TYPES = 192
LEN = 1024
MOLMIN = 16
MOLMAX = 40
STEP = 10
MAXSEG = 24
ROWS = 8
CB = 192
ROWB = 96
N_DP = 8
N_MP = 4


def grad_size():
    return 0.25 / math.sqrt(7 * D * D + (TYPES + 2 * LAP) * D + 11 * D)


def layout(key):
    key_count, key_length, key_first, key_second = jax.random.split(key, 4)
    row_index = jnp.arange(ROWS, dtype=jnp.int32)
    half_rows = ROWS // 2
    pair_index = row_index % half_rows
    upper_count = MAXSEG // 3 + (MAXSEG - MAXSEG // 3) * pair_index // max(half_rows - 1, 1)
    lower_count = jnp.maximum(1, upper_count // 4 + jax.random.randint(key_count, (ROWS,), 0, 2))
    mol_count = jnp.minimum(jnp.where(row_index >= half_rows, upper_count, lower_count), MAXSEG)
    mol_count = jnp.where(row_index == ROWS - 1, MAXSEG, mol_count)
    slot_index = jnp.arange(MAXSEG, dtype=jnp.int32)
    lengths = jax.random.randint(key_length, (ROWS, MAXSEG), MOLMIN, MOLMAX + 1)
    lengths = jnp.where(slot_index[None, :] < mol_count[:, None], lengths, 0)
    mol_ends = jnp.cumsum(lengths, 1)
    begins = mol_ends - lengths
    position = jnp.arange(LEN, dtype=jnp.int32)
    inside = (position[None, None, :] >= begins[:, :, None]) & (position[None, None, :] < mol_ends[:, :, None])
    in_mol = jnp.any(inside, 1)
    seg = jnp.sum(jnp.where(inside, slot_index[None, :, None], 0), 1) + jnp.where(in_mol, 0, MAXSEG)
    begin_tok = jnp.sum(jnp.where(inside, begins[:, :, None], 0), 1)
    length_tok = jnp.sum(jnp.where(inside, lengths[:, :, None], 0), 1)
    local_index = position[None, :] - begin_tok
    node_count = jnp.maximum((length_tok - 1) // 2, 1)
    edge_flag = in_mol & (local_index > node_count)
    pick_first = begin_tok + 1 + jax.random.randint(key_first, (ROWS, LEN), 0, node_count)
    pick_second = begin_tok + 1 + jax.random.randint(key_second, (ROWS, LEN), 0, node_count)
    own_position = jnp.broadcast_to(position[None, :], (ROWS, LEN))
    return (seg, jnp.where(edge_flag, pick_first, own_position), jnp.where(edge_flag, pick_second, own_position))


def draw_seg_ids(key, part):
    seg, _, _ = layout(key)
    return seg.astype(jnp.int32)


def draw_eig_index(key, part):
    _, first_pick, second_pick = layout(key)
    return jnp.stack([first_pick, second_pick], -1).astype(jnp.int32)


def draw_layer_weights(key, part):
    key = jax.random.fold_in(key, 11)
    columns = jnp.arange(6 * D)
    which = columns // CB % 6
    col_scale = jnp.where(which == 3, 4.0, jnp.where(which == 5, 2.0, 1.0)) / math.sqrt(D)
    return jax.random.normal(key, (D, 6 * D), jnp.float32) * col_scale[None, :]


def square_blocks(key, number, order, size):
    key_diag, key_off = jax.random.split(key)
    diagonal = jnp.exp(jax.random.uniform(key_diag, (number, order), jnp.float32, 0.0, math.log(4.0)))
    off_diag = jax.random.uniform(key_off, (number, order, order), jnp.float32, -1.0, 1.0)
    off_diag = (off_diag + jnp.swapaxes(off_diag, 1, 2)) * (0.6 / math.sqrt(order))
    identity = jnp.eye(order, dtype=jnp.float32)
    return (identity[None] * diagonal[:, :, None] + off_diag * (1.0 - identity[None])) * size


def left_layout(values):
    six_groups = 6 * (D // CB)
    return values.reshape(ROWS, six_groups, ROWB, ROWB).transpose(0, 2, 1, 3).reshape(D, six_groups, ROWB)


def draw_left_stats(key, part):
    key = jax.random.fold_in(key, 5)
    return left_layout(square_blocks(key, ROWS * 6 * (D // CB), ROWB, CB * grad_size() ** 2))


def draw_left_roots(key, part):
    key = jax.random.fold_in(key, 6)
    return left_layout(square_blocks(key, ROWS * 6 * (D // CB), ROWB, (CB * grad_size() ** 2) ** (-0.25)))


def draw_right_stats(key, part):
    key = jax.random.fold_in(key, 7)
    values = square_blocks(key, ROWS * 6 * (D // CB), CB, ROWB * grad_size() ** 2)
    return values.reshape(ROWS, 6 * (D // CB), CB, CB)


def draw_right_roots(key, part):
    key = jax.random.fold_in(key, 8)
    values = square_blocks(key, ROWS * 6 * (D // CB), CB, (ROWB * grad_size() ** 2) ** (-0.25))
    return values.reshape(ROWS, 6 * (D // CB), CB, CB)


def first_moment(key, shape, size):
    return jax.random.normal(key, shape, jnp.float32) * size * (0.1 / 0.9)


def second_moment(key, shape, size):
    spread = jnp.exp(jax.random.uniform(key, shape, jnp.float32, 0.0, math.log(4.0)))
    return spread * (0.01 / 0.99) * size * size


def draw_tables_m(key, part):
    key = jax.random.fold_in(key, 21)
    return first_moment(key, (TYPES + 2 * LAP, D), 0.3 * grad_size())


def draw_tables_v(key, part):
    key = jax.random.fold_in(key, 22)
    return second_moment(key, (TYPES + 2 * LAP, D), 0.3 * grad_size())


def draw_head_m(key, part):
    key = jax.random.fold_in(key, 23)
    return first_moment(key, (D, D), 2.0 * grad_size())


def draw_head_v(key, part):
    key = jax.random.fold_in(key, 24)
    return second_moment(key, (D, D), 2.0 * grad_size())


def draw_vectors_m(key, part):
    key = jax.random.fold_in(key, 25)
    return first_moment(key, (11, D), 6.0 * grad_size())


def draw_vectors_v(key, part):
    key = jax.random.fold_in(key, 26)
    return second_moment(key, (11, D), 6.0 * grad_size())


def rising_gains(key, low_end, ratio):
    spot = jnp.arange(D, dtype=jnp.float32) / (D - 1.0)
    rough = jax.random.uniform(key, (11, D), jnp.float32, 0.8, 1.25)
    return rough * (low_end * jnp.exp(spot * math.log(ratio)))[None, :]


def draw_vectors(key, part):
    key = jax.random.fold_in(key, 31)
    key_gain, key_other = jax.random.split(key)
    gain_rows = rising_gains(key_gain, 0.5, 4.0)
    normal_rows = jax.random.normal(key_other, (11, D), jnp.float32)
    row_index = jnp.arange(11)[:, None]
    row_scale = jnp.where((row_index == 1) | (row_index == 3) | (row_index == 5) | (row_index == 9), 0.2, 0.5)
    row_scale = jnp.where(row_index == 10, 1.0 / math.sqrt(D), row_scale)
    is_gain = (row_index == 0) | (row_index == 2) | (row_index == 4)
    return jnp.where(is_gain, gain_rows, normal_rows * row_scale)


def set_ends(result, rng, low, largest):
    place = [jax.random.randint(jax.random.fold_in(rng, axis), (), 0, length) for axis, length in enumerate(result.shape)]
    widest = result.shape.index(max(result.shape))
    beside = place[:widest] + [(place[widest] + 1) % result.shape[widest]] + place[widest + 1:]
    return result.at[tuple(place)].set(low).at[tuple(beside)].set(largest)


def block_scale(key, shape, cuts, smallest, top_value):
    level = 1.0
    for dim, blocks in cuts:
        steps = jax.random.uniform(jax.random.fold_in(jax.random.fold_in(key, 6), dim), (blocks,), jnp.float32, smallest / len(cuts), top_value / len(cuts))
        level = level * jnp.repeat(jnp.exp(steps), shape[dim] // blocks).reshape((-1,) + (1,) * (len(shape) - 1 - dim))
    return level


def normal_values(key, dims, deviation, limit, cuts=(), kind=jnp.bfloat16):
    drawn = deviation * jax.random.normal(key, dims, jnp.float32)
    if cuts:
        drawn = drawn * block_scale(key, dims, cuts, -0.22, 0.18)
    return jnp.clip(drawn, -limit, limit).astype(kind)


def setup_inputs(seed: int = 0) -> dict:
    keys = jax.random.split(jax.random.key(seed), 20)
    lap_vectors = normal_values(keys[0], (ROWS, LEN, LAP), 0.5, 3.0, ((0, 8),), jnp.float32)
    eig_index = draw_eig_index(jax.random.fold_in(keys[19], 71), 0)
    type_ids = set_ends(jax.random.randint(keys[2], (ROWS, LEN), 0, TYPES), jax.random.fold_in(keys[2], 1), 0, TYPES - 1).astype(jnp.int32)
    seg_ids = draw_seg_ids(jax.random.fold_in(keys[19], 71), 0)
    targets = jnp.clip(3.0 + 4.0 * jax.random.uniform(keys[4], (ROWS, MAXSEG), jnp.float32) ** block_scale(keys[4], (ROWS, MAXSEG), ((0, 8),), -0.2, 0.2), 3.0, 7.0)
    layer_weights = draw_layer_weights(jax.random.fold_in(keys[19], 71), 0)
    left_stats = draw_left_stats(jax.random.fold_in(keys[19], 71), 0)
    right_stats = draw_right_stats(jax.random.fold_in(keys[19], 71), 0)
    left_roots = draw_left_roots(jax.random.fold_in(keys[19], 71), 0)
    right_roots = draw_right_roots(jax.random.fold_in(keys[19], 71), 0)
    tables = normal_values(keys[10], (TYPES + 2 * LAP, D), 0.4, 2.4, (), jnp.float32)
    tables_m = draw_tables_m(jax.random.fold_in(keys[19], 71), 0)
    tables_v = draw_tables_v(jax.random.fold_in(keys[19], 71), 0)
    head_weight = normal_values(keys[13], (D, D), D ** -0.5, 0.21875, (), jnp.float32)
    head_m = draw_head_m(jax.random.fold_in(keys[19], 71), 0)
    head_v = draw_head_v(jax.random.fold_in(keys[19], 71), 0)
    vectors = draw_vectors(jax.random.fold_in(keys[19], 71), 0)
    vectors_m = draw_vectors_m(jax.random.fold_in(keys[19], 71), 0)
    vectors_v = draw_vectors_v(jax.random.fold_in(keys[19], 71), 0)
    return {"lap_vectors": lap_vectors, "eig_index": eig_index, "type_ids": type_ids, "seg_ids": seg_ids, "targets": targets, "layer_weights": layer_weights, "left_stats": left_stats, "right_stats": right_stats, "left_roots": left_roots, "right_roots": right_roots, "tables": tables, "tables_m": tables_m, "tables_v": tables_v, "head_weight": head_weight, "head_m": head_m, "head_v": head_v, "vectors": vectors, "vectors_m": vectors_m, "vectors_v": vectors_v}


@jax.custom_vjp
def low(v):
    return lax.optimization_barrier(v.astype(jnp.bfloat16)).astype(jnp.float32)

@jax.custom_vjp
def low_back(v):
    return v

def low_keep(v):
    return (low(v), None)

def low_pass(kept, grad):
    return (grad,)

def back_keep(v):
    return (v, None)

def back_low(kept, grad):
    return (low(grad),)
low.defvjp(low_keep, low_pass)
low_back.defvjp(back_keep, back_low)
HIGHEST_PREC = lax.Precision.HIGHEST
NORM_EPS = 1e-05
CLIP = 0.25
STATS_DECAY = 0.95
RATE_LAYER = 0.15
RATE_TABLES = 0.15
RATE_HEAD = 0.01
RATE_VECTORS = 0.2
BETA_ONE = 0.9
BETA_TWO = 0.99
ADAM_EPS = 1e-08
WEIGHT_DECAY = 0.01
MASKED = -1000000000.0

def layer_norm(values, scale_row, shift_row):
    center = values - lax.optimization_barrier(jnp.mean(values, -1, keepdims=True))
    spread = lax.optimization_barrier(jnp.mean(center * center, -1, keepdims=True))
    return center * lax.rsqrt(spread + NORM_EPS) * scale_row + shift_row

def softmax_rows(scores):
    row_peak = lax.optimization_barrier(jnp.max(scores, -1, keepdims=True))
    exp_scores = jnp.exp(scores - row_peak)
    return exp_scores / lax.optimization_barrier(jnp.sum(exp_scores, -1, keepdims=True))

def row_loss(params, lap_row, eig_row, type_row, seg_row, target_row):
    tables, head_weight, vectors, layer = params
    group_heads = HEADS // N_MP
    lap_pair = low(jnp.concatenate([lap_row[eig_row[:, 0]], lap_row[eig_row[:, 1]]], -1))
    node_flag = eig_row[:, 0] == eig_row[:, 1]
    previous = jnp.concatenate([jnp.full((1,), -1, jnp.int32), seg_row[:-1]])
    is_start = (seg_row != MAXSEG) & (seg_row != previous)
    embedded = tables[type_row] + jnp.dot(lap_pair, low(tables[TYPES:]), precision=HIGHEST_PREC)
    embedded = embedded + jnp.where(node_flag[:, None], vectors[6], vectors[7])
    resid_zero = low_back(jnp.where(is_start[:, None], vectors[8], embedded))
    weights = low(layer).reshape(D, N_MP, 6, CB)
    normed_one = low(layer_norm(resid_zero, vectors[0], vectors[1]))
    normed_groups = low_back(jnp.broadcast_to(normed_one, (N_MP, LEN, D)))
    projected = jnp.einsum('mtd,dmjc->mjtc', normed_groups, weights[:, :, 0:3], precision=HIGHEST_PREC)
    projected = low(low_back(projected))
    queries = projected[:, 0].reshape(N_MP, LEN, group_heads, HEAD_DIM)
    attend_keys = projected[:, 1].reshape(N_MP, LEN, group_heads, HEAD_DIM)
    values = projected[:, 2].reshape(N_MP, LEN, group_heads, HEAD_DIM)
    scores = jnp.einsum('mqhe,mkhe->mhqk', queries, attend_keys, precision=HIGHEST_PREC)
    scores = low_back(scores * HEAD_DIM ** (-0.5))
    same_mol = seg_row[:, None] == seg_row[None, :]
    scores = jnp.where(same_mol[None, None], scores, MASKED)
    attn_probs = low(softmax_rows(scores))
    context = jnp.einsum('mhqk,mkhe->mqhe', attn_probs, values, precision=HIGHEST_PREC).reshape(N_MP, LEN, CB)
    context = low(low_back(context))
    attn_terms = low(jnp.einsum('mtc,dmc->mtd', context, weights[:, :, 3], precision=HIGHEST_PREC))
    resid_one = resid_zero + low_back(lax.optimization_barrier(jnp.sum(attn_terms, 0)))
    normed_two = low(layer_norm(resid_one, vectors[2], vectors[3]))
    normed_groups_two = low_back(jnp.broadcast_to(normed_two, (N_MP, LEN, D)))
    hidden = low_back(jnp.einsum('mtd,dmc->mtc', normed_groups_two, weights[:, :, 4], precision=HIGHEST_PREC))
    activated = low(jax.nn.gelu(hidden))
    ffn_terms = low(jnp.einsum('mtc,dmc->mtd', activated, weights[:, :, 5], precision=HIGHEST_PREC))
    resid_two = resid_one + low_back(lax.optimization_barrier(jnp.sum(ffn_terms, 0)))
    mol_index = jnp.arange(MAXSEG, dtype=jnp.int32)
    select = (seg_row[None, :] == mol_index[:, None]) & is_start[None, :]
    slot_place = lax.optimization_barrier(jnp.sum(jnp.where(select, jnp.arange(LEN, dtype=jnp.int32)[None, :], 0), 1))
    present = jnp.any(select, 1)
    head_in = low(layer_norm(resid_two[slot_place], vectors[4], vectors[5]))
    head_mid = low_back(jnp.dot(head_in, low(head_weight), precision=HIGHEST_PREC) + vectors[9])
    predicted = jnp.dot(low(jax.nn.gelu(head_mid)), low(vectors[10]), precision=HIGHEST_PREC)
    pred_error = predicted - target_row
    return jnp.sum(jnp.where(present, jnp.sqrt(pred_error * pred_error + 1.0) - 1.0, 0.0))

def adam_update(weight, first, second, grad, rate):
    first_new = BETA_ONE * first + (1.0 - BETA_ONE) * grad
    second_new = BETA_TWO * second + (1.0 - BETA_TWO) * grad * grad
    fixed_one = 1.0 - BETA_ONE ** STEP
    fixed_two = 1.0 - BETA_TWO ** STEP
    update_dir = first_new / fixed_one / (jnp.sqrt(second_new / fixed_two) + ADAM_EPS)
    return (first_new, second_new, weight - rate * (update_dir + WEIGHT_DECAY * weight))

def reference(lap_vectors, eig_index, type_ids, seg_ids, targets, layer_weights, left_stats, right_stats, left_roots, right_roots, tables, tables_m, tables_v, head_weight, head_m, head_v, vectors, vectors_m, vectors_v):
    previous = jnp.concatenate([jnp.full((ROWS, 1), -1, jnp.int32), seg_ids[:, :-1]], 1)
    count = jnp.sum(((seg_ids != MAXSEG) & (seg_ids != previous)).astype(jnp.float32))

    def total_loss(params):

        def add_row(running, row_data):
            return (running + jax.checkpoint(row_loss)(params, row_data[0], row_data[1], row_data[2], row_data[3], row_data[4]), None)
        summed, _ = lax.scan(add_row, jnp.zeros((), jnp.float32), (lap_vectors, eig_index, type_ids, seg_ids, targets))
        return summed
    params = (tables, head_weight, vectors, layer_weights)
    loss_sum, pull_back = jax.vjp(total_loss, params)
    gradients = pull_back(jnp.ones((), jnp.float32) / count)[0]
    squares = jnp.zeros((), jnp.float32)
    for grad in gradients:
        squares = squares + jnp.sum(grad * grad)
    grad_norm = jnp.sqrt(squares)
    factor = CLIP / jnp.maximum(grad_norm, CLIP)
    grad_tables = gradients[0] * factor
    grad_head = gradients[1] * factor
    grad_vectors = gradients[2] * factor
    layer_grad = gradients[3] * factor
    blocks = layer_grad.reshape(N_DP, ROWB, N_MP * 6, CB).transpose(0, 2, 1, 3)
    current = layer_weights.reshape(N_DP, ROWB, N_MP * 6, CB).transpose(0, 2, 1, 3)
    left_old = left_stats.reshape(N_DP, ROWB, N_MP * 6, ROWB).transpose(0, 2, 1, 3)
    left_root = left_roots.reshape(N_DP, ROWB, N_MP * 6, ROWB).transpose(0, 2, 1, 3)
    left_block = STATS_DECAY * left_old + (1.0 - STATS_DECAY) * jnp.einsum('pbic,pbkc->pbik', blocks, blocks, precision=HIGHEST_PREC)
    right_new = STATS_DECAY * right_stats + (1.0 - STATS_DECAY) * jnp.einsum('pbic,pbid->pbcd', blocks, blocks, precision=HIGHEST_PREC)
    shaped = jnp.einsum('pbik,pbkc->pbic', left_root, blocks, precision=HIGHEST_PREC)
    shaped = jnp.einsum('pbic,pbcd->pbid', shaped, right_roots, precision=HIGHEST_PREC)
    updated = current - RATE_LAYER * (shaped + WEIGHT_DECAY * current)
    layer_new = updated.transpose(0, 2, 1, 3).reshape(D, 6 * D)
    left_new = left_block.transpose(0, 2, 1, 3).reshape(D, N_MP * 6, ROWB)
    tables_m_new, tables_v_new, tables_new = adam_update(tables, tables_m, tables_v, grad_tables, RATE_TABLES)
    head_m_new, head_v_new, head_new = adam_update(head_weight, head_m, head_v, grad_head, RATE_HEAD)
    vectors_m_new, vectors_v_new, vectors_new = adam_update(vectors, vectors_m, vectors_v, grad_vectors, RATE_VECTORS)
    return (loss_sum, count, grad_norm, layer_grad, layer_new, left_new, right_new, tables_m_new, tables_v_new, tables_new, head_m_new, head_v_new, head_new, vectors_m_new, vectors_v_new, vectors_new)
```

```python
import functools

import jax
import jax.numpy as jnp
from jax import lax
from jax.experimental import pallas as pl
from jax.experimental.pallas import tpu as pltpu
from jax.sharding import PartitionSpec as P

HEAD_DIM = 24
TYPES = 192
STEP = 10
NORM_EPS = 1e-05
CLIP = 0.25
STATS_DECAY = 0.95
RATE_LAYER = 0.15
RATE_TABLES = 0.15
RATE_HEAD = 0.01
RATE_VECTORS = 0.2
BETA_ONE = 0.9
BETA_TWO = 0.99
ADAM_EPS = 1e-08
WEIGHT_DECAY = 0.01
MASKED = -1000000000.0
GELU_C = 0.7978845608028654
GELU_A = 0.044715

BF = jnp.bfloat16
F32 = jnp.float32
I32 = jnp.int32
HIGHEST = lax.Precision.HIGHEST
NN = ((1,), (0,))
NT = ((1,), (1,))
TN = ((0,), (0,))
BLOCK = 256
FEATS = 256
MIB = 1024 * 1024


def dot(a, b, dims=NN, precision=None):
    return lax.dot_general(a, b, (dims, ((), ())), preferred_element_type=F32, precision=precision)


def iota(shape, dim):
    return lax.broadcasted_iota(I32, shape, dim)


def call(kernel, outs, ins, scratch=(), flops=0, vmem=40, in_specs=None, aliases=None):
    moved = sum(x.size * x.dtype.itemsize for x in list(ins) + list(outs))
    full = pl.BlockSpec(memory_space=pltpu.VMEM)
    return pl.pallas_call(
        kernel,
        out_shape=tuple(outs),
        in_specs=in_specs or [full] * len(ins),
        out_specs=tuple([full] * len(outs)),
        scratch_shapes=list(scratch),
        compiler_params=pltpu.CompilerParams(vmem_limit_bytes=vmem * MIB),
        cost_estimate=pl.CostEstimate(flops=flops, bytes_accessed=moved, transcendentals=0),
    )(*ins)


def sds(shape, dtype):
    return jax.ShapeDtypeStruct(shape, dtype)


def norm_parts(values):
    center = values - jnp.mean(values, -1, keepdims=True)
    spread = jnp.mean(center * center, -1, keepdims=True)
    inverse = lax.rsqrt(spread + NORM_EPS)
    return center * inverse, inverse


def norm_back(grad, hat, inverse, gain):
    scaled = grad * gain
    mean_one = jnp.mean(scaled, -1, keepdims=True)
    mean_two = jnp.mean(scaled * hat, -1, keepdims=True)
    return inverse * (scaled - mean_one - hat * mean_two)


def gelu_pair(x):
    t = jnp.tanh(GELU_C * (x + GELU_A * x * x * x))
    value = 0.5 * x * (1.0 + t)
    slope = 0.5 * (1.0 + t) + 0.5 * x * (1.0 - t * t) * (GELU_C * (1.0 + 3.0 * GELU_A * x * x))
    return value, slope


def tree(refs):
    parts = [r[...].astype(F32) for r in refs]
    while len(parts) > 1:
        parts = [parts[i] + parts[i + 1] for i in range(0, len(parts), 2)]
    return parts[0]


def three(x):
    high = x.astype(BF).astype(F32)
    mid = (x - high).astype(BF).astype(F32)
    return high, mid, x - high - mid


def assemble(pieces, whole, first_owner):
    rows = pieces[0].shape[0]
    if len(pieces) == 1:
        whole[...] = pieces[0][...]
        return
    for k, piece in enumerate(pieces):
        start = pl.multiple_of((first_owner ^ k) * rows, 16)
        whole[pl.ds(start, rows), :] = piece[...]


def embed_kernel(mols, lap, eig, kinds, seg, tables, vectors, at, normed, hats, invs, high, low, prev):
    length = seg.shape[1]
    width = vectors.shape[1]
    rows = tables.shape[0]
    tab = tables[...]
    tab_high = tab.astype(BF)
    high[0:rows, :] = tab_high
    rest = jnp.where(iota(tab.shape, 0) < TYPES, tab - tab_high.astype(F32), 0.0)
    low[0:rows, :] = rest.astype(BF)
    r = iota((FEATS - rows, width), 0)
    extra = jnp.where(r == 0, vectors[6:7, :], jnp.where(r == 1, vectors[7:8, :], jnp.where(r == 2, vectors[8:9, :], 0.0)))
    extra_high = extra.astype(BF)
    high[rows:FEATS, :] = extra_high
    low[rows:FEATS, :] = (extra - extra_high.astype(F32)).astype(BF)
    seg_row = seg[...]
    before = pltpu.roll(jnp.broadcast_to(seg_row, (8, length)), 1, 1)
    before = jnp.where(iota((8, length), 1) == 0, -1, before)
    prev[...] = before
    filled = jnp.sum((seg_row != mols).astype(F32)).astype(I32)
    normed[...] = jnp.zeros(normed.shape, BF)
    gain = vectors[0:1, :]
    shift = vectors[1:2, :]
    window = 2 * BLOCK

    def one_block(b, unused):
        start = pl.multiple_of(b * BLOCK, BLOCK)
        here = pl.ds(start, BLOCK)
        first = pl.multiple_of(jnp.clip(start - 128, 0, length - window), 128)
        source = iota((window, BLOCK), 0) + first
        one = eig[0:1, here]
        two = eig[1:2, here]
        near = lap[:, pl.ds(first, window)].astype(BF)
        pair_one = dot(near, (source == one).astype(F32).astype(BF))
        pair_two = dot(near, (source == two).astype(F32).astype(BF))
        seg_here = seg[0:1, here]
        begins = (seg_here != mols) & (seg_here != prev[0:1, here])
        kind = jnp.where(begins, -1, kinds[0:1, here])
        keep = jnp.where(begins, 0.0, 1.0)
        at[0:TYPES, here] = (iota((TYPES, BLOCK), 0) == kind).astype(F32).astype(BF)
        half = pair_one.shape[0]
        at[TYPES : TYPES + half, here] = (pair_one * keep).astype(BF)
        at[TYPES + half : rows, here] = (pair_two * keep).astype(BF)
        which = jnp.where(begins, 2, jnp.where(one == two, 0, 1))
        at[rows:FEATS, here] = (iota((FEATS - rows, BLOCK), 0) == which).astype(F32).astype(BF)
        picks = at[:, here]
        resid = dot(picks, high[...], TN) + dot(picks, low[...], TN)
        hat, inverse = norm_parts(resid)
        normed[here, :] = (hat * gain + shift).astype(BF)
        hats[here, :] = hat.astype(BF)
        invs[here, :] = jnp.broadcast_to(inverse, (BLOCK, 128))
        return 0

    lax.fori_loop(0, (filled + BLOCK - 1) // BLOCK, one_block, 0)


def attn_kernel(npiece, mols, heads, scale, *refs):
    normed, seg, vectors = refs[:3]
    ones = refs[3 : 3 + npiece]
    twos = refs[3 + npiece : 3 + 2 * npiece]
    part, probs, values, ctx_out, keyed, query_out, w1, w2 = refs[3 + 2 * npiece :]
    me = lax.axis_index("dp")
    assemble(ones, w1, me)
    assemble(twos, w2, me)
    width = vectors.shape[1]
    cols = heads * HEAD_DIM
    hat, _ = norm_parts(vectors[8:9, :])
    start_row = (hat * vectors[0:1, :] + vectors[1:2, :]).astype(BF)
    q = dot(jnp.broadcast_to(start_row, (16, width)), w1[:, 0:256])
    q = q.astype(BF).astype(F32)
    q = jnp.where(iota((16, 256), 1) < cols, q, 0.0)
    r = iota((16, 256), 0)
    head_of = iota((16, 256), 1) // HEAD_DIM
    query_out[...] = jnp.where(r == head_of, q, 0.0)[0:8, :]
    shifted = pltpu.roll(q, 64, 1)[0:1, :]
    r = iota((128, 256), 0)
    lane = iota((128, 256), 1) - 64
    pick = (lane >= 0) & ((r & 7) == lane // HEAD_DIM) & (r >= 64) & (r < 80)
    q_keys = jnp.where(pick, shifted, 0.0).astype(BF)
    u = dot(w1[:, 128:384], q_keys, NT)
    u_high = u.astype(BF)
    lane = iota(u.shape, 1)
    u_both = jnp.where(lane < 72, u_high.astype(F32), u - u_high.astype(F32))
    last = w1[:, 512:640].astype(F32)
    side = jnp.where(lane < 64, last, u_both).astype(BF)
    keyed[:, 0:128] = w1[:, 384:512]
    keyed[:, 128:256] = jnp.where(lane < 64, last, jnp.where(lane < 72, u * scale, 0.0)).astype(BF)
    normed_all = normed[...]
    values[:, 0:128] = dot(normed_all, w1[:, 384:512]).astype(BF)
    second = dot(normed_all, side)
    values[:, 128:256] = jnp.where(iota(second.shape, 1) < 64, second, 0.0).astype(BF)
    turned = second.T
    scores = (turned[64:72, :] + turned[72:80, :]) * scale
    seg_row = seg[...]
    length = seg_row.shape[1]
    mine = iota((mols, 1, length), 0) == seg_row[None]
    masked = jnp.where(mine, scores[None], MASKED)
    peak = jnp.max(masked, -1, keepdims=True)
    grown = jnp.where(mine, jnp.exp(masked - peak), 0.0)
    total = jnp.sum(grown, -1, keepdims=True)
    total = jnp.where(total > 0.0, total, 1.0)
    prob = (grown / total).reshape(mols * heads, length).astype(BF)
    probs[...] = prob
    wide = dot(prob, values[...])
    r = iota(wide.shape, 0) & (heads - 1)
    wide = jnp.where(r == iota(wide.shape, 1) // HEAD_DIM, wide, 0.0)
    ctx = jnp.sum(wide.reshape(mols, heads, 256), 1)
    ctx_out[...] = ctx.astype(BF)
    low = ctx.astype(BF)
    tail = pltpu.roll(ctx[:, 128:256], 64, 1)
    tail = jnp.where(iota(tail.shape, 1) >= 64, tail, 0.0).astype(BF)
    out = dot(low[:, 0:128], w2[:, 0:128], NT) + dot(tail, w1[:, 512:640], NT)
    part[...] = out.astype(BF)


def ffn_kernel(npiece, nmp, cols, *refs):
    terms = refs[:nmp]
    vectors = refs[nmp]
    twos = refs[nmp + 1 : nmp + 1 + npiece]
    part, resid_out, normed_out, hidden_out, act_out, w2 = refs[nmp + 1 + npiece :]
    assemble(twos, w2, lax.axis_index("dp"))
    resid = vectors[8:9, :] + tree(terms)
    resid_out[...] = resid
    hat, _ = norm_parts(resid)
    low = (hat * vectors[2:3, :] + vectors[3:4, :]).astype(BF)
    normed_out[...] = low
    hidden = dot(low, w2[:, 128:384])
    hidden = jnp.where(iota(hidden.shape, 1) < cols, hidden, 0.0)
    hidden_out[...] = hidden
    act, _ = gelu_pair(hidden)
    act_out[...] = act.astype(BF)
    turned = pltpu.roll(act, 64, 1).astype(BF)
    part[...] = dot(turned, w2[:, 256:512], NT).astype(BF)


def head_kernel(npiece, nmp, cols, *refs):
    terms = refs[:nmp]
    resid_one, vectors, head, targets, seg, normed_two, ctx, hidden, act = refs[nmp : nmp + 9]
    twos = refs[nmp + 9 : nmp + 9 + npiece]
    part, pack, grad_out, rows_out, w2, head_low = refs[nmp + 9 + npiece :]
    assemble(twos, w2, lax.axis_index("dp"))
    width = vectors.shape[1]
    mols = targets.shape[1]
    head_low[...] = head[...].astype(BF)
    resid = resid_one[...] + tree(terms)
    hat, inverse = norm_parts(resid)
    gain = vectors[4:5, :]
    low = (hat * gain + vectors[5:6, :]).astype(BF)
    mid = dot(low, head_low[...]) + vectors[9:10, :]
    act_head, slope = gelu_pair(mid)
    act_head = act_head.astype(BF).astype(F32)
    readout = vectors[10:11, :].astype(BF).astype(F32)
    predicted = jnp.sum(act_head * readout, -1, keepdims=True)
    spot = iota((mols, mols), 0) == iota((mols, mols), 1)
    goal = jnp.sum(jnp.where(spot, targets[...], 0.0), -1, keepdims=True)
    seg_row = seg[...]
    there = iota((mols, seg_row.shape[1]), 0) == seg_row
    present = jnp.max(there.astype(F32), -1, keepdims=True)
    error = predicted - goal
    root = jnp.sqrt(error * error + 1.0)
    loss = jnp.sum(present * (root - 1.0), 0, keepdims=True)
    count = jnp.sum(present, 0, keepdims=True)
    grad_pred = present * error / root
    grad_readout = jnp.sum(grad_pred * act_head, 0, keepdims=True)
    grad_mid = (grad_pred * readout * slope).astype(BF)
    grad_bias = jnp.sum(grad_mid.astype(F32), 0, keepdims=True)
    grad_rows = dot(grad_mid, head_low[...], NT)
    grad_gain = jnp.sum(grad_rows * hat, 0, keepdims=True)
    grad_shift = jnp.sum(grad_rows, 0, keepdims=True)
    grad_two = norm_back(grad_rows, hat, inverse, gain)
    grad_out[...] = grad_two
    grad_low = grad_two.astype(BF)
    grad_act = dot(grad_low, w2[:, 256:512])
    grad_act = pltpu.roll(grad_act, 192, 1)
    _, slope_hidden = gelu_pair(hidden[...])
    grad_hidden = jnp.where(iota(grad_act.shape, 1) < cols, grad_act * slope_hidden, 0.0).astype(BF)
    part[...] = dot(grad_hidden, w2[:, 128:384], NT).astype(BF)
    pack[:, 0:width] = low
    pack[:, width : 2 * width] = grad_mid
    pack[:, 2 * width : 3 * width] = normed_two[...]
    pack[:, 3 * width : 4 * width] = grad_low
    pack[:, 4 * width : 4 * width + 256] = ctx[...]
    pack[:, 4 * width + 256 : 4 * width + 512] = act[...]
    pack[:, 4 * width + 512 : 4 * width + 768] = grad_hidden
    r = iota((8, width), 0)
    lane = iota((8, width), 1)
    scalars = jnp.where(lane == 0, loss, jnp.where(lane == 1, count, 0.0))
    rows_out[...] = jnp.where(
        r == 0,
        grad_gain,
        jnp.where(r == 1, grad_shift, jnp.where(r == 2, grad_bias, jnp.where(r == 3, grad_readout, jnp.where(r == 4, scalars, 0.0)))),
    )


def back_kernel(npiece, nmp, mols, heads, scale, *refs):
    terms = refs[:nmp]
    resid_one, grad_two, head_rows, vectors, keyed, probs, values, normed, hats, invs, at, seg = refs[nmp : nmp + 12]
    ones = refs[nmp + 12 : nmp + 12 + npiece]
    twos = refs[nmp + 12 + npiece : nmp + 12 + 2 * npiece]
    rest = refs[nmp + 12 + 2 * npiece :]
    outs = rest[:nmp]
    layer, query_grad, w1, w2, sides, comb, total, gains = rest[nmp:]
    assemble(ones, w1, lax.axis_index("dp"))
    assemble(twos, w2, lax.axis_index("dp"))
    group = lax.axis_index("mp")
    width = vectors.shape[1]
    length = seg.shape[1]
    cols = heads * HEAD_DIM
    filled = jnp.sum((seg[...] != mols).astype(F32)).astype(I32)
    grad_normed = tree(terms)
    hat, inverse = norm_parts(resid_one[...])
    grad_gain = jnp.sum(grad_normed * hat, 0, keepdims=True)
    grad_shift = jnp.sum(grad_normed, 0, keepdims=True)
    grad_one = grad_two[...] + norm_back(grad_normed, hat, inverse, vectors[2:3, :])
    low = grad_one.astype(BF)
    grad_start = jnp.sum(low.astype(F32), 0, keepdims=True)
    ctx_one = dot(low, w2[:, 0:128])
    ctx_two = dot(low, w1[:, 512:640])
    ctx_two = pltpu.roll(ctx_two, 64, 1)
    grad_ctx = jnp.concatenate([ctx_one, ctx_two], 1).astype(BF).astype(F32)
    spread = jnp.broadcast_to(grad_ctx[:, None, :], (mols, heads, 256)).reshape(mols * heads, 256)
    r = iota(spread.shape, 0) & (heads - 1)
    spread = jnp.where(r == iota(spread.shape, 1) // HEAD_DIM, spread, 0.0).astype(BF)
    grad_probs = dot(spread, values[...], NT)
    prob = probs[...].astype(F32)
    inner = jnp.sum(prob * grad_probs, -1, keepdims=True)
    grad_scores = (prob * (grad_probs - inner)).astype(BF).astype(F32)
    grad_scores = jnp.sum(grad_scores.reshape(mols, heads, length), 0)
    grad_values = dot(spread, probs[...], TN)
    sides[0:cols, :] = grad_values[0:cols, :].astype(BF)
    sides[cols:256, :] = jnp.concatenate([grad_scores, jnp.zeros((256 - cols - heads, length), F32)], 0).astype(BF)
    sums = dot(sides[...], normed[...])
    comb[...] = keyed[...].astype(F32).T.astype(BF)
    total[...] = jnp.zeros(total.shape, F32)
    gains[...] = jnp.zeros(gains.shape, F32)
    gain = vectors[0:1, :]

    def one_block(b, unused):
        here = pl.ds(pl.multiple_of(b * BLOCK, BLOCK), BLOCK)
        grad = dot(sides[:, here], comb[...], TN)
        hat_here = hats[here, :].astype(F32)
        low_grad = norm_back(grad, hat_here, invs[here, 0:1], gain).astype(BF)
        total[...] += dot(at[:, here], low_grad)
        gains[0:8, :] += jnp.sum((grad * hat_here).reshape(BLOCK // 8, 8, width), 0)
        gains[8:16, :] += jnp.sum(grad.reshape(BLOCK // 8, 8, width), 0)
        return 0

    lax.fori_loop(0, (filled + BLOCK - 1) // BLOCK, one_block, 0)
    grad_keys = sums[cols : cols + heads, :]
    turned = dot(grad_keys.astype(BF), w1[:, 128:384])
    lane = iota(turned.shape, 1) - 64
    picked = jnp.where((lane >= 0) & (lane // HEAD_DIM == iota(turned.shape, 0)), turned, 0.0)
    grad_query = jnp.sum(pltpu.roll(picked, 192, 1), 0, keepdims=True) * scale
    query_grad[...] = jnp.broadcast_to(grad_query, query_grad.shape)
    grad_query = jnp.broadcast_to(grad_query.astype(BF), (16, 256))
    grad_row = dot(grad_query, w1[:, 0:256], NT)[0:1, :]
    hat_start, inverse_start = norm_parts(vectors[8:9, :])
    start_row = (hat_start * gain + vectors[1:2, :]).astype(BF).astype(F32)
    first = jnp.where(group == 0, 1.0, 0.0)
    row_graph = norm_back(grad_row, hat_start, inverse_start, gain) + first * grad_start
    row_gain = jnp.sum(gains[0:8, :], 0, keepdims=True) + grad_row * hat_start
    row_shift = jnp.sum(gains[8:16, :], 0, keepdims=True) + grad_row
    base = TYPES + 32
    r = iota((FEATS - base, width), 0)
    extra = jnp.where(r == 2, row_graph, 0.0)
    extra = jnp.where(r == 3, row_gain, extra)
    extra = jnp.where(r == 4, row_shift, extra)
    extra = jnp.where(r == 5, first * grad_gain, extra)
    extra = jnp.where(r == 6, first * grad_shift, extra)
    for i in range(4):
        extra = jnp.where(r == 7 + i, first * head_rows[i : i + 1, :], extra)
    total[base:FEATS, :] += extra
    each = FEATS // nmp
    for k in range(nmp):
        start = pl.multiple_of((group ^ k) * each, 16)
        outs[k][...] = total[pl.ds(start, each), :].astype(BF)
    lay = jnp.concatenate(
        [
            sums[0:cols, :],
            grad_one,
            jnp.zeros((32 - mols, width), F32),
            grad_keys,
            jnp.broadcast_to(start_row, (8, width)),
            jnp.zeros((256 - cols - 48, width), F32),
        ],
        0,
    )
    layer[...] = lay.T.astype(BF)


def packet_kernel(nmp, owners, *refs):
    terms = refs[:nmp]
    layer, head_rows, query_grad, out = refs[nmp:]
    dp, deep = layer.shape[0], layer.shape[1]
    half = terms[0].shape[1] // 2
    summed = tree(terms)
    scal = head_rows[4:5, 0:128]
    loss, count = scal[:, 0:1], scal[:, 1:2]
    a, b, c = three(loss)
    lane = iota((16, 128), 1)
    first = jnp.where(lane == 0, a, jnp.where(lane == 1, b, jnp.where(lane == 2, c, jnp.where(lane == 3, count, 0.0))))
    r = iota((16, 128), 0)
    side = jnp.where(r == 0, first, jnp.where(r == 1, query_grad[0:1, 0:128], jnp.where(r == 2, query_grad[0:1, 128:256], 0.0)))
    for p in range(dp):
        if p < owners:
            each = summed[p * 8 : p * 8 + 8, :]
        else:
            each = jnp.zeros((8, 2 * half), F32)
        each = jnp.concatenate([each[:, 0:half], each[:, half:]], 0)
        out[p, 0:deep, :] = layer[p]
        out[p, deep : deep + 16, :] = each[:, 0:256].astype(BF)
        out[p, deep + 16 : deep + 32, :] = jnp.concatenate([each[:, 256:384], side], 1).astype(BF)


def outer_kernel(own, head_in, grad_mid, normed, grad_low, act, grad_hidden, head_grad, up_grad, down_grad, squares, full):
    me = lax.axis_index("dp")
    grad = dot(head_in[...], grad_mid[...], TN)
    head_grad[...] = grad
    squares[...] = jnp.broadcast_to(jnp.sum(jnp.sum(grad * grad, 0, keepdims=True), 1, keepdims=True), squares.shape)
    kept = up_grad.shape[0]
    start = 0 if kept == full.shape[0] else pl.multiple_of(me * own, 8)
    full[...] = dot(normed[...], grad_hidden[...], TN)
    up_grad[...] = full[pl.ds(start, kept), :]
    full[...] = dot(grad_low[...], act[...], TN)
    down_grad[...] = full[pl.ds(start, kept), :]


def owner_kernel(own, mols, cols, scale, packets, ctx, query, up_grad, down_grad, layer, send, scalars):
    dp = packets.shape[0]
    deep = packets.shape[1] - 32
    acc = jnp.zeros((deep, 256), F32)
    table = jnp.zeros((16, 256), F32)
    rest = jnp.zeros((16, 256), F32)
    out_grad = jnp.zeros((deep, 256), F32)
    for p in range(dp):
        piece = packets[p, 0:deep, :]
        acc += piece.astype(F32)
        table += packets[p, deep : deep + 16, :].astype(F32)
        rest += packets[p, deep + 16 : deep + 32, :].astype(F32)
        rows = ctx[p * mols : (p + 1) * mols, :].astype(F32)
        rows = jnp.concatenate([jnp.zeros((64, 256), F32), rows, jnp.zeros((64 - mols, 256), F32)], 0).astype(BF)
        out_grad += dot(piece[:, 128:256], rows)
    keys = jnp.concatenate([jnp.zeros((96, 256), F32), query[...], jnp.zeros((24, 256), F32)], 0)
    key_grad = dot(acc[:, 128:256], keys, precision=HIGHEST) * scale
    start_col = packets[0, 0:deep, 128:256].astype(F32)[:, 104:105]
    side = rest[:, 128:256]
    query_row = jnp.concatenate([side[1:2, :], side[2:3, :]], 1)
    grads = [start_col * query_row, key_grad, acc, out_grad]
    square = jnp.zeros((1, 1), F32)

    def add(value):
        return jnp.sum(jnp.sum(value * value, 0, keepdims=True), 1, keepdims=True)

    for j in range(6):
        g = grads[j][0:own, 0:cols] if j < 4 else (up_grad if j == 4 else down_grad)[:, 0:cols]
        layer[j] = g
        square += add(g)
    third = rest[:, 0:128]
    square += add(table) + add(third)
    a, b, c = three(square)
    lane = iota((16, 128), 1)
    r = iota((16, 128), 0)
    tail = jnp.where(r == 0, jnp.where(lane == 0, a, jnp.where(lane == 1, b, jnp.where(lane == 2, c, 0.0))), 0.0)
    packet = jnp.concatenate([table, third, tail], 1).astype(BF)
    for p in range(dp):
        send[p] = packet
    loss = side[0:1, 0:1] + side[0:1, 1:2] + side[0:1, 2:3]
    count = side[0:1, 3:4]
    lane = iota((8, 128), 1)
    scalars[...] = jnp.where(lane == 0, loss, jnp.where(lane == 1, count, 0.0))


def stats_kernel(layer, left_roots, right_roots, left, right, shaped):
    for j in range(6):
        g = layer[j]
        left[j] = dot(g, g, NT, HIGHEST)
        right[j] = dot(g, g, TN, HIGHEST)
        shaped[j] = dot(dot(left_roots[j], g, NN, HIGHEST), right_roots[j], NN, HIGHEST)


def adam(weight, first, second, grad, rate):
    first_new = BETA_ONE * first + (1.0 - BETA_ONE) * grad
    second_new = BETA_TWO * second + (1.0 - BETA_TWO) * grad * grad
    fixed_one = 1.0 - BETA_ONE**STEP
    fixed_two = 1.0 - BETA_TWO**STEP
    update = first_new / fixed_one / (jnp.sqrt(second_new / fixed_two) + ADAM_EPS)
    return first_new, second_new, weight - rate * (update + WEIGHT_DECAY * weight)


def update_kernel(nmp, owners, cols, *refs):
    packets = refs[:nmp]
    (
        squares, scalars, layer, left_add, right_add, shaped, weights, left, right,
        tables, tables_m, tables_v, head, head_m, head_v, head_grad, vectors, vectors_m, vectors_v,
        loss_out, layer_out, weights_out, left_out, right_out,
        tm_out, tv_out, t_out, hm_out, hv_out, h_out, vm_out, vv_out, v_out, factors, grads,
    ) = refs[nmp:]
    step = pl.program_id(0)

    @pl.when(step == 0)
    def _():
        parts = []
        for ref in packets:
            s = jnp.zeros((1, 1), F32)
            for p in range(ref.shape[0]):
                tail = ref[p, :, 384:512].astype(F32)
                s += tail[0:1, 0:1] + tail[0:1, 1:2] + tail[0:1, 2:3]
            parts.append(s)
        while len(parts) > 1:
            parts = [parts[i] + parts[i + 1] for i in range(0, len(parts), 2)]
        square = parts[0] + squares[0:1, 0:1]
        loss, count = scalars[0:1, 0:1], scalars[0:1, 1:2]
        norm = jnp.sqrt(square) / count
        factor = CLIP / jnp.maximum(norm, CLIP) / count
        lane = iota((8, 128), 1)
        loss_out[...] = jnp.where(lane == 0, loss, jnp.where(lane == 1, count, norm))
        factors[...] = jnp.broadcast_to(factor, (8, 128))
        group = lax.axis_index("mp")
        each = FEATS // nmp
        half = 384
        for k in range(nmp):
            start = pl.multiple_of((group ^ k) * each, 8)
            for p in range(owners):
                piece = packets[k][p, :, 0:half].astype(F32)
                piece = jnp.concatenate([piece[0:8, :], piece[8:16, :]], 1) * factor
                grads[pl.ds(pl.multiple_of(start + p * 8, 8), 8), :] = piece
        rows = tables.shape[0]
        tm_out[...], tv_out[...], t_out[...] = adam(tables[...], tables_m[...], tables_v[...], grads[0:rows, :], RATE_TABLES)
        order = (3, 4, 5, 6, 7, 8, 0, 1, 2, 9, 10)
        r = iota((16, vectors.shape[1]), 0)
        tail = jnp.zeros(r.shape, F32)
        for i, o in enumerate(order):
            tail = jnp.where(r == i, grads[rows + o : rows + o + 1, :], tail)
        nrows = vectors.shape[0]
        vm_out[...], vv_out[...], v_out[...] = adam(vectors[...], vectors_m[...], vectors_v[...], tail[0:nrows, :], RATE_VECTORS)
        for j in range(6):
            span = slice(j * cols, (j + 1) * cols)
            layer_out[:, span] = layer[j] * factor
            weights_out[:, span] = weights[:, span] - RATE_LAYER * (shaped[j] * factor + WEIGHT_DECAY * weights[:, span])

    factor = factors[0:1, 0:1]
    hm_out[...], hv_out[...], h_out[...] = adam(head[...], head_m[...], head_v[...], head_grad[...] * factor, RATE_HEAD)
    scale = (1.0 - STATS_DECAY) * factor * factor
    left_out[...] = STATS_DECAY * left[...] + scale[None] * left_add[...]
    right_out[...] = STATS_DECAY * right[...] + scale[None] * right_add[...]


def exchange(x, axis):
    n = lax.axis_size(axis)
    return [x] + [lax.ppermute(x, axis, [(i, i ^ k) for i in range(n)]) for k in range(1, n)]


def gather_rows(x):
    if lax.axis_size("dp") == 8 and x.shape[0] % 16 == 0:
        return exchange(x, "dp")
    return [lax.all_gather(x, "dp", axis=0, tiled=True)]


def per_device(
    lap_vectors,
    eig_index,
    type_ids,
    seg_ids,
    targets,
    layer_weights,
    left_stats,
    right_stats,
    left_roots,
    right_roots,
    tables,
    tables_m,
    tables_v,
    head_weight,
    head_m,
    head_v,
    vectors,
    vectors_m,
    vectors_v,
):
    dp = lax.axis_size("dp")
    nmp = lax.axis_size("mp")
    length = seg_ids.shape[1]
    mols = targets.shape[1]
    width = vectors.shape[1]
    own, group_cols = layer_weights.shape[0], layer_weights.shape[1]
    cols = group_cols // 6
    heads = cols // HEAD_DIM
    scale = HEAD_DIM ** (-0.5)
    owners = FEATS // nmp // 8

    split = 3 * cols + 128
    w = layer_weights.astype(BF)
    ones = gather_rows(jnp.concatenate([w[:, : 3 * cols], w[:, split : 4 * cols]], 1))
    twos = gather_rows(jnp.concatenate([w[:, 3 * cols : split], w[:, 4 * cols :]], 1))
    np_ = len(ones)

    at, normed, hats, invs = call(
        functools.partial(embed_kernel, mols),
        [sds((FEATS, length), BF), sds((length, width), BF), sds((length, width), BF), sds((length, 128), F32)],
        [lap_vectors[0].T, eig_index[0].T, type_ids, seg_ids, tables, vectors],
        [pltpu.VMEM((FEATS, width), BF), pltpu.VMEM((FEATS, width), BF), pltpu.VMEM((8, length), I32)],
        flops=4 * length * FEATS * width,
    )
    wbuf = [pltpu.VMEM((width, 640), BF), pltpu.VMEM((width, 512), BF)]
    part, probs, values, ctx, keyed, query = call(
        functools.partial(attn_kernel, np_, mols, heads, scale),
        [
            sds((mols, width), BF),
            sds((mols * heads, length), BF),
            sds((length, 256), BF),
            sds((mols, 256), BF),
            sds((width, 256), BF),
            sds((8, 256), F32),
        ],
        [normed, seg_ids, vectors, *ones, *twos],
        wbuf,
        flops=4 * length * 256 * width,
    )
    part, resid_one, normed_two, hidden, act = call(
        functools.partial(ffn_kernel, np_, nmp, cols),
        [sds((mols, width), BF), sds((mols, width), F32), sds((mols, width), BF), sds((mols, 256), F32), sds((mols, 256), BF)],
        [*exchange(part, "mp"), vectors, *twos],
        wbuf[1:],
        flops=4 * mols * width * 256,
    )
    part, pack, grad_two, head_rows = call(
        functools.partial(head_kernel, np_, nmp, cols),
        [sds((mols, width), BF), sds((mols, 4 * width + 768), BF), sds((mols, width), F32), sds((8, width), F32)],
        [*exchange(part, "mp"), resid_one, vectors, head_weight, targets, seg_ids, normed_two, ctx, hidden, act, *twos],
        [wbuf[1], pltpu.VMEM((width, width), BF)],
        flops=4 * width * width * mols,
    )
    packs = lax.all_gather(pack, "dp", axis=0, tiled=True)
    back = call(
        functools.partial(back_kernel, np_, nmp, mols, heads, scale),
        [sds((FEATS // nmp, width), BF) for _ in range(nmp)] + [sds((width, 256), BF), sds((8, 256), F32)],
        [
            *exchange(part, "mp"), resid_one, grad_two, head_rows, vectors, keyed, probs, values, normed, hats, invs, at,
            seg_ids, *ones, *twos,
        ],
        [
            *wbuf,
            pltpu.VMEM((256, length), BF),
            pltpu.VMEM((256, width), BF),
            pltpu.VMEM((FEATS, width), F32),
            pltpu.VMEM((16, width), F32),
        ],
        flops=8 * length * 256 * width,
    )
    shares, layer_part, query_grad = back[:nmp], back[nmp], back[nmp + 1]
    moved = [shares[0]] + [lax.ppermute(shares[k], "mp", [(i, i ^ k) for i in range(nmp)]) for k in range(1, nmp)]
    deep = (own + 15) // 16 * 16
    layer_part = layer_part.reshape(dp, own, 256)
    if deep != own:
        layer_part = jnp.pad(layer_part, ((0, 0), (0, deep - own), (0, 0)))
    (packet,) = call(
        functools.partial(packet_kernel, nmp, owners),
        [sds((dp, deep + 32, 256), BF)],
        [*moved, layer_part, head_rows, query_grad],
    )
    packets = lax.all_to_all(packet, "dp", 0, 0, tiled=True)
    total = dp * mols

    def lanes(first, size):
        return pl.BlockSpec((total, size), lambda *unused: (0, first // size))

    kept = width if own % 8 else own
    head_grad, up_grad, down_grad, squares = pl.pallas_call(
        functools.partial(outer_kernel, own),
        out_shape=(sds((width, width), F32), sds((kept, 256), F32), sds((kept, 256), F32), sds((8, 128), F32)),
        grid=(1,),
        in_specs=[
            lanes(0, width),
            lanes(width, width),
            lanes(2 * width, width),
            lanes(3 * width, width),
            lanes(4 * width + 256, 256),
            lanes(4 * width + 512, 256),
        ],
        out_specs=(
            pl.BlockSpec((width, width), lambda i: (0, 0)),
            pl.BlockSpec((kept, 256), lambda i: (0, 0)),
            pl.BlockSpec((kept, 256), lambda i: (0, 0)),
            pl.BlockSpec((8, 128), lambda i: (0, 0)),
        ),
        scratch_shapes=[pltpu.VMEM((width, 256), F32)],
        compiler_params=pltpu.CompilerParams(vmem_limit_bytes=40 * MIB),
        cost_estimate=pl.CostEstimate(flops=2 * total * width * (width + 512), bytes_accessed=4 * width * width, transcendentals=0),
    )(*[packs] * 6)
    if kept != own:
        up_grad, down_grad = [lax.dynamic_slice_in_dim(x, lax.axis_index("dp") * own, own) for x in (up_grad, down_grad)]
    layer, send, scalars = pl.pallas_call(
        functools.partial(owner_kernel, own, mols, cols, scale),
        out_shape=(sds((6, own, cols), F32), sds((dp, 16, 512), BF), sds((8, 128), F32)),
        grid=(1,),
        in_specs=[
            pl.BlockSpec((dp, deep + 32, 256), lambda i: (0, 0, 0)),
            lanes(4 * width, 256),
            pl.BlockSpec((8, 256), lambda i: (0, 0)),
            pl.BlockSpec((own, 256), lambda i: (0, 0)),
            pl.BlockSpec((own, 256), lambda i: (0, 0)),
        ],
        out_specs=(
            pl.BlockSpec((6, own, cols), lambda i: (0, 0, 0)),
            pl.BlockSpec((dp, 16, 512), lambda i: (0, 0, 0)),
            pl.BlockSpec((8, 128), lambda i: (0, 0)),
        ),
        compiler_params=pltpu.CompilerParams(vmem_limit_bytes=40 * MIB),
        cost_estimate=pl.CostEstimate(flops=2 * own * 256 * 1024, bytes_accessed=1 << 20, transcendentals=0),
    )(packets, packs, query, up_grad, down_grad)
    sums = exchange(lax.all_to_all(send, "dp", 0, 0, tiled=True), "mp")
    left_add, right_add, shaped = call(
        stats_kernel,
        [sds((6, own, own), F32), sds((6, cols, cols), F32), sds((6, own, cols), F32)],
        [layer, jnp.swapaxes(left_roots, 0, 1), right_roots[0]],
        flops=12 * 6 * own * cols * (2 * own + 2 * cols),
    )
    steps = 6
    rows_each = width // steps

    def fixed(shape):
        return pl.BlockSpec(shape, lambda i: (0,) * len(shape))

    head_spec = pl.BlockSpec((rows_each, width), lambda i: (i, 0))
    left_spec = pl.BlockSpec((1, own, own), lambda i: (i, 0, 0))
    right_spec = pl.BlockSpec((1, cols, cols), lambda i: (i, 0, 0))
    layer_spec = fixed((own, group_cols))
    table_spec = fixed(tables.shape)
    vector_spec = fixed(vectors.shape)
    outs = pl.pallas_call(
        functools.partial(update_kernel, nmp, owners, cols),
        out_shape=(
            sds((8, 128), F32),
            sds((own, group_cols), F32),
            sds((own, group_cols), F32),
            sds((6, own, own), F32),
            sds((6, cols, cols), F32),
            *[sds(tables.shape, F32)] * 3,
            *[sds(head_weight.shape, F32)] * 3,
            *[sds(vectors.shape, F32)] * 3,
        ),
        grid=(steps,),
        in_specs=[fixed((dp, 16, 512))] * nmp
        + [fixed((8, 128)), fixed((8, 128)), fixed((6, own, cols)), left_spec, right_spec, fixed((6, own, cols))]
        + [layer_spec, left_spec, right_spec]
        + [table_spec] * 3
        + [head_spec] * 4
        + [vector_spec] * 3,
        out_specs=(
            fixed((8, 128)),
            layer_spec,
            layer_spec,
            left_spec,
            right_spec,
            *[table_spec] * 3,
            *[head_spec] * 3,
            *[vector_spec] * 3,
        ),
        scratch_shapes=[pltpu.VMEM((8, 128), F32), pltpu.VMEM((FEATS, width), F32)],
        compiler_params=pltpu.CompilerParams(vmem_limit_bytes=48 * MIB),
        cost_estimate=pl.CostEstimate(flops=20 * width * width, bytes_accessed=28 * width * width, transcendentals=0),
    )(
        *sums, squares, scalars, layer, left_add, right_add, shaped, layer_weights, jnp.swapaxes(left_stats, 0, 1), right_stats[0],
        tables, tables_m, tables_v, head_weight, head_m, head_v, head_grad, vectors, vectors_m, vectors_v,
    )
    facts, layer_grad, layer_new, left_new, right_new, tm, tv, tn, hm, hv, hn, vm, vv, vn = outs
    return (
        facts[0, 0],
        facts[0, 1],
        facts[0, 2],
        layer_grad,
        layer_new,
        jnp.swapaxes(left_new, 0, 1),
        right_new[None],
        tm,
        tv,
        tn,
        hm,
        hv,
        hn,
        vm,
        vv,
        vn,
    )


def solution(mesh):
    placed = (
        P("dp", None, None),
        P("dp", None, None),
        P("dp", None),
        P("dp", None),
        P("dp", None),
        P("dp", "mp"),
        P("dp", "mp", None),
        P("dp", "mp", None, None),
        P("dp", "mp", None),
        P("dp", "mp", None, None),
        *[P()] * 9,
    )
    return jax.shard_map(
        per_device,
        mesh=mesh,
        in_specs=placed,
        out_specs=(
            P(),
            P(),
            P(),
            P("dp", "mp"),
            P("dp", "mp"),
            P("dp", "mp", None),
            P("dp", "mp", None, None),
            *[P()] * 9,
        ),
        check_vma=False,
    )
```

```python
import functools

import jax
import jax.numpy as jnp
from jax import lax
from jax.experimental import pallas as pl
from jax.experimental.pallas import tpu as pltpu
from jax.sharding import PartitionSpec as P

HEAD_DIM = 24
TYPES = 192
STEP = 10
NORM_EPS = 1e-05
CLIP = 0.25
STATS_DECAY = 0.95
RATE_LAYER = 0.15
RATE_TABLES = 0.15
RATE_HEAD = 0.01
RATE_VECTORS = 0.2
BETA_ONE = 0.9
BETA_TWO = 0.99
ADAM_EPS = 1e-08
WEIGHT_DECAY = 0.01
MASKED = -1000000000.0
GELU_C = 0.7978845608028654
GELU_A = 0.044715

BF = jnp.bfloat16
F32 = jnp.float32
I32 = jnp.int32
HIGHEST = lax.Precision.HIGHEST
NN = ((1,), (0,))
NT = ((1,), (1,))
TN = ((0,), (0,))
BLOCK = 256
FEATS = 256
MIB = 1024 * 1024


def dot(a, b, dims=NN, precision=None):
    return lax.dot_general(a, b, (dims, ((), ())), preferred_element_type=F32, precision=precision)


def iota(shape, dim):
    return lax.broadcasted_iota(I32, shape, dim)


IN_VMEM = pl.BlockSpec(memory_space=pltpu.VMEM)
IN_PLACE = pl.BlockSpec(memory_space=pl.ANY)


def call(kernel, outs, ins, scratch=(), flops=0, vmem=16, in_specs=None, out_specs=None):
    moved = sum(x.size * x.dtype.itemsize for x in list(ins) + list(outs))
    return pl.pallas_call(
        kernel,
        out_shape=tuple(outs),
        in_specs=in_specs or [IN_VMEM] * len(ins),
        out_specs=tuple(out_specs or [IN_VMEM] * len(outs)),
        scratch_shapes=list(scratch),
        compiler_params=pltpu.CompilerParams(vmem_limit_bytes=vmem * MIB),
        cost_estimate=pl.CostEstimate(flops=flops, bytes_accessed=moved, transcendentals=0),
    )(*ins)


def sds(shape, dtype):
    return jax.ShapeDtypeStruct(shape, dtype)


def norm_parts(values):
    center = values - jnp.mean(values, -1, keepdims=True)
    spread = jnp.mean(center * center, -1, keepdims=True)
    inverse = lax.rsqrt(spread + NORM_EPS)
    return center * inverse, inverse


def norm_back(grad, hat, inverse, gain):
    scaled = grad * gain
    mean_one = jnp.mean(scaled, -1, keepdims=True)
    mean_two = jnp.mean(scaled * hat, -1, keepdims=True)
    return inverse * (scaled - mean_one - hat * mean_two)


def gelu_pair(x):
    t = jnp.tanh(GELU_C * (x + GELU_A * x * x * x))
    value = 0.5 * x * (1.0 + t)
    slope = 0.5 * (1.0 + t) + 0.5 * x * (1.0 - t * t) * (GELU_C * (1.0 + 3.0 * GELU_A * x * x))
    return value, slope


def tree(refs):
    parts = [r[...].astype(F32) for r in refs]
    while len(parts) > 1:
        parts = [parts[i] + parts[i + 1] for i in range(0, len(parts), 2)]
    return parts[0]


def three(x):
    high = x.astype(BF).astype(F32)
    mid = (x - high).astype(BF).astype(F32)
    return high, mid, x - high - mid


def assemble(pieces, whole, first_owner):
    rows = pieces[0].shape[0]
    if len(pieces) == 1:
        whole[...] = pieces[0][...]
        return
    for k, piece in enumerate(pieces):
        start = pl.multiple_of((first_owner ^ k) * rows, 16)
        whole[pl.ds(start, rows), :] = piece[...]


def embed_kernel(mols, *refs):
    sources, (at, normed, hats, invs), held, (high, low, prev, sems) = refs[:6], refs[6:10], refs[10:16], refs[16:]
    copies = [pltpu.make_async_copy(a, b, sems.at[i]) for i, (a, b) in enumerate(zip(sources, held))]
    for copy in copies:
        copy.start()
    normed[...] = jnp.zeros(normed.shape, BF)
    for copy in copies:
        copy.wait()
    lap, eig, kinds, seg, tables, vectors = held
    length = seg.shape[1]
    width = vectors.shape[1]
    rows = tables.shape[0]
    tab = tables[...]
    tab_high = tab.astype(BF)
    high[0:rows, :] = tab_high
    rest = jnp.where(iota(tab.shape, 0) < TYPES, tab - tab_high.astype(F32), 0.0)
    low[0:rows, :] = rest.astype(BF)
    r = iota((FEATS - rows, width), 0)
    extra = jnp.where(r == 0, vectors[6:7, :], jnp.where(r == 1, vectors[7:8, :], jnp.where(r == 2, vectors[8:9, :], 0.0)))
    extra_high = extra.astype(BF)
    high[rows:FEATS, :] = extra_high
    low[rows:FEATS, :] = (extra - extra_high.astype(F32)).astype(BF)
    seg_row = seg[...]
    before = pltpu.roll(jnp.broadcast_to(seg_row, (8, length)), 1, 1)
    before = jnp.where(iota((8, length), 1) == 0, -1, before)
    prev[...] = before
    filled = jnp.sum((seg_row != mols).astype(F32)).astype(I32)
    gain = vectors[0:1, :]
    shift = vectors[1:2, :]
    window = 2 * BLOCK

    def one_block(b, unused):
        start = pl.multiple_of(b * BLOCK, BLOCK)
        here = pl.ds(start, BLOCK)
        first = pl.multiple_of(jnp.clip(start - 128, 0, length - window), 128)
        source = iota((window, BLOCK), 0) + first
        one = eig[0:1, here]
        two = eig[1:2, here]
        near = lap[:, pl.ds(first, window)].astype(BF)
        pair_one = dot(near, (source == one).astype(F32).astype(BF))
        pair_two = dot(near, (source == two).astype(F32).astype(BF))
        seg_here = seg[0:1, here]
        begins = (seg_here != mols) & (seg_here != prev[0:1, here])
        kind = jnp.where(begins, -1, kinds[0:1, here])
        keep = jnp.where(begins, 0.0, 1.0)
        at[0:TYPES, here] = (iota((TYPES, BLOCK), 0) == kind).astype(F32).astype(BF)
        half = pair_one.shape[0]
        at[TYPES : TYPES + half, here] = (pair_one * keep).astype(BF)
        at[TYPES + half : rows, here] = (pair_two * keep).astype(BF)
        which = jnp.where(begins, 2, jnp.where(one == two, 0, 1))
        at[rows:FEATS, here] = (iota((FEATS - rows, BLOCK), 0) == which).astype(F32).astype(BF)
        picks = at[:, here]
        resid = dot(picks, high[...], TN) + dot(picks, low[...], TN)
        hat, inverse = norm_parts(resid)
        normed[here, :] = (hat * gain + shift).astype(BF)
        hats[here, :] = hat.astype(BF)
        invs[here, :] = jnp.broadcast_to(inverse, (BLOCK, 128))
        return 0

    lax.fori_loop(0, (filled + BLOCK - 1) // BLOCK, one_block, 0)


def attn_kernel(npiece, mols, heads, scale, *refs):
    normed, seg, vectors = refs[:3]
    ones = refs[3 : 3 + npiece]
    part, probs, values, ctx_out, keyed, query_out, w1 = refs[3 + npiece :]
    assemble(ones, w1, lax.axis_index("dp"))
    width = vectors.shape[1]
    cols = heads * HEAD_DIM
    hat, _ = norm_parts(vectors[8:9, :])
    start_row = (hat * vectors[0:1, :] + vectors[1:2, :]).astype(BF)
    q = dot(jnp.broadcast_to(start_row, (16, width)), w1[:, 0:256])
    q = q.astype(BF).astype(F32)
    q = jnp.where(iota((16, 256), 1) < cols, q, 0.0)
    r = iota((16, 256), 0)
    head_of = iota((16, 256), 1) // HEAD_DIM
    query_out[...] = jnp.where(r == head_of, q, 0.0)[0:8, :]
    shifted = pltpu.roll(q, 64, 1)[0:1, :]
    r = iota((128, 256), 0)
    lane = iota((128, 256), 1) - 64
    pick = (lane >= 0) & ((r & 7) == lane // HEAD_DIM) & (r >= 64) & (r < 80)
    q_keys = jnp.where(pick, shifted, 0.0).astype(BF)
    u = dot(w1[:, 128:384], q_keys, NT)
    u_high = u.astype(BF)
    lane = iota(u.shape, 1)
    u_both = jnp.where(lane < 72, u_high.astype(F32), u - u_high.astype(F32))
    last = w1[:, 512:640].astype(F32)
    side = jnp.where(lane < 64, last, u_both).astype(BF)
    keyed[:, 0:128] = w1[:, 384:512]
    keyed[:, 128:256] = jnp.where(lane < 64, last, jnp.where(lane < 72, u * scale, 0.0)).astype(BF)
    normed_all = normed[...]
    values[:, 0:128] = dot(normed_all, w1[:, 384:512]).astype(BF)
    second = dot(normed_all, side)
    values[:, 128:256] = jnp.where(iota(second.shape, 1) < 64, second, 0.0).astype(BF)
    turned = second.T
    scores = (turned[64:72, :] + turned[72:80, :]) * scale
    seg_row = seg[...]
    length = seg_row.shape[1]
    mine = iota((mols, 1, length), 0) == seg_row[None]
    masked = jnp.where(mine, scores[None], MASKED)
    peak = jnp.max(masked, -1, keepdims=True)
    grown = jnp.where(mine, jnp.exp(masked - peak), 0.0)
    total = jnp.sum(grown, -1, keepdims=True)
    total = jnp.where(total > 0.0, total, 1.0)
    prob = (grown / total).reshape(mols * heads, length).astype(BF)
    probs[...] = prob
    wide = dot(prob, values[...])
    r = iota(wide.shape, 0) & (heads - 1)
    wide = jnp.where(r == iota(wide.shape, 1) // HEAD_DIM, wide, 0.0)
    ctx = jnp.sum(wide.reshape(mols, heads, 256), 1)
    ctx_out[...] = ctx.astype(BF)
    turned_ctx = pltpu.roll(ctx, 64, 1).astype(BF)
    part[...] = dot(turned_ctx, w1[:, 512:768], NT).astype(BF)


def ffn_kernel(npiece, nmp, cols, *refs):
    terms = refs[:nmp]
    vectors = refs[nmp]
    twos = refs[nmp + 1 : nmp + 1 + npiece]
    part, resid_out, normed_out, hidden_out, act_out, w2 = refs[nmp + 1 + npiece :]
    assemble(twos, w2, lax.axis_index("dp"))
    resid = vectors[8:9, :] + tree(terms)
    resid_out[...] = resid
    hat, _ = norm_parts(resid)
    low = (hat * vectors[2:3, :] + vectors[3:4, :]).astype(BF)
    normed_out[...] = low
    hidden = dot(low, w2[:, 0:256])
    hidden = jnp.where(iota(hidden.shape, 1) < cols, hidden, 0.0)
    hidden_out[...] = hidden
    act, _ = gelu_pair(hidden)
    act_out[...] = act.astype(BF)
    turned = pltpu.roll(act, 64, 1).astype(BF)
    part[...] = dot(turned, w2[:, 128:384], NT).astype(BF)


def head_kernel(nmp, cols, *refs):
    terms = refs[:nmp]
    resid_one, vectors, head, targets, seg, normed_two, ctx, hidden, act, w2 = refs[nmp : nmp + 10]
    part, pack, grad_out, rows_out, head_low = refs[nmp + 10 :]
    width = vectors.shape[1]
    mols = targets.shape[1]
    head_low[...] = head[...].astype(BF)
    resid = resid_one[...] + tree(terms)
    hat, inverse = norm_parts(resid)
    gain = vectors[4:5, :]
    low = (hat * gain + vectors[5:6, :]).astype(BF)
    mid = dot(low, head_low[...]) + vectors[9:10, :]
    act_head, slope = gelu_pair(mid)
    act_head = act_head.astype(BF).astype(F32)
    readout = vectors[10:11, :].astype(BF).astype(F32)
    predicted = jnp.sum(act_head * readout, -1, keepdims=True)
    spot = iota((mols, mols), 0) == iota((mols, mols), 1)
    goal = jnp.sum(jnp.where(spot, targets[...], 0.0), -1, keepdims=True)
    seg_row = seg[...]
    there = iota((mols, seg_row.shape[1]), 0) == seg_row
    present = jnp.max(there.astype(F32), -1, keepdims=True)
    error = predicted - goal
    root = jnp.sqrt(error * error + 1.0)
    loss = jnp.sum(present * (root - 1.0), 0, keepdims=True)
    count = jnp.sum(present, 0, keepdims=True)
    grad_pred = present * error / root
    grad_readout = jnp.sum(grad_pred * act_head, 0, keepdims=True)
    grad_mid = (grad_pred * readout * slope).astype(BF)
    grad_bias = jnp.sum(grad_mid.astype(F32), 0, keepdims=True)
    grad_rows = dot(grad_mid, head_low[...], NT)
    grad_gain = jnp.sum(grad_rows * hat, 0, keepdims=True)
    grad_shift = jnp.sum(grad_rows, 0, keepdims=True)
    grad_two = norm_back(grad_rows, hat, inverse, gain)
    grad_out[...] = grad_two
    grad_low = grad_two.astype(BF)
    grad_act = dot(grad_low, w2[:, 128:384])
    grad_act = pltpu.roll(grad_act, 192, 1)
    _, slope_hidden = gelu_pair(hidden[...])
    grad_hidden = jnp.where(iota(grad_act.shape, 1) < cols, grad_act * slope_hidden, 0.0).astype(BF)
    part[...] = dot(grad_hidden, w2[:, 0:256], NT).astype(BF)
    pack[:, 0:width] = low
    pack[:, width : 2 * width] = grad_mid
    pack[:, 2 * width : 3 * width] = normed_two[...]
    pack[:, 3 * width : 4 * width] = grad_low
    pack[:, 4 * width : 4 * width + 256] = ctx[...]
    pack[:, 4 * width + 256 : 4 * width + 512] = act[...]
    pack[:, 4 * width + 512 : 4 * width + 768] = grad_hidden
    r = iota((8, width), 0)
    lane = iota((8, width), 1)
    scalars = jnp.where(lane == 0, loss, jnp.where(lane == 1, count, 0.0))
    rows_out[...] = jnp.where(
        r == 0,
        grad_gain,
        jnp.where(r == 1, grad_shift, jnp.where(r == 2, grad_bias, jnp.where(r == 3, grad_readout, jnp.where(r == 4, scalars, 0.0)))),
    )


def back_kernel(nmp, nlayer, mols, heads, scale, *refs):
    terms = refs[:nmp]
    resid_one, grad_two, head_rows, vectors, keyed, probs, values, normed, hats, invs, at, seg, w1 = refs[nmp : nmp + 13]
    rest = refs[nmp + 13 :]
    outs = rest[:nmp]
    layer_outs = rest[nmp : nmp + nlayer]
    side, sides, comb, total, gains = rest[nmp + nlayer : nmp + nlayer + 5]
    group = lax.axis_index("mp")
    width = vectors.shape[1]
    length = seg.shape[1]
    cols = heads * HEAD_DIM
    filled = jnp.sum((seg[...] != mols).astype(F32)).astype(I32)
    grad_normed = tree(terms)
    hat, inverse = norm_parts(resid_one[...])
    grad_gain = jnp.sum(grad_normed * hat, 0, keepdims=True)
    grad_shift = jnp.sum(grad_normed, 0, keepdims=True)
    grad_one = grad_two[...] + norm_back(grad_normed, hat, inverse, vectors[2:3, :])
    low = grad_one.astype(BF)
    grad_start = jnp.sum(low.astype(F32), 0, keepdims=True)
    grad_ctx = pltpu.roll(dot(low, w1[:, 512:768]), 192, 1).astype(BF).astype(F32)
    spread = jnp.broadcast_to(grad_ctx[:, None, :], (mols, heads, 256)).reshape(mols * heads, 256)
    r = iota(spread.shape, 0) & (heads - 1)
    spread = jnp.where(r == iota(spread.shape, 1) // HEAD_DIM, spread, 0.0).astype(BF)
    grad_probs = dot(spread, values[...], NT)
    prob = probs[...].astype(F32)
    inner = jnp.sum(prob * grad_probs, -1, keepdims=True)
    grad_scores = (prob * (grad_probs - inner)).astype(BF).astype(F32)
    grad_scores = jnp.sum(grad_scores.reshape(mols, heads, length), 0)
    grad_values = dot(spread, probs[...], TN)
    sides[0:cols, :] = grad_values[0:cols, :].astype(BF)
    sides[cols:256, :] = jnp.concatenate([grad_scores, jnp.zeros((256 - cols - heads, length), F32)], 0).astype(BF)
    sums = dot(sides[...], normed[...])
    comb[...] = keyed[...].astype(F32).T.astype(BF)
    total[...] = jnp.zeros(total.shape, F32)
    gains[...] = jnp.zeros(gains.shape, F32)
    gain = vectors[0:1, :]

    def one_block(b, unused):
        here = pl.ds(pl.multiple_of(b * BLOCK, BLOCK), BLOCK)
        grad = dot(sides[:, here], comb[...], TN)
        hat_here = hats[here, :].astype(F32)
        low_grad = norm_back(grad, hat_here, invs[here, 0:1], gain).astype(BF)
        total[...] += dot(at[:, here], low_grad)
        gains[0:8, :] += jnp.sum((grad * hat_here).reshape(BLOCK // 8, 8, width), 0)
        gains[8:16, :] += jnp.sum(grad.reshape(BLOCK // 8, 8, width), 0)
        return 0

    lax.fori_loop(0, (filled + BLOCK - 1) // BLOCK, one_block, 0)
    grad_keys = sums[cols : cols + heads, :]
    turned = dot(grad_keys.astype(BF), w1[:, 128:384])
    lane = iota(turned.shape, 1) - 64
    picked = jnp.where((lane >= 0) & (lane // HEAD_DIM == iota(turned.shape, 0)), turned, 0.0)
    grad_query = jnp.sum(pltpu.roll(picked, 192, 1), 0, keepdims=True) * scale
    r = iota(side.shape, 0)
    side[...] = jnp.where(r == 0, grad_query, jnp.where(r == 1, head_rows[4:5, 0:256], 0.0))
    grad_query = jnp.broadcast_to(grad_query.astype(BF), (16, 256))
    grad_row = dot(grad_query, w1[:, 0:256], NT)[0:1, :]
    hat_start, inverse_start = norm_parts(vectors[8:9, :])
    start_row = (hat_start * gain + vectors[1:2, :]).astype(BF).astype(F32)
    first = jnp.where(group == 0, 1.0, 0.0)
    row_graph = norm_back(grad_row, hat_start, inverse_start, gain) + first * grad_start
    row_gain = jnp.sum(gains[0:8, :], 0, keepdims=True) + grad_row * hat_start
    row_shift = jnp.sum(gains[8:16, :], 0, keepdims=True) + grad_row
    base = TYPES + 32
    r = iota((FEATS - base, width), 0)
    extra = jnp.where(r == 2, row_graph, 0.0)
    extra = jnp.where(r == 3, row_gain, extra)
    extra = jnp.where(r == 4, row_shift, extra)
    extra = jnp.where(r == 5, first * grad_gain, extra)
    extra = jnp.where(r == 6, first * grad_shift, extra)
    for i in range(4):
        extra = jnp.where(r == 7 + i, first * head_rows[i : i + 1, :], extra)
    total[base:FEATS, :] += extra
    each = FEATS // nmp
    for k in range(nmp):
        start = pl.multiple_of((group ^ k) * each, 16)
        outs[k][...] = total[pl.ds(start, each), :].astype(BF)
    odd = lax.axis_index("dp") & 1
    even_share = jnp.where(odd == 0, 1.0, 0.0)
    lay = jnp.concatenate(
        [
            sums[0:cols, :],
            grad_one * even_share,
            grad_one * (1.0 - even_share),
            grad_keys,
            jnp.zeros((256 - cols - 2 * mols - heads, width), F32),
        ],
        0,
    )
    lay = lay.T.astype(BF)
    if nlayer == 1:
        layer_outs[0][...] = lay
    else:
        turned_lay = rest[nmp + nlayer + 5]
        turned_lay[...] = lay
        keep, send = layer_outs
        high, own = keep.shape[0], keep.shape[1]
        for z in range(high):
            keep[z] = turned_lay[pl.ds(pl.multiple_of((2 * z + odd) * own, 16), own), :]
            send[z] = turned_lay[pl.ds(pl.multiple_of((2 * z + 1 - odd) * own, 16), own), :]


def merge_kernel(nmp, owners, *refs):
    terms = refs[:nmp]
    layer_keep, layer_came, side_keep, side_came = refs[nmp : nmp + 4]
    high, deep = layer_keep.shape[0], layer_keep.shape[1]
    table_keep, table_send, side = refs[nmp + 4 : nmp + 7]
    outs = refs[nmp + 7 : nmp + 7 + high]
    layer_sum, table_sum = refs[nmp + 7 + high :]
    me = lax.axis_index("dp")
    odd, mine = me & 1, me >> 1
    for z in range(high):
        layer_sum[z] = (layer_keep[z].astype(F32) + layer_came[z].astype(F32)).astype(BF)
    for k in range(high):
        outs[k][...] = layer_sum[mine ^ k]
    side[...] = side_keep[...] + side_came[...]
    table_sum[...] = tree(terms)
    width = table_sum.shape[1]
    for z in range(0, high, 2):
        kept, sent = [], []
        for y in (z, z + 1):
            if 2 * y + 1 < owners:
                kept.append(table_sum[pl.ds(pl.multiple_of((2 * y + odd) * 8, 8), 8), :])
                sent.append(table_sum[pl.ds(pl.multiple_of((2 * y + 1 - odd) * 8, 8), 8), :])
            else:
                kept.append(jnp.zeros((8, width), F32))
                sent.append(jnp.zeros((8, width), F32))
        table_keep[z * 8 : z * 8 + 16, :] = jnp.concatenate(kept, 0)
        table_send[z * 8 : z * 8 + 16, :] = jnp.concatenate(sent, 0).astype(BF)


def table_kernel(keep, came, side, *outs):
    mine = lax.axis_index("dp") >> 1
    high = keep.shape[0] // 8
    width = keep.shape[1]
    summed = outs[high]
    summed[...] = keep[...] + came[...].astype(F32)
    for k in range(high):
        outs[k][:, 0:width] = summed[pl.ds(pl.multiple_of((mine ^ k) * 8, 8), 8), :]
        outs[k][:, width:] = side[...]


def sum_squares(value):
    return jnp.sum(jnp.sum(value * value, 0, keepdims=True), 1, keepdims=True)


def outer_kernel(own, dp, *refs):
    pieces = refs[:-6]
    head_grad, up_grad, down_grad, squares, packs, full = refs[-6:]
    me = lax.axis_index("dp")
    width = head_grad.shape[0]
    if len(pieces) == 1:
        packs[...] = pieces[0][...]
    mols = pieces[0].shape[0]
    slot = packs.shape[0] // dp
    for k, piece in enumerate(pieces[: dp if len(pieces) > 1 else 0]):
        rows = piece[...].astype(F32)
        rows = jnp.concatenate([rows, jnp.zeros((slot - mols, rows.shape[1]), F32)], 0).astype(BF)
        packs[pl.ds(pl.multiple_of((me ^ k) * slot, 16), slot), :] = rows
    grad = dot(packs[:, 0:width], packs[:, width : 2 * width], TN)
    head_grad[...] = grad
    head_square = sum_squares(grad)
    kept = up_grad.shape[0]
    start = 0 if kept == full.shape[0] else pl.multiple_of(me * own, 8)
    first = 4 * width
    grad = dot(packs[:, 2 * width : 3 * width], packs[:, first + 512 : first + 768], TN)
    square = sum_squares(grad)
    full[...] = grad
    up_grad[...] = full[pl.ds(start, kept), :]
    grad = dot(packs[:, 3 * width : 4 * width], packs[:, first + 256 : first + 512], TN)
    square += sum_squares(grad)
    full[...] = grad
    down_grad[...] = full[pl.ds(start, kept), :]
    squares[...] = jnp.where(iota((8, 128), 1) == 0, square, head_square)


def owner_kernel(own, cols, scale, dp, *refs):
    high = dp // 2
    table_parts, layer_parts, packs = refs[:high], refs[high : 2 * high], refs[2 * high : 2 * high + dp]
    query, vectors, layer, send, scalars = refs[2 * high + dp :]
    deep = layer_parts[0].shape[0]
    me = lax.axis_index("dp")
    even = (me & 1) == 0
    mols = packs[0].shape[0]
    width = vectors.shape[1]
    first = packs[0].shape[1] - 3 * 256
    acc = tree(layer_parts)
    summed = tree(table_parts)
    out_grad = jnp.zeros((deep, 256), F32)
    for j in range(high):
        near = packs[2 * j][:, first : first + 256].astype(F32)
        far = packs[2 * j + 1][:, first : first + 256].astype(F32)
        rows = [jnp.where(even, near, far), jnp.where(even, far, near)]
        rows = jnp.concatenate([jnp.zeros((64, 256), F32), *rows, jnp.zeros((64 - 2 * mols, 256), F32)], 0)
        out_grad += dot(layer_parts[j][:, 128:256], rows.astype(BF))
    keys = jnp.concatenate([jnp.zeros((64 + 2 * mols, 256), F32), query[...], jnp.zeros((56 - 2 * mols, 256), F32)], 0)
    key_grad = dot(acc[:, 128:256], keys, precision=HIGHEST) * scale
    hat, _ = norm_parts(vectors[8:9, :])
    start_row = (hat * vectors[0:1, :] + vectors[1:2, :]).astype(BF).astype(F32)
    here = iota((deep, width), 1) == iota((deep, width), 0) + me * own
    start_col = jnp.sum(jnp.where(here, start_row, 0.0), -1, keepdims=True)
    table, side = summed[:, 0:width], summed[:, width:]
    square = jnp.zeros((1, 1), F32)
    for j, grad in enumerate([start_col * side[0:1, :], key_grad, acc, out_grad]):
        grad = grad[0:own, 0:cols]
        layer[j] = grad
        square += sum_squares(grad)
    square += sum_squares(table)
    a, b, c = three(square)
    lane = iota((16, 128), 1)
    r = iota((16, 128), 0)
    tail = jnp.where(r == 0, jnp.where(lane == 0, a, jnp.where(lane == 1, b, jnp.where(lane == 2, c, 0.0))), 0.0)
    half = width // 2
    table = jnp.concatenate([table[:, 0:half], table[:, half:]], 0)
    packet = jnp.concatenate([table, tail], 1).astype(BF)
    for p in range(dp):
        send[p] = packet
    scalars[...] = jnp.broadcast_to(side[1:2, 0:128], scalars.shape)


def stats_kernel(cols, layer, up_grad, down_grad, left_roots, right_roots, left, right, shaped):
    for j in range(6):
        g = layer[j] if j < 4 else (up_grad if j == 4 else down_grad)[:, 0:cols]
        left[j] = dot(g, g, NT, HIGHEST)
        right[j] = dot(g, g, TN, HIGHEST)
        shaped[j] = dot(dot(left_roots[j], g, NN, HIGHEST), right_roots[j], NN, HIGHEST)


def adam(weight, first, second, grad, rate):
    first_new = BETA_ONE * first + (1.0 - BETA_ONE) * grad
    second_new = BETA_TWO * second + (1.0 - BETA_TWO) * grad * grad
    fixed_one = 1.0 - BETA_ONE**STEP
    fixed_two = 1.0 - BETA_TWO**STEP
    update = first_new * (1.0 / fixed_one) / (jnp.sqrt(second_new * (1.0 / fixed_two)) + ADAM_EPS)
    return first_new, second_new, weight - rate * (update + WEIGHT_DECAY * weight)


def update_kernel(nmp, owners, cols, *refs):
    packets, squares = refs[:nmp], refs[nmp : 2 * nmp]
    (
        scalars, layer, up_grad, down_grad, left_add, right_add, shaped, weights, left, right,
        tables, tables_m, tables_v, head, head_m, head_v, head_grad, vectors, vectors_m, vectors_v,
    ) = refs[2 * nmp : 2 * nmp + 20]
    loss_out, count_out, norm_out = refs[2 * nmp + 20 : 2 * nmp + 23]
    outs = refs[2 * nmp + 23 : 2 * nmp + 36]
    held = refs[2 * nmp + 36 : 2 * nmp + 49]
    grads, sems = refs[2 * nmp + 49 :]
    layer_out, weights_out, left_out, right_out, tm_out, tv_out, t_out, hm_out, hv_out, h_out, vm_out, vv_out, v_out = held
    started = []

    def send(i, rows=None):
        src, dst = held[i], outs[i]
        if rows is not None:
            src, dst = src.at[rows], dst.at[rows]
        copy = pltpu.make_async_copy(src, dst, sems.at[len(started)])
        copy.start()
        started.append(copy)

    parts = []
    for packet, ref in zip(packets, squares):
        s = ref[0:1, 0:1]
        for p in range(packet.shape[0]):
            tail = packet[p, :, 384:512].astype(F32)
            s += tail[0:1, 0:1] + tail[0:1, 1:2] + tail[0:1, 2:3]
        parts.append(s)
    while len(parts) > 1:
        parts = [parts[i] + parts[i + 1] for i in range(0, len(parts), 2)]
    square = parts[0] + squares[0][0:1, 1:2]
    loss, count = scalars[0:1, 0:1], scalars[0:1, 1:2]
    norm = jnp.sqrt(square) / count
    factor = CLIP / jnp.maximum(norm, CLIP) / count
    loss_out[...] = loss
    count_out[...] = count
    norm_out[...] = norm
    width = head.shape[0]
    each = width // 4
    for i in range(4):
        rows = slice(i * each, (i + 1) * each)
        hm_out[rows, :], hv_out[rows, :], h_out[rows, :] = adam(
            head[rows, :], head_m[rows, :], head_v[rows, :], head_grad[rows, :] * factor, RATE_HEAD
        )
        for k in (7, 8, 9):
            send(k, pl.ds(i * each, each))
    scale = (1.0 - STATS_DECAY) * factor * factor
    right_out[...] = STATS_DECAY * right[...] + scale[None] * right_add[...]
    send(3)
    left_out[...] = STATS_DECAY * left[...] + scale[None] * left_add[...]
    send(2)
    for j in range(6):
        span = slice(j * cols, (j + 1) * cols)
        g = layer[j] if j < 4 else (up_grad if j == 4 else down_grad)[:, 0:cols]
        layer_out[:, span] = g * factor
        weights_out[:, span] = weights[:, span] - RATE_LAYER * (shaped[j] * factor + WEIGHT_DECAY * weights[:, span])
    send(0)
    send(1)
    group = lax.axis_index("mp")
    share = FEATS // nmp
    half = 384
    for k in range(nmp):
        start = pl.multiple_of((group ^ k) * share, 8)
        for p in range(owners):
            piece = packets[k][p, :, 0:half].astype(F32)
            piece = jnp.concatenate([piece[0:8, :], piece[8:16, :]], 1) * factor
            grads[pl.ds(pl.multiple_of(start + p * 8, 8), 8), :] = piece
    rows = tables.shape[0]
    tm_out[...], tv_out[...], t_out[...] = adam(tables[...], tables_m[...], tables_v[...], grads[0:rows, :], RATE_TABLES)
    for k in (4, 5, 6):
        send(k)
    order = (3, 4, 5, 6, 7, 8, 0, 1, 2, 9, 10)
    r = iota((16, vectors.shape[1]), 0)
    tail = jnp.zeros(r.shape, F32)
    for i, o in enumerate(order):
        tail = jnp.where(r == i, grads[rows + o : rows + o + 1, :], tail)
    nrows = vectors.shape[0]
    vm_out[...], vv_out[...], v_out[...] = adam(vectors[...], vectors_m[...], vectors_v[...], tail[0:nrows, :], RATE_VECTORS)
    for k in (10, 11, 12):
        send(k)
    for copy in started:
        copy.wait()


def exchange(x, axis):
    n = lax.axis_size(axis)
    return [x] + [lax.ppermute(x, axis, [(i, i ^ k) for i in range(n)]) for k in range(1, n)]


def flip(x, k):
    n = lax.axis_size("dp")
    return lax.ppermute(x, "dp", [(i, i ^ k) for i in range(n)])


def after(values, *others):
    return lax.optimization_barrier((tuple(values), tuple(others)))[0]


def gather_rows(x):
    if lax.axis_size("dp") != 8 or x.shape[0] % 16:
        return [lax.all_gather(x, "dp", axis=0, tiled=True)]
    return spread(x, (), ())


def spread(x, second, third):
    four, one, two = after([flip(x, 4), flip(x, 1), flip(x, 2)], *second)
    far = after([flip(one, 2), flip(four, 2), flip(four, 1)], *third)
    return [x, one, two, far[0], four, far[2], far[1], flip(far[1], 1)]


def per_device(
    lap_vectors,
    eig_index,
    type_ids,
    seg_ids,
    targets,
    layer_weights,
    left_stats,
    right_stats,
    left_roots,
    right_roots,
    tables,
    tables_m,
    tables_v,
    head_weight,
    head_m,
    head_v,
    vectors,
    vectors_m,
    vectors_v,
):
    dp = lax.axis_size("dp")
    nmp = lax.axis_size("mp")
    length = seg_ids.shape[1]
    mols = targets.shape[1]
    width = vectors.shape[1]
    own, group_cols = layer_weights.shape[0], layer_weights.shape[1]
    cols = group_cols // 6
    heads = cols // HEAD_DIM
    scale = HEAD_DIM ** (-0.5)
    owners = FEATS // nmp // 8

    w = layer_weights.astype(BF)
    ones = gather_rows(w[:, : 4 * cols])
    twos = gather_rows(w[:, 4 * cols :])
    np_ = len(ones)

    sources = [lap_vectors[0].T, eig_index[0].T, type_ids, seg_ids, tables, vectors]
    at, normed, hats, invs = call(
        functools.partial(embed_kernel, mols),
        [sds((FEATS, length), BF), sds((length, width), BF), sds((length, width), BF), sds((length, 128), F32)],
        sources,
        [pltpu.VMEM(x.shape, x.dtype) for x in sources]
        + [pltpu.VMEM((FEATS, width), BF), pltpu.VMEM((FEATS, width), BF), pltpu.VMEM((8, length), I32), pltpu.SemaphoreType.DMA((6,))],
        flops=4 * length * FEATS * width,
        in_specs=[IN_PLACE] * 6,
    )
    part, probs, values, ctx, keyed, query, w1 = call(
        functools.partial(attn_kernel, np_, mols, heads, scale),
        [
            sds((mols, width), BF),
            sds((mols * heads, length), BF),
            sds((length, 256), BF),
            sds((mols, 256), BF),
            sds((width, 256), BF),
            sds((8, 256), F32),
            sds((width, 4 * cols), BF),
        ],
        [normed, seg_ids, vectors, *ones],
        flops=4 * length * 256 * width,
    )
    part, resid_one, normed_two, hidden, act, w2 = call(
        functools.partial(ffn_kernel, np_, nmp, cols),
        [
            sds((mols, width), BF),
            sds((mols, width), F32),
            sds((mols, width), BF),
            sds((mols, 256), F32),
            sds((mols, 256), BF),
            sds((width, 2 * cols), BF),
        ],
        [*exchange(part, "mp"), vectors, *twos],
        flops=4 * mols * width * 256,
    )
    part, pack, grad_two, head_rows = call(
        functools.partial(head_kernel, nmp, cols),
        [sds((mols, width), BF), sds((mols, 4 * width + 768), BF), sds((mols, width), F32), sds((8, width), F32)],
        [*exchange(part, "mp"), resid_one, vectors, head_weight, targets, seg_ids, normed_two, ctx, hidden, act, w2],
        [pltpu.VMEM((width, width), BF)],
        flops=4 * width * width * mols,
    )
    odd = lax.axis_index("dp") & 1
    high = dp // 2
    deep = (own + 15) // 16 * 16
    simple = own == deep
    layer_shape = [sds((high, own, 256), BF)] * 2 if simple else [sds((width, 256), BF)]
    nlayer = len(layer_shape)
    back = call(
        functools.partial(back_kernel, nmp, nlayer, mols, heads, scale),
        [sds((FEATS // nmp, width), BF) for _ in range(nmp)] + layer_shape + [sds((8, 256), F32)],
        [
            *exchange(part, "mp"), resid_one, grad_two, head_rows, vectors, keyed, probs, values, normed, hats, invs, at,
            seg_ids, w1,
        ],
        [
            pltpu.VMEM((256, length), BF),
            pltpu.VMEM((256, width), BF),
            pltpu.VMEM((FEATS, width), F32),
            pltpu.VMEM((16, width), F32),
            pltpu.VMEM((width, 256), BF),
        ],
        flops=8 * length * 256 * width,
    )
    shares, side = back[:nmp], back[nmp + nlayer]
    if simple:
        layer_keep, layer_send = back[nmp], back[nmp + 1]
    else:
        both = back[nmp].reshape(high, 2, own, 256)
        both = jnp.pad(both, ((0, 0), (0, 0), (0, deep - own), (0, 0)))
        layer_keep, layer_send = [lax.dynamic_index_in_dim(both, i, 1, False) for i in (odd, 1 - odd)]
    moved = [shares[0]] + [lax.ppermute(shares[k], "mp", [(i, i ^ k) for i in range(nmp)]) for k in range(1, nmp)]
    merged = call(
        functools.partial(merge_kernel, nmp, owners),
        [sds((high * 8, width), F32), sds((high * 8, width), BF), sds((8, 256), F32)] + [sds((deep, 256), BF)] * high,
        [*moved, layer_keep, flip(layer_send, 1), side, flip(side, 1)],
        [pltpu.VMEM((high, deep, 256), BF), pltpu.VMEM((FEATS // nmp, width), F32)],
    )
    table_keep, table_send, side, *layer_parts = merged
    if dp == 8:
        packs = spread(pack, (shares[0],), (table_keep,))
        contexts = packs
    else:
        packs = lax.all_gather(pack, "dp", axis=0)
        near = packs[:, :, 4 * width :]
        contexts = [lax.dynamic_index_in_dim(near, lax.axis_index("dp") ^ k, 0, False) for k in range(dp)]
        packs = [jnp.pad(packs, ((0, 0), (0, 32 - mols), (0, 0))).reshape(dp * 32, -1)]
    layer_parts = [layer_parts[0]] + [flip(layer_parts[k], 2 * k) for k in range(1, high)]
    table_parts = call(
        table_kernel,
        [sds((8, width + 256), F32)] * high,
        [table_keep, flip(table_send, 1), side],
        [pltpu.VMEM((high * 8, width), F32)],
    )
    table_parts = [table_parts[0]] + [flip(table_parts[k], 2 * k) for k in range(1, high)]
    layer, send, scalars = call(
        functools.partial(owner_kernel, own, cols, scale, dp),
        [sds((4, own, cols), F32), sds((dp, 16, 512), BF), sds((8, 128), F32)],
        [*table_parts, *layer_parts, *contexts, query, vectors],
        flops=2 * own * 256 * 1024,
    )
    sums = lax.all_to_all(send, "dp", 0, 0, tiled=True)
    kept = width if own % 8 else own
    head_grad, up_grad, down_grad, squares = call(
        functools.partial(outer_kernel, own, dp),
        [sds((width, width), F32), sds((kept, 256), F32), sds((kept, 256), F32), sds((8, 128), F32)],
        packs,
        [pltpu.VMEM((dp * 32, pack.shape[1]), BF), pltpu.VMEM((width, 256), F32)],
        vmem=16 + dp // 4,
        flops=2 * dp * mols * width * (width + 512),
    )
    sums = exchange(sums, "mp")
    squares = exchange(squares, "mp")
    if kept != own:
        up_grad, down_grad = [lax.dynamic_slice_in_dim(x, lax.axis_index("dp") * own, own) for x in (up_grad, down_grad)]
    left_add, right_add, shaped = call(
        functools.partial(stats_kernel, cols),
        [sds((6, own, own), F32), sds((6, cols, cols), F32), sds((6, own, cols), F32)],
        [layer, up_grad, down_grad, jnp.swapaxes(left_roots, 0, 1), right_roots[0]],
        flops=12 * 6 * own * cols * (2 * own + 2 * cols),
    )
    results = [
        sds((own, group_cols), F32),
        sds((own, group_cols), F32),
        sds((6, own, own), F32),
        sds((6, cols, cols), F32),
        *[sds(tables.shape, F32)] * 3,
        *[sds(head_weight.shape, F32)] * 3,
        *[sds(vectors.shape, F32)] * 3,
    ]
    outs = call(
        functools.partial(update_kernel, nmp, owners, cols),
        [sds((1, 1), F32)] * 3 + results,
        [
            *sums, *squares, scalars, layer, up_grad, down_grad, left_add, right_add, shaped, layer_weights,
            jnp.swapaxes(left_stats, 0, 1), right_stats[0], tables, tables_m, tables_v, head_weight, head_m, head_v, head_grad,
            vectors, vectors_m, vectors_v,
        ],
        [pltpu.VMEM(x.shape, x.dtype) for x in results] + [pltpu.VMEM((FEATS, width), F32), pltpu.SemaphoreType.DMA((22,))],
        flops=20 * width * width,
        vmem=24,
        out_specs=[IN_VMEM] * 3 + [IN_PLACE] * 13,
    )
    loss, count, norm, layer_grad, layer_new, left_new, right_new, tm, tv, tn, hm, hv, hn, vm, vv, vn = outs
    return (
        loss.reshape(()),
        count.reshape(()),
        norm.reshape(()),
        layer_grad,
        layer_new,
        jnp.swapaxes(left_new, 0, 1),
        right_new[None],
        tm,
        tv,
        tn,
        hm,
        hv,
        hn,
        vm,
        vv,
        vn,
    )


def solution(mesh):
    placed = (
        P("dp", None, None),
        P("dp", None, None),
        P("dp", None),
        P("dp", None),
        P("dp", None),
        P("dp", "mp"),
        P("dp", "mp", None),
        P("dp", "mp", None, None),
        P("dp", "mp", None),
        P("dp", "mp", None, None),
        *[P()] * 9,
    )
    return jax.shard_map(
        per_device,
        mesh=mesh,
        in_specs=placed,
        out_specs=(
            P(),
            P(),
            P(),
            P("dp", "mp"),
            P("dp", "mp"),
            P("dp", "mp", None),
            P("dp", "mp", None, None),
            *[P()] * 9,
        ),
        check_vma=False,
    )
```

```python
import functools
import math

import jax
import jax.numpy as jnp
from jax import lax
from jax.experimental import pallas as pl
from jax.experimental.pallas import tpu as pltpu
from jax.sharding import PartitionSpec as P

HEAD_DIM = 24
TYPES = 192
STEP = 10
NORM_EPS = 1e-05
CLIP = 0.25
STATS_DECAY = 0.95
RATE_LAYER = 0.15
RATE_TABLES = 0.15
RATE_HEAD = 0.01
RATE_VECTORS = 0.2
BETA_ONE = 0.9
BETA_TWO = 0.99
ADAM_EPS = 1e-08
WEIGHT_DECAY = 0.01
MASKED = -1000000000.0
GELU_C = 0.7978845608028654
GELU_A = 0.044715

BF = jnp.bfloat16
F32 = jnp.float32
I32 = jnp.int32
HIGHEST = lax.Precision.HIGHEST
NN = ((1,), (0,))
NT = ((1,), (1,))
TN = ((0,), (0,))
BLOCK = 256
FEATS = 256
MIB = 1024 * 1024


def dot(a, b, dims=NN, precision=None):
    return lax.dot_general(a, b, (dims, ((), ())), preferred_element_type=F32, precision=precision)


def iota(shape, dim):
    return lax.broadcasted_iota(I32, shape, dim)


IN_VMEM = pl.BlockSpec(memory_space=pltpu.VMEM)
IN_PLACE = pl.BlockSpec(memory_space=pltpu.HBM)


def call(kernel, outs, ins, scratch=(), flops=0, vmem=16, in_specs=None, out_specs=None):
    moved = sum(math.prod(x.shape) * x.dtype.itemsize for x in list(ins) + list(outs))
    return pl.pallas_call(
        kernel,
        out_shape=tuple(outs),
        in_specs=in_specs or [IN_VMEM] * len(ins),
        out_specs=tuple(out_specs or [IN_VMEM] * len(outs)),
        scratch_shapes=list(scratch),
        compiler_params=pltpu.CompilerParams(vmem_limit_bytes=vmem * MIB),
        cost_estimate=pl.CostEstimate(flops=flops, bytes_accessed=moved, transcendentals=0),
    )(*ins)


def in_hbm(x):
    return pltpu.with_memory_space_constraint(x, pltpu.HBM)


def in_vmem(x):
    return pltpu.with_memory_space_constraint(x, pltpu.VMEM)


def sds(shape, dtype):
    return jax.ShapeDtypeStruct(shape, dtype)


def norm_parts(values):
    center = values - jnp.mean(values, -1, keepdims=True)
    spread = jnp.mean(center * center, -1, keepdims=True)
    inverse = lax.rsqrt(spread + NORM_EPS)
    return center * inverse, inverse


def norm_back(grad, hat, inverse, gain):
    scaled = grad * gain
    mean_one = jnp.mean(scaled, -1, keepdims=True)
    mean_two = jnp.mean(scaled * hat, -1, keepdims=True)
    return inverse * (scaled - mean_one - hat * mean_two)


def gelu_pair(x):
    t = jnp.tanh(GELU_C * (x + GELU_A * x * x * x))
    value = 0.5 * x * (1.0 + t)
    slope = 0.5 * (1.0 + t) + 0.5 * x * (1.0 - t * t) * (GELU_C * (1.0 + 3.0 * GELU_A * x * x))
    return value, slope


def tree(refs):
    parts = [r[...].astype(F32) for r in refs]
    while len(parts) > 1:
        parts = [parts[i] + parts[i + 1] for i in range(0, len(parts), 2)]
    return parts[0]


def three(x):
    high = x.astype(BF).astype(F32)
    mid = (x - high).astype(BF).astype(F32)
    return high, mid, x - high - mid


def assemble(pieces, first, second, owner):
    rows = pieces[0].shape[0]
    split = first.shape[1]
    for k, piece in enumerate(pieces):
        here = pl.ds(0 if len(pieces) == 1 else pl.multiple_of((owner ^ k) * rows, 16), rows)
        first[here, :] = piece[:, 0:split]
        second[here, :] = piece[:, split:]


def embed_kernel(mols, *refs):
    sources, (at, normed, hats, invs), held, (high, low, prev, sems) = refs[:6], refs[6:10], refs[10:16], refs[16:]
    copies = [pltpu.make_async_copy(a, b, sems.at[i]) for i, (a, b) in enumerate(zip(sources, held))]
    for copy in copies:
        copy.start()
    normed[...] = jnp.zeros(normed.shape, BF)
    for copy in copies:
        copy.wait()
    lap, eig, kinds, seg, tables, vectors = held
    length = seg.shape[1]
    width = vectors.shape[1]
    rows = tables.shape[0]
    tab = tables[...]
    tab_high = tab.astype(BF)
    high[0:rows, :] = tab_high
    rest = jnp.where(iota(tab.shape, 0) < TYPES, tab - tab_high.astype(F32), 0.0)
    low[0:rows, :] = rest.astype(BF)
    r = iota((FEATS - rows, width), 0)
    extra = jnp.where(r == 0, vectors[6:7, :], jnp.where(r == 1, vectors[7:8, :], jnp.where(r == 2, vectors[8:9, :], 0.0)))
    extra_high = extra.astype(BF)
    high[rows:FEATS, :] = extra_high
    low[rows:FEATS, :] = (extra - extra_high.astype(F32)).astype(BF)
    seg_row = seg[...]
    before = pltpu.roll(jnp.broadcast_to(seg_row, (8, length)), 1, 1)
    before = jnp.where(iota((8, length), 1) == 0, -1, before)
    prev[...] = before
    filled = jnp.sum((seg_row != mols).astype(F32)).astype(I32)
    gain = vectors[0:1, :]
    shift = vectors[1:2, :]
    window = 2 * BLOCK

    def one_block(b, unused):
        start = pl.multiple_of(b * BLOCK, BLOCK)
        here = pl.ds(start, BLOCK)
        first = pl.multiple_of(jnp.clip(start - 128, 0, length - window), 128)
        source = iota((window, BLOCK), 0) + first
        one = eig[0:1, here]
        two = eig[1:2, here]
        near = lap[:, pl.ds(first, window)].astype(BF)
        pair_one = dot(near, (source == one).astype(F32).astype(BF))
        pair_two = dot(near, (source == two).astype(F32).astype(BF))
        seg_here = seg[0:1, here]
        begins = (seg_here != mols) & (seg_here != prev[0:1, here])
        kind = jnp.where(begins, -1, kinds[0:1, here])
        keep = jnp.where(begins, 0.0, 1.0)
        at[0:TYPES, here] = (iota((TYPES, BLOCK), 0) == kind).astype(F32).astype(BF)
        half = pair_one.shape[0]
        at[TYPES : TYPES + half, here] = (pair_one * keep).astype(BF)
        at[TYPES + half : rows, here] = (pair_two * keep).astype(BF)
        which = jnp.where(begins, 2, jnp.where(one == two, 0, 1))
        at[rows:FEATS, here] = (iota((FEATS - rows, BLOCK), 0) == which).astype(F32).astype(BF)
        picks = at[:, here]
        resid = dot(picks, high[...], TN) + dot(picks, low[...], TN)
        hat, inverse = norm_parts(resid)
        normed[here, :] = (hat * gain + shift).astype(BF)
        hats[here, :] = hat.astype(BF)
        invs[here, :] = jnp.broadcast_to(inverse, (BLOCK, 128))
        return 0

    lax.fori_loop(0, (filled + BLOCK - 1) // BLOCK, one_block, 0)


def attn_kernel(npiece, mols, heads, scale, *refs):
    normed, seg, vectors = refs[:3]
    ones = refs[3 : 3 + npiece]
    part, probs, values, ctx_out, keyed, query_out, w1, w2 = refs[3 + npiece :]
    assemble(ones, w1, w2, lax.axis_index("dp"))
    width = vectors.shape[1]
    cols = heads * HEAD_DIM
    hat, _ = norm_parts(vectors[8:9, :])
    start_row = (hat * vectors[0:1, :] + vectors[1:2, :]).astype(BF)
    q = dot(jnp.broadcast_to(start_row, (16, width)), w1[:, 0:256])
    q = q.astype(BF).astype(F32)
    q = jnp.where(iota((16, 256), 1) < cols, q, 0.0)
    r = iota((16, 256), 0)
    head_of = iota((16, 256), 1) // HEAD_DIM
    query_out[...] = jnp.where(r == head_of, q, 0.0)[0:8, :]
    shifted = pltpu.roll(q, 64, 1)[0:1, :]
    r = iota((128, 256), 0)
    lane = iota((128, 256), 1) - 64
    pick = (lane >= 0) & ((r & 7) == lane // HEAD_DIM) & (r >= 64) & (r < 80)
    q_keys = jnp.where(pick, shifted, 0.0).astype(BF)
    u = dot(w1[:, 128:384], q_keys, NT)
    u_high = u.astype(BF)
    lane = iota(u.shape, 1)
    u_both = jnp.where(lane < 72, u_high.astype(F32), u - u_high.astype(F32))
    last = w1[:, 512:640].astype(F32)
    side = jnp.where(lane < 64, last, u_both).astype(BF)
    keyed[:, 0:128] = w1[:, 384:512]
    keyed[:, 128:256] = jnp.where(lane < 64, last, jnp.where(lane < 72, u * scale, 0.0)).astype(BF)
    normed_all = normed[...]
    values[:, 0:128] = dot(normed_all, w1[:, 384:512]).astype(BF)
    second = dot(normed_all, side)
    values[:, 128:256] = jnp.where(iota(second.shape, 1) < 64, second, 0.0).astype(BF)
    turned = second.T
    scores = (turned[64:72, :] + turned[72:80, :]) * scale
    seg_row = seg[...]
    length = seg_row.shape[1]
    mine = iota((mols, 1, length), 0) == seg_row[None]
    masked = jnp.where(mine, scores[None], MASKED)
    peak = jnp.max(masked, -1, keepdims=True)
    grown = jnp.where(mine, jnp.exp(masked - peak), 0.0)
    total = jnp.sum(grown, -1, keepdims=True)
    total = jnp.where(total > 0.0, total, 1.0)
    prob = (grown / total).reshape(mols * heads, length).astype(BF)
    probs[...] = prob
    wide = dot(prob, values[...])
    r = iota(wide.shape, 0) & (heads - 1)
    wide = jnp.where(r == iota(wide.shape, 1) // HEAD_DIM, wide, 0.0)
    ctx = jnp.sum(wide.reshape(mols, heads, 256), 1)
    ctx_out[...] = ctx.astype(BF)
    turned_ctx = pltpu.roll(ctx, 64, 1).astype(BF)
    part[...] = dot(turned_ctx, w1[:, 512:768], NT).astype(BF)


def ffn_kernel(nmp, cols, *refs):
    terms = refs[:nmp]
    vectors, w2, part, resid_out, normed_out, hidden_out, act_out = refs[nmp:]
    resid = vectors[8:9, :] + tree(terms)
    resid_out[...] = resid
    hat, _ = norm_parts(resid)
    low = (hat * vectors[2:3, :] + vectors[3:4, :]).astype(BF)
    normed_out[...] = low
    hidden = dot(low, w2[:, 0:256])
    hidden = jnp.where(iota(hidden.shape, 1) < cols, hidden, 0.0)
    hidden_out[...] = hidden
    act, _ = gelu_pair(hidden)
    act_out[...] = act.astype(BF)
    turned = pltpu.roll(act, 64, 1).astype(BF)
    part[...] = dot(turned, w2[:, 128:384], NT).astype(BF)


def head_kernel(nmp, cols, *refs):
    terms = refs[:nmp]
    resid_one, vectors, head, targets, seg, hidden, w2 = refs[nmp : nmp + 7]
    part, pack, grad_out, low_out, hidden_out, rows_out, head_low = refs[nmp + 7 :]
    width = vectors.shape[1]
    mols = targets.shape[1]
    head_low[...] = head[...].astype(BF)
    resid = resid_one[...] + tree(terms)
    hat, inverse = norm_parts(resid)
    gain = vectors[4:5, :]
    low = (hat * gain + vectors[5:6, :]).astype(BF)
    mid = dot(low, head_low[...]) + vectors[9:10, :]
    act_head, slope = gelu_pair(mid)
    act_head = act_head.astype(BF).astype(F32)
    readout = vectors[10:11, :].astype(BF).astype(F32)
    predicted = jnp.sum(act_head * readout, -1, keepdims=True)
    spot = iota((mols, mols), 0) == iota((mols, mols), 1)
    goal = jnp.sum(jnp.where(spot, targets[...], 0.0), -1, keepdims=True)
    seg_row = seg[...]
    there = iota((mols, seg_row.shape[1]), 0) == seg_row
    present = jnp.max(there.astype(F32), -1, keepdims=True)
    error = predicted - goal
    root = jnp.sqrt(error * error + 1.0)
    loss = jnp.sum(present * (root - 1.0), 0, keepdims=True)
    count = jnp.sum(present, 0, keepdims=True)
    grad_pred = present * error / root
    grad_readout = jnp.sum(grad_pred * act_head, 0, keepdims=True)
    grad_mid = (grad_pred * readout * slope).astype(BF)
    grad_bias = jnp.sum(grad_mid.astype(F32), 0, keepdims=True)
    grad_rows = dot(grad_mid, head_low[...], NT)
    grad_gain = jnp.sum(grad_rows * hat, 0, keepdims=True)
    grad_shift = jnp.sum(grad_rows, 0, keepdims=True)
    grad_two = norm_back(grad_rows, hat, inverse, gain)
    grad_out[...] = grad_two
    grad_low = grad_two.astype(BF)
    grad_act = dot(grad_low, w2[:, 128:384])
    grad_act = pltpu.roll(grad_act, 192, 1)
    _, slope_hidden = gelu_pair(hidden[...])
    grad_hidden = jnp.where(iota(grad_act.shape, 1) < cols, grad_act * slope_hidden, 0.0).astype(BF)
    part[...] = dot(grad_hidden, w2[:, 0:256], NT).astype(BF)
    pack[:, 0:width] = low
    pack[:, width : 2 * width] = grad_mid
    low_out[...] = grad_low
    hidden_out[...] = grad_hidden
    r = iota((8, width), 0)
    lane = iota((8, width), 1)
    scalars = jnp.where(lane == 0, loss, jnp.where(lane == 1, count, 0.0))
    rows_out[...] = jnp.where(
        r == 0,
        grad_gain,
        jnp.where(r == 1, grad_shift, jnp.where(r == 2, grad_bias, jnp.where(r == 3, grad_readout, jnp.where(r == 4, scalars, 0.0)))),
    )


def parts_for(rows, keep, send, each, odd, high, number=1):
    for z in range(high):
        for i in range(number):
            keep[z * number + i] = rows[pl.ds(pl.multiple_of(((2 * z + odd) * number + i) * each, 16), each), :]
            send[z * number + i] = rows[pl.ds(pl.multiple_of(((2 * z + 1 - odd) * number + i) * each, 16), each), :]


def ffn_grad_kernel(nlayer, high, normed, grad_hidden, grad_low, act, pack, keyed, *refs):
    outs, (comb, rows) = refs[:nlayer], refs[nlayer:]
    comb[...] = keyed[...].astype(F32).T.astype(BF)
    up = dot(normed[...], grad_hidden[...], TN)
    turned = pltpu.roll(act[...].astype(F32), 64, 1).astype(BF)
    down = dot(grad_low[...], turned, TN)
    target = rows if nlayer == 2 else outs[0]
    target[:, 0:128] = up[:, 0:128].astype(BF)
    target[:, 128:256] = (up[:, 128:256] + down[:, 0:128]).astype(BF)
    target[:, 256:384] = down[:, 128:256].astype(BF)
    if nlayer == 2:
        half = outs[0].shape[1]
        parts_for(rows, *outs, half, lax.axis_index("dp") & 1, high, 2)
        if outs[0].shape[0] > 2 * high:
            width = pack.shape[1] // 2
            lanes = pack[...].astype(F32)
            lanes = jnp.where((lax.axis_index("mp") & 1) == 0, lanes[:, 0:width], lanes[:, width:])
            lanes = jnp.concatenate([lanes[:, 0:384], lanes[:, 384:768]], 0).astype(BF)
            outs[0][2 * high] = lanes
            outs[1][2 * high] = lanes


def attn_back_kernel(nmp, nlayer, high, mols, heads, scale, *refs):
    terms = refs[:nmp]
    resid_one, grad_two, head_rows, vectors, probs, values, normed, w1, ctx = refs[nmp : nmp + 9]
    layer_outs = refs[nmp + 9 : nmp + 9 + nlayer]
    side, key_rows, sides, extras, turned_lay = refs[nmp + 9 + nlayer :]
    group = lax.axis_index("mp")
    width = vectors.shape[1]
    length = probs.shape[1]
    cols = heads * HEAD_DIM
    grad_normed = tree(terms)
    hat, inverse = norm_parts(resid_one[...])
    grad_gain = jnp.sum(grad_normed * hat, 0, keepdims=True)
    grad_shift = jnp.sum(grad_normed, 0, keepdims=True)
    grad_one = grad_two[...] + norm_back(grad_normed, hat, inverse, vectors[2:3, :])
    low = grad_one.astype(BF)
    grad_start = jnp.sum(low.astype(F32), 0, keepdims=True)
    grad_ctx = pltpu.roll(dot(low, w1[:, 512:768]), 192, 1).astype(BF).astype(F32)
    spread_ctx = jnp.broadcast_to(grad_ctx[:, None, :], (mols, heads, 256)).reshape(mols * heads, 256)
    r = iota(spread_ctx.shape, 0) & (heads - 1)
    spread_ctx = jnp.where(r == iota(spread_ctx.shape, 1) // HEAD_DIM, spread_ctx, 0.0).astype(BF)
    grad_probs = dot(spread_ctx, values[...], NT)
    prob = probs[...].astype(F32)
    inner = jnp.sum(prob * grad_probs, -1, keepdims=True)
    grad_scores = (prob * (grad_probs - inner)).astype(BF).astype(F32)
    grad_scores = jnp.sum(grad_scores.reshape(mols, heads, length), 0)
    grad_values = dot(spread_ctx, probs[...], TN)
    sides[0:cols, :] = grad_values[0:cols, :].astype(BF)
    sides[cols:256, :] = jnp.concatenate([grad_scores, jnp.zeros((256 - cols - heads, length), F32)], 0).astype(BF)
    sums = dot(sides[...], normed[...])
    turned_ctx = pltpu.roll(ctx[...].astype(F32), 64, 1).astype(BF)
    out_grad = dot(low, turned_ctx, TN)
    r = iota(sums.shape, 0)
    value_grad = jnp.where(r < cols, sums, 0.0).T
    lay = layer_outs[0] if nlayer == 1 else turned_lay
    lay[:, 0:128] = value_grad[:, 0:128].astype(BF)
    lay[:, 128:256] = (value_grad[:, 128:256] + out_grad[:, 0:128]).astype(BF)
    lay[:, 256:384] = out_grad[:, 128:256].astype(BF)
    if nlayer == 2:
        parts_for(lay, *layer_outs, layer_outs[0].shape[1], lax.axis_index("dp") & 1, high)
    gain = vectors[0:1, :]
    grad_keys = sums[cols : cols + heads, :]
    key_rows[...] = grad_keys
    turned = dot(grad_keys.astype(BF), w1[:, 128:384])
    lane = iota(turned.shape, 1) - 64
    picked = jnp.where((lane >= 0) & (lane // HEAD_DIM == iota(turned.shape, 0)), turned, 0.0)
    grad_query = jnp.sum(pltpu.roll(picked, 192, 1), 0, keepdims=True) * scale
    r = iota(side.shape, 0)
    side[...] = jnp.where(r == 0, grad_query, jnp.where(r == 1, head_rows[4:5, 0:256], 0.0))
    grad_query = jnp.broadcast_to(grad_query.astype(BF), (16, 256))
    grad_row = dot(grad_query, w1[:, 0:256], NT)[0:1, :]
    hat_start, inverse_start = norm_parts(vectors[8:9, :])
    first = jnp.where(group == 0, 1.0, 0.0)
    row_graph = norm_back(grad_row, hat_start, inverse_start, gain) + first * grad_start
    r = iota(extras.shape, 0)
    extra = jnp.where(r == 2, row_graph, 0.0)
    extra = jnp.where(r == 3, grad_row * hat_start, extra)
    extra = jnp.where(r == 4, grad_row, extra)
    extra = jnp.where(r == 5, first * grad_gain, extra)
    extra = jnp.where(r == 6, first * grad_shift, extra)
    for i in range(4):
        extra = jnp.where(r == 7 + i, first * head_rows[i : i + 1, :], extra)
    extras[...] = extra


def embed_back_kernel(nmp, mols, *refs):
    sides, comb, extras, vectors, hats, invs, at, seg = refs[:8]
    outs, (total, gains) = refs[8 : 8 + nmp], refs[8 + nmp :]
    width = vectors.shape[1]
    filled = jnp.sum((seg[...] != mols).astype(F32)).astype(I32)
    total[...] = jnp.zeros(total.shape, F32)
    gains[...] = jnp.zeros(gains.shape, F32)
    gain = vectors[0:1, :]

    def one_block(b, unused):
        here = pl.ds(pl.multiple_of(b * BLOCK, BLOCK), BLOCK)
        grad = dot(sides[:, here], comb[...], TN)
        hat_here = hats[here, :].astype(F32)
        low_grad = norm_back(grad, hat_here, invs[here, 0:1], gain).astype(BF)
        total[...] += dot(at[:, here], low_grad)
        gains[0:8, :] += jnp.sum((grad * hat_here).reshape(BLOCK // 8, 8, width), 0)
        gains[8:16, :] += jnp.sum(grad.reshape(BLOCK // 8, 8, width), 0)
        return 0

    lax.fori_loop(0, (filled + BLOCK - 1) // BLOCK, one_block, 0)
    base = FEATS - extras.shape[0]
    r = iota(extras.shape, 0)
    extra = extras[...] + jnp.where(r == 3, jnp.sum(gains[0:8, :], 0, keepdims=True), 0.0)
    extra += jnp.where(r == 4, jnp.sum(gains[8:16, :], 0, keepdims=True), 0.0)
    total[base:FEATS, :] += extra
    group = lax.axis_index("mp")
    each = FEATS // nmp
    for k in range(nmp):
        start = pl.multiple_of((group ^ k) * each, 16)
        outs[k][...] = total[pl.ds(start, each), :].astype(BF)


def loss_row(value, count, lanes):
    a, b, c = three(value)
    lane = iota((1, lanes), 1)
    return jnp.where(lane == 0, a, jnp.where(lane == 1, b, jnp.where(lane == 2, c, jnp.where(lane == 3, count, 0.0))))


def merge_table_kernel(nmp, owners, own, high, *refs):
    terms = refs[:nmp]
    side, key_rows, table_keep, table_send, table_sum, key_sum = refs[nmp:]
    odd = lax.axis_index("dp") & 1
    table_sum[...] = tree(terms)
    half = table_sum.shape[1] // 2
    query = jnp.concatenate([side[0:1, :], jnp.zeros((1, 128), F32)], 1)
    scal = loss_row(side[1:2, 0:1], side[1:2, 1:2], 384)
    r = iota((8, 384), 0)
    scal = jnp.where(r == 0, query, jnp.where(r == 1, scal, 0.0))
    fill = jnp.zeros((8, 384 - own), F32)
    for p in range(2 * high):
        key_sum[p] = jnp.concatenate([key_rows[:, p * own : (p + 1) * own], fill], 1)
    for z in range(high):
        for out, x in ((table_keep, odd), (table_send, 1 - odd)):
            p = 2 * z + x
            if 2 * z < owners:
                each = table_sum[pl.ds(pl.multiple_of(p * 8, 8), 8), :]
            else:
                each = jnp.zeros((8, 2 * half), F32)
            out[z] = jnp.concatenate([each[:, 0:half], each[:, half:], key_sum[p], scal], 0).astype(BF)


def merge_kernel(layer_keep, layer_came, table_keep, table_came, *outs):
    deep = layer_keep.shape[1]
    mine = lax.axis_index("dp") >> 1
    r = iota((16, 384), 0)
    for k, out in enumerate(outs):
        z = mine ^ k
        out[0:deep, :] = (layer_keep[z].astype(F32) + layer_came[z].astype(F32)).astype(BF)
        out[deep : deep + 16, :] = (table_keep[z, 0:16].astype(F32) + table_came[z, 0:16].astype(F32)).astype(BF)
        both = table_keep[z, 16:32].astype(F32) + table_came[z, 16:32].astype(F32)
        loss = both[9:10, 0:1] + both[9:10, 1:2] + both[9:10, 2:3]
        out[deep + 16 :, :] = jnp.where(r == 9, loss_row(loss, both[9:10, 3:4], 384), both).astype(BF)


def ffn_all_kernel(keep, came, *outs):
    mine = lax.axis_index("dp") >> 1
    for k, out in enumerate(outs):
        out[...] = (keep[mine ^ k].astype(F32) + came[mine ^ k].astype(F32)).astype(BF)


def ffn_x_kernel(keep, came, near_keep, near_send, pair):
    me = lax.axis_index("dp")
    odd, side = me & 1, (me >> 1) & 1
    for out, s in ((near_keep, side), (near_send, 1 - side)):
        for h in range(2):
            for i in range(2):
                p = (2 * h + s) * 2 + i
                out[h, i * 48 : (i + 1) * 48, :] = (keep[p].astype(F32) + came[p].astype(F32)).astype(BF)
    last = keep.shape[0] - 1
    pair[odd] = keep[last]
    pair[1 - odd] = came[last]


def ffn_z_kernel(keep, came, far_keep, far_send):
    side = lax.axis_index("dp") >> 2
    for out, h in ((far_keep, side), (far_send, 1 - side)):
        out[...] = (keep[h].astype(F32) + came[h].astype(F32)).astype(BF)


def sum_squares(value):
    return jnp.sum(jnp.sum(value * value, 0, keepdims=True), 1, keepdims=True)


def rows_kernel(*refs):
    pieces, out = refs[:-1], refs[-1]
    mine = lax.axis_index("dp") >> 1
    slot = out.shape[0] // (2 * len(pieces))
    for k, piece in enumerate(pieces):
        for x in range(2):
            rows = piece[x].astype(F32)
            mols = rows.shape[0] // 2
            rows = jnp.concatenate([rows[0:mols, :], rows[mols:, :]], 1)
            rows = jnp.concatenate([rows, jnp.zeros((slot - mols, rows.shape[1]), F32)], 0).astype(BF)
            out[pl.ds(pl.multiple_of(((mine ^ k) * 2 + x) * slot, 16), slot), :] = rows


def outer_kernel(keep, came, head_grad, square):
    first = (lax.axis_index("mp") & 1) == 0
    mine, other = keep[...].astype(F32), came[...].astype(F32)
    head_in = jnp.where(first, mine, other).astype(BF)
    grad_mid = jnp.where(first, other, mine).astype(BF)
    grad = dot(head_in, grad_mid, TN)
    head_grad[...] = grad
    square[...] = jnp.broadcast_to(sum_squares(grad), square.shape)


def owner_kernel(own, cols, scale, dp, *refs):
    parts, ffn_parts, (query, vectors, layer, send, scalars) = refs[: dp // 2], refs[dp // 2 : -5], refs[-5:]
    width = vectors.shape[1]
    summed = tree(parts)
    ffn = tree(ffn_parts)
    deep = ffn.shape[0]
    acc, summed = summed[0:deep, :], summed[deep:, :]
    table, keys, side = summed[0:16, :], summed[16:24, 0:128], summed[24:32, :]
    key_grad = dot(keys, query[...], TN, HIGHEST) * scale
    hat, _ = norm_parts(vectors[8:9, :])
    start_row = (hat * vectors[0:1, :] + vectors[1:2, :]).astype(BF).astype(F32)
    here = iota((deep, width), 1) == iota((deep, width), 0) + lax.axis_index("dp") * own
    start_col = jnp.sum(jnp.where(here, start_row, 0.0), -1, keepdims=True)
    square = sum_squares(table)
    grads = [start_col * side[0:1, 0:256], key_grad, acc[:, 0:256], acc[:, 192:384], ffn[:, 0:256], ffn[:, 192:384]]
    for j, grad in enumerate(grads):
        grad = grad[0:own, 0:cols]
        layer[j] = grad
        square += sum_squares(grad)
    a, b, c = three(square)
    lane = iota((16, 128), 1)
    r = iota((16, 128), 0)
    tail = jnp.where(r == 0, jnp.where(lane == 0, a, jnp.where(lane == 1, b, jnp.where(lane == 2, c, 0.0))), 0.0)
    packet = jnp.concatenate([table, tail], 1).astype(BF)
    for p in range(dp):
        send[p] = packet
    loss = side[1:2, 0:1] + side[1:2, 1:2] + side[1:2, 2:3]
    scalars[...] = jnp.where(iota(scalars.shape, 1) == 0, loss, side[1:2, 3:4])


def stats_kernel(nkept, layer, left_source, right_source, *refs):
    sources, (left, right, shaped), kept = refs[:nkept], refs[nkept : nkept + 3], refs[nkept + 3 : 2 * nkept + 3]
    left_roots, right_roots, sems = refs[2 * nkept + 3 :]
    pairs = [(left_source, left_roots), (right_source, right_roots), *zip(sources, kept)]
    copies = [pltpu.make_async_copy(a, b, sems.at[i]) for i, (a, b) in enumerate(pairs)]
    for copy in copies:
        copy.start()
    for j in range(6):
        low = layer[j].astype(BF)
        left[j] = dot(low, low, NT)
        right[j] = dot(low, low, TN)
    copies[0].wait()
    copies[1].wait()
    for j in range(6):
        near = dot(left_roots[j].astype(BF), layer[j].astype(BF))
        shaped[j] = dot(near.astype(BF), right_roots[j].astype(BF))
    for copy in copies[2:]:
        copy.wait()


def adam(weight, first, second, grad, rate):
    first_new = BETA_ONE * first + (1.0 - BETA_ONE) * grad
    second_new = BETA_TWO * second + (1.0 - BETA_TWO) * grad * grad
    fixed_one = 1.0 - BETA_ONE**STEP
    fixed_two = 1.0 - BETA_TWO**STEP
    update = first_new * (1.0 / fixed_one) / (jnp.sqrt(second_new * (1.0 / fixed_two)) + ADAM_EPS)
    return first_new, second_new, weight - rate * (update + WEIGHT_DECAY * weight)


def update_kernel(nmp, owners, cols, *refs):
    packets = refs[:nmp]
    (
        head_square, scalars, layer, left_add, right_add, shaped, weights, left, right,
        tables, tables_m, tables_v, head, head_m, head_v, head_grad, vectors, vectors_m, vectors_v,
    ) = refs[nmp : nmp + 19]
    loss_out, count_out, norm_out = refs[nmp + 19 : nmp + 22]
    outs = refs[nmp + 22 : nmp + 35]
    held = refs[nmp + 35 : nmp + 48]
    grads, sems = refs[nmp + 48 :]
    layer_out, weights_out, left_out, right_out, tm_out, tv_out, t_out, hm_out, hv_out, h_out, vm_out, vv_out, v_out = held
    started = []

    def send(i, rows=None):
        src, dst = held[i], outs[i]
        if rows is not None:
            src, dst = src.at[rows], dst.at[rows]
        copy = pltpu.make_async_copy(src, dst, sems.at[len(started)])
        copy.start()
        started.append(copy)

    parts = []
    for packet in packets:
        s = jnp.zeros((1, 1), F32)
        for p in range(packet.shape[0]):
            tail = packet[p, :, 384:512].astype(F32)
            s += tail[0:1, 0:1] + tail[0:1, 1:2] + tail[0:1, 2:3]
        parts.append(s)
    while len(parts) > 1:
        parts = [parts[i] + parts[i + 1] for i in range(0, len(parts), 2)]
    square = parts[0] + head_square[0:1, 0:1]
    loss, count = scalars[0:1, 0:1], scalars[0:1, 1:2]
    norm = jnp.sqrt(square) / count
    factor = CLIP / jnp.maximum(norm, CLIP) / count
    loss_out[...] = loss
    count_out[...] = count
    norm_out[...] = norm
    width = head.shape[0]
    parts = 8
    each = width // parts
    for i in range(parts):

        def some_rows(t, unused, i=i):
            rows = pl.ds(pl.multiple_of(i * each + t * 8, 8), 8)
            hm_out[rows, :], hv_out[rows, :], h_out[rows, :] = adam(
                head[rows, :], head_m[rows, :], head_v[rows, :], head_grad[rows, :] * factor, RATE_HEAD
            )
            return 0

        lax.fori_loop(0, each // 8, some_rows, 0, unroll=4)
        for k in (7, 8, 9):
            send(k, pl.ds(i * each, each))
    scale = (1.0 - STATS_DECAY) * factor * factor
    right_out[...] = STATS_DECAY * right[...] + scale[None] * right_add[...]
    send(3)
    left_out[...] = STATS_DECAY * left[...] + scale[None] * left_add[...]
    send(2)
    for j in range(6):
        span = slice(j * cols, (j + 1) * cols)
        layer_out[:, span] = layer[j] * factor
        weights_out[:, span] = weights[:, span] - RATE_LAYER * (shaped[j] * factor + WEIGHT_DECAY * weights[:, span])
    send(0)
    send(1)
    group = lax.axis_index("mp")
    share = FEATS // nmp
    half = 384
    for k in range(nmp):
        start = pl.multiple_of((group ^ k) * share, 8)
        for p in range(owners):
            piece = packets[k][p, :, 0:half].astype(F32)
            piece = jnp.concatenate([piece[0:8, :], piece[8:16, :]], 1) * factor
            grads[pl.ds(pl.multiple_of(start + p * 8, 8), 8), :] = piece
    rows = tables.shape[0]

    def table_rows(t, unused):
        r = pl.ds(pl.multiple_of(t * 8, 8), 8)
        tm_out[r, :], tv_out[r, :], t_out[r, :] = adam(tables[r, :], tables_m[r, :], tables_v[r, :], grads[r, :], RATE_TABLES)
        return 0

    lax.fori_loop(0, rows // 8, table_rows, 0, unroll=4)
    for k in (4, 5, 6):
        send(k)
    order = (3, 4, 5, 6, 7, 8, 0, 1, 2, 9, 10)
    r = iota((16, vectors.shape[1]), 0)
    tail = jnp.zeros(r.shape, F32)
    for i, o in enumerate(order):
        tail = jnp.where(r == i, grads[rows + o : rows + o + 1, :], tail)
    nrows = vectors.shape[0]
    vm_out[...], vv_out[...], v_out[...] = adam(vectors[...], vectors_m[...], vectors_v[...], tail[0:nrows, :], RATE_VECTORS)
    for k in (10, 11, 12):
        send(k)
    for copy in started:
        copy.wait()


def exchange(x, axis):
    n = lax.axis_size(axis)
    return [x] + [lax.ppermute(x, axis, [(i, i ^ k) for i in range(n)]) for k in range(1, n)]


def flip(x, k):
    n = lax.axis_size("dp")
    return lax.ppermute(x, "dp", [(i, i ^ k) for i in range(n)])


def after(values, *others):
    return lax.optimization_barrier((tuple(values), tuple(others)))[0]


def spread(x, second=()):
    four, one, two = after([flip(x, 4), flip(x, 1), flip(x, 2)], *second)
    return [x, one, two, flip(two, 1), four, flip(four, 1), flip(four, 2), flip(one, 6)]


def per_device(
    lap_vectors,
    eig_index,
    type_ids,
    seg_ids,
    targets,
    layer_weights,
    left_stats,
    right_stats,
    left_roots,
    right_roots,
    tables,
    tables_m,
    tables_v,
    head_weight,
    head_m,
    head_v,
    vectors,
    vectors_m,
    vectors_v,
):
    dp = lax.axis_size("dp")
    nmp = lax.axis_size("mp")
    length = seg_ids.shape[1]
    mols = targets.shape[1]
    width = vectors.shape[1]
    own, group_cols = layer_weights.shape[0], layer_weights.shape[1]
    cols = group_cols // 6
    heads = cols // HEAD_DIM
    scale = HEAD_DIM ** (-0.5)
    owners = FEATS // nmp // 8

    w = layer_weights.astype(BF)
    sources = [in_hbm(x) for x in (lap_vectors[0].T, eig_index[0].T, type_ids, seg_ids, tables, vectors)]
    at, normed, hats, invs = call(
        functools.partial(embed_kernel, mols),
        [sds((FEATS, length), BF), sds((length, width), BF), sds((length, width), BF), sds((length, 128), F32)],
        sources,
        [pltpu.VMEM(x.shape, x.dtype) for x in sources]
        + [pltpu.VMEM((FEATS, width), BF), pltpu.VMEM((FEATS, width), BF), pltpu.VMEM((8, length), I32), pltpu.SemaphoreType.DMA((6,))],
        flops=4 * length * FEATS * width,
        in_specs=[IN_PLACE] * 6,
    )
    direct = dp == 8 and own == 4 * mols and own % 16 == 0
    if direct:
        ones = spread(w, (normed,))
    else:
        ones = [lax.all_gather(w, "dp", axis=0, tiled=True)]
    np_ = len(ones)
    part, probs, values, ctx, keyed, query, w1, w2 = call(
        functools.partial(attn_kernel, np_, mols, heads, scale),
        [
            sds((mols, width), BF),
            sds((mols * heads, length), BF),
            sds((length, 256), BF),
            sds((mols, 256), BF),
            sds((width, 256), BF),
            sds((8, 256), F32),
            sds((width, 4 * cols), BF),
            sds((width, 2 * cols), BF),
        ],
        [normed, seg_ids, vectors, *ones],
        flops=4 * length * 256 * width,
    )
    part, resid_one, normed_two, hidden, act = call(
        functools.partial(ffn_kernel, nmp, cols),
        [
            sds((mols, width), BF),
            sds((mols, width), F32),
            sds((mols, width), BF),
            sds((mols, 256), F32),
            sds((mols, 256), BF),
        ],
        [*exchange(part, "mp"), vectors, w2],
        flops=4 * mols * width * 256,
    )
    part, pack, grad_two, grad_low, grad_hidden, head_rows = call(
        functools.partial(head_kernel, nmp, cols),
        [
            sds((mols, width), BF),
            sds((mols, 2 * width), BF),
            sds((mols, width), F32),
            sds((mols, width), BF),
            sds((mols, 256), BF),
            sds((8, width), F32),
        ],
        [*exchange(part, "mp"), resid_one, vectors, head_weight, targets, seg_ids, hidden, w2],
        [pltpu.VMEM((width, width), BF)],
        flops=4 * width * width * mols,
    )
    odd = lax.axis_index("dp") & 1
    high = dp // 2
    deep = (own + 15) // 16 * 16
    nlayer = 2 if own == deep else 1

    def halves(parts):
        if nlayer == 2:
            return parts
        both = parts[0].reshape(high, 2, own, -1)
        both = jnp.pad(both, ((0, 0), (0, 0), (0, deep - own), (0, 0)))
        return [lax.dynamic_index_in_dim(both, i, 1, False) for i in (odd, 1 - odd)]

    def half_shapes(lanes, number=1, more=0):
        return [sds((high * number + more, own // number, lanes), BF)] * 2 if nlayer == 2 else [sds((width, lanes), BF)]

    number = 2 if direct else 1
    *ffn_parts, comb = call(
        functools.partial(ffn_grad_kernel, nlayer, high),
        half_shapes(384, number, number - 1) + [sds((256, width), BF)],
        [normed_two, grad_hidden, grad_low, act, pack, keyed],
        [pltpu.VMEM((width, 384), BF)],
        flops=4 * mols * width * 256,
    )
    ffn_keep, ffn_send = halves(ffn_parts)
    ffn_came = flip(ffn_send, 1)
    if direct:
        near_keep, near_send, pair = call(
            ffn_x_kernel,
            [sds((2, own, 384), BF)] * 2 + [sds((2, 2 * mols, width // 2), BF)],
            [ffn_keep, ffn_came],
        )
        far_keep, far_send = call(ffn_z_kernel, [sds((own, 384), BF)] * 2, [near_keep, flip(near_send, 2)])
        ffn_parts = [far_keep, flip(far_send, 4)]
    else:
        ffn_parts = call(ffn_all_kernel, [sds((deep, 384), BF)] * high, [ffn_keep, ffn_came])
        ffn_parts = [ffn_parts[0]] + [flip(ffn_parts[k], 2 * k) for k in range(1, high)]
    *layer_halves, side, key_rows, sides, extras = call(
        functools.partial(attn_back_kernel, nmp, nlayer, high, mols, heads, scale),
        half_shapes(384)
        + [sds((8, 256), F32), sds((8, width), F32), sds((256, length), BF), sds((FEATS - TYPES - 32, width), F32)],
        [*exchange(part, "mp"), resid_one, grad_two, head_rows, vectors, probs, values, normed, w1, ctx],
        [pltpu.VMEM((width, 384), BF)],
        flops=4 * length * 256 * width,
    )
    layer_keep, layer_send = halves(layer_halves)
    layer_came = flip(layer_send, 1)
    shares = call(
        functools.partial(embed_back_kernel, nmp, mols),
        [sds((FEATS // nmp, width), BF) for _ in range(nmp)],
        [sides, comb, extras, vectors, hats, invs, at, seg_ids],
        [pltpu.VMEM((FEATS, width), F32), pltpu.VMEM((16, width), F32)],
        flops=4 * length * 256 * width,
    )
    moved = [shares[0]] + [lax.ppermute(shares[k], "mp", [(i, i ^ k) for i in range(nmp)]) for k in range(1, nmp)]
    table_keep, table_send = call(
        functools.partial(merge_table_kernel, nmp, owners, own, high),
        [sds((high, 32, 384), BF)] * 2,
        [*moved, side, key_rows],
        [pltpu.VMEM((FEATS // nmp, width), F32), pltpu.VMEM((dp, 8, 384), F32)],
    )
    merged = call(
        merge_kernel,
        [sds((deep + 32, 384), BF)] * high,
        [layer_keep, layer_came, table_keep, flip(table_send, 1)],
    )
    merged = [merged[0]] + [flip(merged[k], 2 * k) for k in range(1, high)]
    if direct:
        two, four = flip(pair, 2), flip(pair, 4)
        merged = after(merged, two, four)
    layer, send, scalars = call(
        functools.partial(owner_kernel, own, cols, scale, dp),
        [sds((6, own, cols), F32), sds((dp, 16, 512), BF), sds((8, 128), F32)],
        [*merged, *ffn_parts, query, vectors],
        flops=2 * own * 256 * 1024,
    )
    sums = lax.all_to_all(send, "dp", 0, 0, tiled=True)
    swap = [(i, i ^ 1) for i in range(nmp)]
    if direct:
        (later,) = after([four], scalars)
        (six,) = after([flip(later, 2)], sums)
        (mine,) = call(rows_kernel, [sds((dp * 32, width), BF)], [pair, two, four, six])
        other = lax.ppermute(mine, "mp", swap)
    else:
        packs = lax.all_gather(pack, "dp", axis=0)
        packs = jnp.pad(packs, ((0, 0), (0, 32 - mols), (0, 0))).reshape(dp * 32, -1)
        first = (lax.axis_index("mp") & 1) == 0
        mine = jnp.where(first, packs[:, :width], packs[:, width:])
        other = jnp.where(first, packs[:, width:], packs[:, :width])
    sums = exchange(sums, "mp")
    head_grad, head_square = call(
        outer_kernel,
        [sds((width, width), F32), sds((8, 128), F32)],
        [mine, other],
        flops=2 * dp * mols * width * width,
        vmem=16 + dp // 4,
    )
    left_roots, right_roots = jnp.swapaxes(left_roots, 0, 1), right_roots[0]
    kept = [
        layer_weights, jnp.swapaxes(left_stats, 0, 1), right_stats[0],
        tables, tables_m, tables_v, head_weight, head_m, head_v, vectors, vectors_m, vectors_v,
    ]
    left_add, right_add, shaped, *kept = call(
        functools.partial(stats_kernel, len(kept)),
        [sds((6, own, own), F32), sds((6, cols, cols), F32), sds((6, own, cols), F32)] + [pltpu.VMEM(x.shape, F32) for x in kept],
        [layer, *[in_hbm(x) for x in (left_roots, right_roots, *kept)]],
        [pltpu.VMEM(left_roots.shape, F32), pltpu.VMEM(right_roots.shape, F32), pltpu.SemaphoreType.DMA((14,))],
        flops=12 * 6 * own * cols * (2 * own + 2 * cols),
        in_specs=[IN_VMEM] + [IN_PLACE] * 14,
    )
    kept = [in_vmem(x) for x in kept]
    results = [
        sds((own, group_cols), F32),
        sds((own, group_cols), F32),
        sds((6, own, own), F32),
        sds((6, cols, cols), F32),
        *[sds(tables.shape, F32)] * 3,
        *[sds(head_weight.shape, F32)] * 3,
        *[sds(vectors.shape, F32)] * 3,
    ]
    outs = call(
        functools.partial(update_kernel, nmp, owners, cols),
        [sds((1, 1), F32)] * 3 + results,
        [
            *sums, head_square, scalars, layer, left_add, right_add, shaped, *kept[:9], head_grad, *kept[9:],
        ],
        [pltpu.VMEM(x.shape, x.dtype) for x in results] + [pltpu.VMEM((FEATS, width), F32), pltpu.SemaphoreType.DMA((34,))],
        flops=20 * width * width,
        vmem=24,
        out_specs=[IN_VMEM] * 3 + [IN_PLACE] * 13,
    )
    loss, count, norm, layer_grad, layer_new, left_new, right_new, tm, tv, tn, hm, hv, hn, vm, vv, vn = outs
    return (
        loss.reshape(()),
        count.reshape(()),
        norm.reshape(()),
        layer_grad,
        layer_new,
        jnp.swapaxes(left_new, 0, 1),
        right_new[None],
        tm,
        tv,
        tn,
        hm,
        hv,
        hn,
        vm,
        vv,
        vn,
    )


def solution(mesh):
    placed = (
        P("dp", None, None),
        P("dp", None, None),
        P("dp", None),
        P("dp", None),
        P("dp", None),
        P("dp", "mp"),
        P("dp", "mp", None),
        P("dp", "mp", None, None),
        P("dp", "mp", None),
        P("dp", "mp", None, None),
        *[P()] * 9,
    )
    return jax.shard_map(
        per_device,
        mesh=mesh,
        in_specs=placed,
        out_specs=(
            P(),
            P(),
            P(),
            P("dp", "mp"),
            P("dp", "mp"),
            P("dp", "mp", None),
            P("dp", "mp", None, None),
            *[P()] * 9,
        ),
        check_vma=False,
    )
```

```python
import functools
import math

import jax
import jax.numpy as jnp
from jax import lax
from jax.experimental import pallas as pl
from jax.experimental.pallas import tpu as pltpu
from jax.sharding import PartitionSpec as P

HEAD_DIM = 24
TYPES = 192
STEP = 10
NORM_EPS = 1e-05
CLIP = 0.25
STATS_DECAY = 0.95
RATE_LAYER = 0.15
RATE_TABLES = 0.15
RATE_HEAD = 0.01
RATE_VECTORS = 0.2
BETA_ONE = 0.9
BETA_TWO = 0.99
ADAM_EPS = 1e-08
WEIGHT_DECAY = 0.01
MASKED = -1000000000.0
GELU_C = 0.7978845608028654
GELU_A = 0.044715

BF = jnp.bfloat16
F32 = jnp.float32
I32 = jnp.int32
HIGHEST = lax.Precision.HIGHEST
NN = ((1,), (0,))
NT = ((1,), (1,))
TN = ((0,), (0,))
BLOCK = 256
FEATS = 256
MIB = 1024 * 1024


def dot(a, b, dims=NN, precision=None):
    return lax.dot_general(a, b, (dims, ((), ())), preferred_element_type=F32, precision=precision)


def iota(shape, dim):
    return lax.broadcasted_iota(I32, shape, dim)


IN_VMEM = pl.BlockSpec(memory_space=pltpu.VMEM)
IN_PLACE = pl.BlockSpec(memory_space=pltpu.HBM)


def call(kernel, outs, ins, scratch=(), flops=0, vmem=16, in_specs=None, out_specs=None):
    moved = sum(math.prod(x.shape) * x.dtype.itemsize for x in list(ins) + list(outs))
    return pl.pallas_call(
        kernel,
        out_shape=tuple(outs),
        in_specs=in_specs or [IN_VMEM] * len(ins),
        out_specs=tuple(out_specs or [IN_VMEM] * len(outs)),
        scratch_shapes=list(scratch),
        compiler_params=pltpu.CompilerParams(vmem_limit_bytes=vmem * MIB),
        cost_estimate=pl.CostEstimate(flops=flops, bytes_accessed=moved, transcendentals=0),
    )(*ins)


def in_hbm(x):
    return pltpu.with_memory_space_constraint(x, pltpu.HBM)


def in_vmem(x):
    return pltpu.with_memory_space_constraint(x, pltpu.VMEM)


def sds(shape, dtype):
    return jax.ShapeDtypeStruct(shape, dtype)


def norm_parts(values):
    center = values - jnp.mean(values, -1, keepdims=True)
    spread = jnp.mean(center * center, -1, keepdims=True)
    inverse = lax.rsqrt(spread + NORM_EPS)
    return center * inverse, inverse


def norm_back(grad, hat, inverse, gain):
    scaled = grad * gain
    mean_one = jnp.mean(scaled, -1, keepdims=True)
    mean_two = jnp.mean(scaled * hat, -1, keepdims=True)
    return inverse * (scaled - mean_one - hat * mean_two)


def gelu_pair(x):
    t = jnp.tanh(GELU_C * (x + GELU_A * x * x * x))
    value = 0.5 * x * (1.0 + t)
    slope = 0.5 * (1.0 + t) + 0.5 * x * (1.0 - t * t) * (GELU_C * (1.0 + 3.0 * GELU_A * x * x))
    return value, slope


def tree(refs):
    parts = [r[...].astype(F32) for r in refs]
    while len(parts) > 1:
        parts = [parts[i] + parts[i + 1] for i in range(0, len(parts), 2)]
    return parts[0]


def three(x):
    high = x.astype(BF).astype(F32)
    mid = (x - high).astype(BF).astype(F32)
    return high, mid, x - high - mid


def assemble(pieces, first, second, owner):
    rows = pieces[0].shape[0]
    split = first.shape[1]
    for k, piece in enumerate(pieces):
        here = pl.ds(0 if len(pieces) == 1 else pl.multiple_of((owner ^ k) * rows, 16), rows)
        first[here, :] = piece[:, 0:split]
        second[here, :] = piece[:, split:]


def spaced(t):
    return t + ((t * 9363) >> 16)


def embed_kernel(mols, *refs):
    sources, (at, normed, hats, invs), held, (high, low, prev, sems) = refs[:6], refs[6:10], refs[10:16], refs[16:]
    copies = [pltpu.make_async_copy(a, b, sems.at[i]) for i, (a, b) in enumerate(zip(sources, held))]
    for copy in copies:
        copy.start()
    normed[...] = jnp.zeros(normed.shape, BF)
    for copy in copies:
        copy.wait()
    lap, eig, kinds, seg, tables, vectors = held
    length = seg.shape[1]
    width = vectors.shape[1]
    rows = tables.shape[0]
    tab = tables[...]
    tab_high = tab.astype(BF)
    rest = jnp.where(iota(tab.shape, 0) < TYPES, tab - tab_high.astype(F32), 0.0).astype(BF)
    place = (iota((FEATS, rows), 0) == spaced(iota((FEATS, rows), 1))).astype(F32).astype(BF)
    r = iota((32, width), 0)
    extra = jnp.where(r == 7, vectors[6:7, :], jnp.where(r == 15, vectors[7:8, :], jnp.where(r == 23, vectors[8:9, :], 0.0)))
    extra_high = extra.astype(BF)
    placed = dot(place, tab_high)
    high[0:32, :] = (placed[0:32, :] + extra_high.astype(F32)).astype(BF)
    high[32:, :] = placed[32:, :].astype(BF)
    placed = dot(place, rest)
    low[0:32, :] = (placed[0:32, :] + extra - extra_high.astype(F32)).astype(BF)
    low[32:, :] = placed[32:, :].astype(BF)
    place = place[:, TYPES:]
    seg_row = seg[...]
    before = pltpu.roll(jnp.broadcast_to(seg_row, (8, length)), 1, 1)
    before = jnp.where(iota((8, length), 1) == 0, -1, before)
    prev[...] = before
    filled = jnp.sum((seg_row != mols).astype(F32)).astype(I32)
    gain = vectors[0:1, :]
    shift = vectors[1:2, :]
    window = 2 * BLOCK

    def one_block(b, unused):
        start = pl.multiple_of(b * BLOCK, BLOCK)
        here = pl.ds(start, BLOCK)
        first = pl.multiple_of(jnp.clip(start - 128, 0, length - window), 128)
        source = iota((window, BLOCK), 0) + first
        one = eig[0:1, here]
        two = eig[1:2, here]
        near = lap[:, pl.ds(first, window)].astype(BF)
        pair_one = dot(near, (source == one).astype(F32).astype(BF))
        pair_two = dot(near, (source == two).astype(F32).astype(BF))
        seg_here = seg[0:1, here]
        begins = (seg_here != mols) & (seg_here != prev[0:1, here])
        kind = jnp.where(begins, -1, spaced(kinds[0:1, here]))
        keep = jnp.where(begins, 0.0, 1.0)
        which = jnp.where(begins, 23, jnp.where(one == two, 7, 15))
        pair = (jnp.concatenate([pair_one, pair_two], 0) * keep).astype(BF)
        spot = iota((FEATS, BLOCK), 0)
        at[:, here] = (((spot == kind) | (spot == which)).astype(F32) + dot(place, pair)).astype(BF)
        picks = at[:, here]
        resid = dot(picks, high[...], TN) + dot(picks, low[...], TN)
        hat, inverse = norm_parts(resid)
        normed[here, :] = (hat * gain + shift).astype(BF)
        hats[here, :] = hat.astype(BF)
        invs[here, :] = jnp.broadcast_to(inverse, (BLOCK, 128))
        return 0

    lax.fori_loop(0, (filled + BLOCK - 1) // BLOCK, one_block, 0)


def attn_kernel(npiece, mols, heads, scale, *refs):
    normed, seg, vectors = refs[:3]
    ones = refs[3 : 3 + npiece]
    part, probs, values, ctx_out, keyed, query_out, w1, w2 = refs[3 + npiece :]
    assemble(ones, w1, w2, lax.axis_index("dp"))
    width = vectors.shape[1]
    cols = heads * HEAD_DIM
    hat, _ = norm_parts(vectors[8:9, :])
    start_row = (hat * vectors[0:1, :] + vectors[1:2, :]).astype(BF)
    q = dot(jnp.broadcast_to(start_row, (16, width)), w1[:, 0:256])
    q = q.astype(BF).astype(F32)
    q = jnp.where(iota((16, 256), 1) < cols, q, 0.0)
    r = iota((16, 256), 0)
    head_of = iota((16, 256), 1) // HEAD_DIM
    query_out[...] = jnp.where(r == head_of, q, 0.0)[0:8, :]
    shifted = pltpu.roll(q, 64, 1)[0:1, :]
    r = iota((128, 256), 0)
    lane = iota((128, 256), 1) - 64
    pick = (lane >= 0) & ((r & 7) == lane // HEAD_DIM) & (r >= 64) & (r < 80)
    q_keys = jnp.where(pick, shifted, 0.0).astype(BF)
    u = dot(w1[:, 128:384], q_keys, NT)
    u_high = u.astype(BF)
    lane = iota(u.shape, 1)
    u_both = jnp.where(lane < 72, u_high.astype(F32), u - u_high.astype(F32))
    last = w1[:, 512:640].astype(F32)
    side = jnp.where(lane < 64, last, u_both).astype(BF)
    keyed[:, 0:128] = w1[:, 384:512]
    keyed[:, 128:256] = jnp.where(lane < 64, last, jnp.where(lane < 72, u * scale, 0.0)).astype(BF)
    normed_all = normed[...]
    values[:, 0:128] = dot(normed_all, w1[:, 384:512]).astype(BF)
    second = dot(normed_all, side)
    values[:, 128:256] = jnp.where(iota(second.shape, 1) < 64, second, 0.0).astype(BF)
    turned = second.T
    scores = (turned[64:72, :] + turned[72:80, :]) * scale
    seg_row = seg[...]
    length = seg_row.shape[1]
    mine = iota((mols, 1, length), 0) == seg_row[None]
    masked = jnp.where(mine, scores[None], MASKED)
    peak = jnp.max(masked, -1, keepdims=True)
    grown = jnp.where(mine, jnp.exp(masked - peak), 0.0)
    total = jnp.sum(grown, -1, keepdims=True)
    total = jnp.where(total > 0.0, total, 1.0)
    prob = (grown / total).reshape(mols * heads, length).astype(BF)
    probs[...] = prob
    wide = dot(prob, values[...])
    r = iota(wide.shape, 0) & (heads - 1)
    wide = jnp.where(r == iota(wide.shape, 1) // HEAD_DIM, wide, 0.0)
    ctx = jnp.sum(wide.reshape(mols, heads, 256), 1)
    ctx_out[...] = ctx.astype(BF)
    turned_ctx = pltpu.roll(ctx, 64, 1).astype(BF)
    part[...] = dot(turned_ctx, w1[:, 512:768], NT).astype(BF)


def ffn_kernel(nmp, cols, *refs):
    terms = refs[:nmp]
    vectors, w2, part, resid_out, normed_out, hidden_out, act_out = refs[nmp:]
    resid = vectors[8:9, :] + tree(terms)
    resid_out[...] = resid
    hat, _ = norm_parts(resid)
    low = (hat * vectors[2:3, :] + vectors[3:4, :]).astype(BF)
    normed_out[...] = low
    hidden = dot(low, w2[:, 0:256])
    hidden = jnp.where(iota(hidden.shape, 1) < cols, hidden, 0.0)
    hidden_out[...] = hidden
    act, _ = gelu_pair(hidden)
    act_out[...] = act.astype(BF)
    turned = pltpu.roll(act, 64, 1).astype(BF)
    part[...] = dot(turned, w2[:, 128:384], NT).astype(BF)


def head_kernel(nmp, cols, *refs):
    terms = refs[:nmp]
    resid_one, vectors, head, targets, seg, hidden, w2 = refs[nmp : nmp + 7]
    part, pack, grad_out, low_out, hidden_out, rows_out, head_low = refs[nmp + 7 :]
    width = vectors.shape[1]
    mols = targets.shape[1]
    head_low[...] = head[...].astype(BF)
    resid = resid_one[...] + tree(terms)
    hat, inverse = norm_parts(resid)
    gain = vectors[4:5, :]
    low = (hat * gain + vectors[5:6, :]).astype(BF)
    mid = dot(low, head_low[...]) + vectors[9:10, :]
    act_head, slope = gelu_pair(mid)
    act_head = act_head.astype(BF).astype(F32)
    readout = vectors[10:11, :].astype(BF).astype(F32)
    predicted = jnp.sum(act_head * readout, -1, keepdims=True)
    spot = iota((mols, mols), 0) == iota((mols, mols), 1)
    goal = jnp.sum(jnp.where(spot, targets[...], 0.0), -1, keepdims=True)
    seg_row = seg[...]
    there = iota((mols, seg_row.shape[1]), 0) == seg_row
    present = jnp.max(there.astype(F32), -1, keepdims=True)
    error = predicted - goal
    root = jnp.sqrt(error * error + 1.0)
    loss = jnp.sum(present * (root - 1.0), 0, keepdims=True)
    count = jnp.sum(present, 0, keepdims=True)
    grad_pred = present * error / root
    grad_readout = jnp.sum(grad_pred * act_head, 0, keepdims=True)
    grad_mid = (grad_pred * readout * slope).astype(BF)
    grad_bias = jnp.sum(grad_mid.astype(F32), 0, keepdims=True)
    grad_rows = dot(grad_mid, head_low[...], NT)
    grad_gain = jnp.sum(grad_rows * hat, 0, keepdims=True)
    grad_shift = jnp.sum(grad_rows, 0, keepdims=True)
    grad_two = norm_back(grad_rows, hat, inverse, gain)
    grad_out[...] = grad_two
    grad_low = grad_two.astype(BF)
    grad_act = dot(grad_low, w2[:, 128:384])
    grad_act = pltpu.roll(grad_act, 192, 1)
    _, slope_hidden = gelu_pair(hidden[...])
    grad_hidden = jnp.where(iota(grad_act.shape, 1) < cols, grad_act * slope_hidden, 0.0).astype(BF)
    part[...] = dot(grad_hidden, w2[:, 0:256], NT).astype(BF)
    pack[:, 0:width] = low
    pack[:, width : 2 * width] = grad_mid
    low_out[...] = grad_low
    hidden_out[...] = grad_hidden
    r = iota((8, width), 0)
    lane = iota((8, width), 1)
    scalars = jnp.where(lane == 0, loss, jnp.where(lane == 1, count, 0.0))
    rows_out[...] = jnp.where(
        r == 0,
        grad_gain,
        jnp.where(r == 1, grad_shift, jnp.where(r == 2, grad_bias, jnp.where(r == 3, grad_readout, jnp.where(r == 4, scalars, 0.0)))),
    )


def parts_for(rows, keep, send, each, odd, high, number=1):
    for z in range(high):
        for i in range(number):
            keep[z * number + i] = rows[pl.ds(pl.multiple_of(((2 * z + odd) * number + i) * each, 16), each), :]
            send[z * number + i] = rows[pl.ds(pl.multiple_of(((2 * z + 1 - odd) * number + i) * each, 16), each), :]


def ffn_grad_kernel(nlayer, high, normed, grad_hidden, grad_low, act, pack, keyed, *refs):
    outs, (comb, rows) = refs[:nlayer], refs[nlayer:]
    comb[...] = keyed[...].astype(F32).T.astype(BF)
    up = dot(normed[...], grad_hidden[...], TN)
    turned = pltpu.roll(act[...].astype(F32), 64, 1).astype(BF)
    down = dot(grad_low[...], turned, TN)
    target = rows if nlayer == 2 else outs[0]
    target[:, 0:128] = up[:, 0:128].astype(BF)
    target[:, 128:256] = (up[:, 128:256] + down[:, 0:128]).astype(BF)
    target[:, 256:384] = down[:, 128:256].astype(BF)
    if nlayer == 2:
        half = outs[0].shape[1]
        parts_for(rows, *outs, half, lax.axis_index("dp") & 1, high, 2)
        if outs[0].shape[0] > 2 * high:
            width = pack.shape[1] // 2
            lanes = pack[...].astype(F32)
            lanes = jnp.where((lax.axis_index("mp") & 1) == 0, lanes[:, 0:width], lanes[:, width:])
            lanes = jnp.concatenate([lanes[:, 0:384], lanes[:, 384:768]], 0).astype(BF)
            outs[0][2 * high] = lanes
            outs[1][2 * high] = lanes


def attn_back_kernel(nmp, nlayer, high, mols, heads, scale, *refs):
    terms = refs[:nmp]
    resid_one, grad_two, head_rows, vectors, probs, values, normed, w1, ctx = refs[nmp : nmp + 9]
    layer_outs = refs[nmp + 9 : nmp + 9 + nlayer]
    side, key_rows, sides, extras, turned_lay = refs[nmp + 9 + nlayer :]
    group = lax.axis_index("mp")
    width = vectors.shape[1]
    length = probs.shape[1]
    cols = heads * HEAD_DIM
    grad_normed = tree(terms)
    hat, inverse = norm_parts(resid_one[...])
    grad_gain = jnp.sum(grad_normed * hat, 0, keepdims=True)
    grad_shift = jnp.sum(grad_normed, 0, keepdims=True)
    grad_one = grad_two[...] + norm_back(grad_normed, hat, inverse, vectors[2:3, :])
    low = grad_one.astype(BF)
    grad_start = jnp.sum(low.astype(F32), 0, keepdims=True)
    grad_ctx = pltpu.roll(dot(low, w1[:, 512:768]), 192, 1).astype(BF).astype(F32)
    spread_ctx = jnp.broadcast_to(grad_ctx[:, None, :], (mols, heads, 256)).reshape(mols * heads, 256)
    r = iota(spread_ctx.shape, 0) & (heads - 1)
    spread_ctx = jnp.where(r == iota(spread_ctx.shape, 1) // HEAD_DIM, spread_ctx, 0.0).astype(BF)
    grad_probs = dot(spread_ctx, values[...], NT)
    prob = probs[...].astype(F32)
    inner = jnp.sum(prob * grad_probs, -1, keepdims=True)
    grad_scores = (prob * (grad_probs - inner)).astype(BF).astype(F32)
    grad_scores = jnp.sum(grad_scores.reshape(mols, heads, length), 0)
    grad_values = dot(spread_ctx, probs[...], TN)
    sides[0:cols, :] = grad_values[0:cols, :].astype(BF)
    sides[cols:256, :] = jnp.concatenate([grad_scores, jnp.zeros((256 - cols - heads, length), F32)], 0).astype(BF)
    sums = dot(sides[...], normed[...])
    turned_ctx = pltpu.roll(ctx[...].astype(F32), 64, 1).astype(BF)
    out_grad = dot(low, turned_ctx, TN)
    r = iota(sums.shape, 0)
    value_grad = jnp.where(r < cols, sums, 0.0).T
    lay = layer_outs[0] if nlayer == 1 else turned_lay
    lay[:, 0:128] = value_grad[:, 0:128].astype(BF)
    lay[:, 128:256] = (value_grad[:, 128:256] + out_grad[:, 0:128]).astype(BF)
    lay[:, 256:384] = out_grad[:, 128:256].astype(BF)
    if nlayer == 2:
        parts_for(lay, *layer_outs, layer_outs[0].shape[1], lax.axis_index("dp") & 1, high)
    gain = vectors[0:1, :]
    grad_keys = sums[cols : cols + heads, :]
    key_rows[...] = grad_keys
    turned = dot(grad_keys.astype(BF), w1[:, 128:384])
    lane = iota(turned.shape, 1) - 64
    picked = jnp.where((lane >= 0) & (lane // HEAD_DIM == iota(turned.shape, 0)), turned, 0.0)
    grad_query = jnp.sum(pltpu.roll(picked, 192, 1), 0, keepdims=True) * scale
    r = iota(side.shape, 0)
    side[...] = jnp.where(r == 0, grad_query, jnp.where(r == 1, head_rows[4:5, 0:256], 0.0))
    grad_query = jnp.broadcast_to(grad_query.astype(BF), (16, 256))
    grad_row = dot(grad_query, w1[:, 0:256], NT)[0:1, :]
    hat_start, inverse_start = norm_parts(vectors[8:9, :])
    first = jnp.where(group == 0, 1.0, 0.0)
    row_graph = norm_back(grad_row, hat_start, inverse_start, gain) + first * grad_start
    r = iota(extras.shape, 0)
    extra = jnp.where(r == 0, grad_row * hat_start, 0.0)
    extra = jnp.where(r == 1, grad_row, extra)
    extra = jnp.where(r == 2, first * grad_gain, extra)
    extra = jnp.where(r == 3, first * grad_shift, extra)
    extra = jnp.where(r == 8, row_graph, extra)
    for i, o in enumerate((4, 5, 9, 10)):
        extra = jnp.where(r == o, first * head_rows[i : i + 1, :], extra)
    extras[...] = extra


def embed_back_kernel(nmp, mols, *refs):
    sides, comb, extras, vectors, hats, invs, at, seg = refs[:8]
    outs, (total, gains) = refs[8 : 8 + nmp], refs[8 + nmp :]
    width = vectors.shape[1]
    filled = jnp.sum((seg[...] != mols).astype(F32)).astype(I32)
    total[...] = jnp.zeros(total.shape, F32)
    gains[...] = jnp.zeros(gains.shape, F32)
    gain = vectors[0:1, :]

    def one_block(b, unused):
        here = pl.ds(pl.multiple_of(b * BLOCK, BLOCK), BLOCK)
        grad = dot(sides[:, here], comb[...], TN)
        hat_here = hats[here, :].astype(F32)
        low_grad = norm_back(grad, hat_here, invs[here, 0:1], gain).astype(BF)
        total[...] += dot(at[:, here], low_grad)
        gains[0:8, :] += jnp.sum((grad * hat_here).reshape(BLOCK // 8, 8, width), 0)
        gains[8:16, :] += jnp.sum(grad.reshape(BLOCK // 8, 8, width), 0)
        return 0

    lax.fori_loop(0, (filled + BLOCK - 1) // BLOCK, one_block, 0)
    r = iota(extras.shape, 0)
    extra = extras[...] + jnp.where(r == 0, jnp.sum(gains[0:8, :], 0, keepdims=True), 0.0)
    extra += jnp.where(r == 1, jnp.sum(gains[8:16, :], 0, keepdims=True), 0.0)
    for i in range(3):
        extra += jnp.where(r == 6 + i, total[8 * i + 7 : 8 * i + 8, :], 0.0)
    half = width // 2
    nothing = jnp.zeros((1, half), F32)
    for d in range(FEATS // 8):
        row = extra[d // 2 : d // 2 + 1, d % 2 * half : (d % 2 + 1) * half] if d < 22 else nothing
        total[8 * d + 7 : 8 * d + 8, :] = jnp.concatenate([row, nothing], 1)
    group = lax.axis_index("mp")
    each = FEATS // nmp
    for k in range(nmp):
        start = pl.multiple_of((group ^ k) * each, 16)
        outs[k][...] = total[pl.ds(start, each), :].astype(BF)


def loss_row(value, count, lanes):
    a, b, c = three(value)
    lane = iota((1, lanes), 1)
    return jnp.where(lane == 0, a, jnp.where(lane == 1, b, jnp.where(lane == 2, c, jnp.where(lane == 3, count, 0.0))))


def merge_table_kernel(nmp, owners, own, high, *refs):
    terms = refs[:nmp]
    side, key_rows, table_keep, table_send, table_sum, key_sum = refs[nmp:]
    odd = lax.axis_index("dp") & 1
    table_sum[...] = tree(terms)
    half = table_sum.shape[1] // 2
    query = jnp.concatenate([side[0:1, :], jnp.zeros((1, 128), F32)], 1)
    scal = loss_row(side[1:2, 0:1], side[1:2, 1:2], 384)
    r = iota((8, 384), 0)
    scal = jnp.where(r == 0, query, jnp.where(r == 1, scal, 0.0))
    fill = jnp.zeros((8, 384 - own), F32)
    for p in range(2 * high):
        key_sum[p] = jnp.concatenate([key_rows[:, p * own : (p + 1) * own], fill], 1)
    for z in range(high):
        for out, x in ((table_keep, odd), (table_send, 1 - odd)):
            p = 2 * z + x
            if 2 * z < owners:
                each = table_sum[pl.ds(pl.multiple_of(p * 8, 8), 8), :]
            else:
                each = jnp.zeros((8, 2 * half), F32)
            out[z] = jnp.concatenate([each[:, 0:half], each[:, half:], key_sum[p], scal], 0).astype(BF)


def merge_kernel(layer_keep, layer_came, table_keep, table_came, *outs):
    deep = layer_keep.shape[1]
    mine = lax.axis_index("dp") >> 1
    r = iota((16, 384), 0)
    for k, out in enumerate(outs):
        z = mine ^ k
        out[0:deep, :] = (layer_keep[z].astype(F32) + layer_came[z].astype(F32)).astype(BF)
        out[deep : deep + 16, :] = (table_keep[z, 0:16].astype(F32) + table_came[z, 0:16].astype(F32)).astype(BF)
        both = table_keep[z, 16:32].astype(F32) + table_came[z, 16:32].astype(F32)
        loss = both[9:10, 0:1] + both[9:10, 1:2] + both[9:10, 2:3]
        out[deep + 16 :, :] = jnp.where(r == 9, loss_row(loss, both[9:10, 3:4], 384), both).astype(BF)


def ffn_all_kernel(keep, came, *outs):
    mine = lax.axis_index("dp") >> 1
    for k, out in enumerate(outs):
        out[...] = (keep[mine ^ k].astype(F32) + came[mine ^ k].astype(F32)).astype(BF)


def ffn_x_kernel(keep, came, near_keep, near_send, pair):
    me = lax.axis_index("dp")
    odd, side = me & 1, (me >> 1) & 1
    for out, s in ((near_keep, side), (near_send, 1 - side)):
        for h in range(2):
            for i in range(2):
                p = (2 * h + s) * 2 + i
                out[h, i * 48 : (i + 1) * 48, :] = (keep[p].astype(F32) + came[p].astype(F32)).astype(BF)
    last = keep.shape[0] - 1
    pair[odd] = keep[last]
    pair[1 - odd] = came[last]


def ffn_z_kernel(keep, came, pair, far_keep, far_send):
    side = lax.axis_index("dp") >> 2
    each = far_send.shape[1]
    for i in range(2):
        rows = slice(i * each, (i + 1) * each)
        far_keep[i] = (keep[side, rows].astype(F32) + came[side, rows].astype(F32)).astype(BF)
        far_send[i] = (keep[1 - side, rows].astype(F32) + came[1 - side, rows].astype(F32)).astype(BF)
        far_send[2 + i] = pair[i]


def sum_squares(value):
    return jnp.sum(jnp.sum(value * value, 0, keepdims=True), 1, keepdims=True)


def rows_kernel(npiece, nkept, *refs):
    pieces, sources, out, kept = refs[:npiece], refs[npiece : npiece + nkept], refs[npiece + nkept], refs[npiece + nkept + 1 : -1]
    sems = refs[-1]
    copies = [pltpu.make_async_copy(a, b, sems.at[i]) for i, (a, b) in enumerate(zip(sources, kept))]
    for copy in copies:
        copy.start()
    mine = lax.axis_index("dp") >> 1
    if npiece == 1:
        out[...] = pieces[0][...]
    for k in range(4 if npiece == 2 else 0):
        for x in range(2):
            rows = pieces[k & 1][(k & 2) + x].astype(F32)
            mols = rows.shape[0] // 2
            rows = jnp.concatenate([rows[0:mols, :], rows[mols:, :]], 1)
            slot = out.shape[0] // 8
            rows = jnp.concatenate([rows, jnp.zeros((slot - mols, rows.shape[1]), F32)], 0).astype(BF)
            out[pl.ds(pl.multiple_of(((mine ^ k) * 2 + x) * slot, 16), slot), :] = rows
    for copy in copies:
        copy.wait()


def outer_kernel(keep, came, head_grad, square):
    first = (lax.axis_index("mp") & 1) == 0
    mine, other = keep[...].astype(F32), came[...].astype(F32)
    head_in = jnp.where(first, mine, other).astype(BF)
    grad_mid = jnp.where(first, other, mine).astype(BF)
    grad = dot(head_in, grad_mid, TN)
    head_grad[...] = grad
    square[...] = jnp.broadcast_to(sum_squares(grad), square.shape)


def owner_kernel(own, cols, scale, dp, *refs):
    parts, ffn_parts, (query, vectors, layer, send, scalars, quad) = refs[: dp // 2], refs[dp // 2 : -6], refs[-6:]
    width = vectors.shape[1]
    summed = tree(parts)
    if len(ffn_parts) == 3:
        near, far, pair = ffn_parts
        ffn = jnp.concatenate([near[i].astype(F32) + far[i].astype(F32) for i in range(2)], 0)
        for i in range(2):
            quad[i] = pair[i]
            quad[2 + i] = far[2 + i]
    else:
        ffn = tree(ffn_parts)
        quad[...] = jnp.zeros(quad.shape, BF)
    deep = ffn.shape[0]
    acc, summed = summed[0:deep, :], summed[deep:, :]
    table, keys, side = summed[0:16, :], summed[16:24, 0:128], summed[24:32, :]
    key_grad = dot(keys, query[...], TN, HIGHEST) * scale
    hat, _ = norm_parts(vectors[8:9, :])
    start_row = (hat * vectors[0:1, :] + vectors[1:2, :]).astype(BF).astype(F32)
    here = iota((deep, width), 1) == iota((deep, width), 0) + lax.axis_index("dp") * own
    start_col = jnp.sum(jnp.where(here, start_row, 0.0), -1, keepdims=True)
    square = sum_squares(table)
    grads = [start_col * side[0:1, 0:256], key_grad, acc[:, 0:256], acc[:, 192:384], ffn[:, 0:256], ffn[:, 192:384]]
    for j, grad in enumerate(grads):
        grad = grad[0:own, 0:cols]
        layer[j] = grad
        square += sum_squares(grad)
    a, b, c = three(square)
    lane = iota((16, 384), 1)
    tail = jnp.where(lane == 0, a, jnp.where(lane == 1, b, jnp.where(lane == 2, c, 0.0)))
    packet = jnp.where(iota((16, 384), 0) == 15, tail, table).astype(BF)
    for p in range(send.shape[0]):
        send[p] = packet
    loss = side[1:2, 0:1] + side[1:2, 1:2] + side[1:2, 2:3]
    scalars[...] = jnp.where(iota(scalars.shape, 1) == 0, loss, side[1:2, 3:4])


def adam(weight, first, second, grad, rate):
    first_new = BETA_ONE * first + (1.0 - BETA_ONE) * grad
    second_new = BETA_TWO * second + (1.0 - BETA_TWO) * grad * grad
    fixed_one = 1.0 - BETA_ONE**STEP
    fixed_two = 1.0 - BETA_TWO**STEP
    update = first_new * (1.0 / fixed_one) / (jnp.sqrt(second_new * (1.0 / fixed_two)) + ADAM_EPS)
    return first_new, second_new, weight - rate * (update + WEIGHT_DECAY * weight)


def update_kernel(nmp, cols, *refs):
    arrived, refs = refs[:nmp], refs[nmp:]
    (
        head_square, scalars, layer, left_roots, right_roots, weights, left, right,
        tables, tables_m, tables_v, head, head_m, head_v, head_grad, vectors, vectors_m, vectors_v,
    ) = refs[:18]
    loss_out, count_out, norm_out = refs[18:21]
    outs = refs[21:34]
    held = refs[34:47]
    grads, vector_grads, packets, sems = refs[47:]
    layer_out, weights_out, left_out, right_out, tm_out, tv_out, t_out, hm_out, hv_out, h_out, vm_out, vv_out, v_out = held
    started = []

    def send(i, rows=None):
        src, dst = held[i], outs[i]
        if rows is not None:
            src, dst = src.at[rows], dst.at[rows]
        copy = pltpu.make_async_copy(src, dst, sems.at[len(started)])
        copy.start()
        started.append(copy)

    group = lax.axis_index("mp")
    for k in range(nmp):
        packets[group ^ k] = arrived[k][...]
    tails = jnp.zeros((16, 128), F32)
    for m in range(nmp):
        for p in range(packets.shape[1]):
            tails += packets[m, p, :, 0:128].astype(F32)
    square = head_square[0:1, 0:1] + tails[15:16, 0:1] + tails[15:16, 1:2] + tails[15:16, 2:3]
    loss, count = scalars[0:1, 0:1], scalars[0:1, 1:2]
    norm = jnp.sqrt(square) / count
    factor = CLIP / jnp.maximum(norm, CLIP) / count
    loss_out[...] = loss
    count_out[...] = count
    norm_out[...] = norm
    width = head.shape[0]
    parts = 8
    each = width // parts
    for i in range(parts):

        def some_rows(t, unused, i=i):
            rows = pl.ds(pl.multiple_of(i * each + t * 8, 8), 8)
            hm_out[rows, :], hv_out[rows, :], h_out[rows, :] = adam(
                head[rows, :], head_m[rows, :], head_v[rows, :], head_grad[rows, :] * factor, RATE_HEAD
            )
            return 0

        lax.fori_loop(0, each // 8, some_rows, 0, unroll=4)
        for k in (7, 8, 9):
            send(k, pl.ds(i * each, each))
    scale = (1.0 - STATS_DECAY) * factor * factor
    for j in range(6):
        low = layer[j].astype(BF)
        right_out[j] = STATS_DECAY * right[j] + scale * dot(low, low, TN)
        left_out[j] = STATS_DECAY * left[j] + scale * dot(low, low, NT)
    send(3)
    send(2)
    for j in range(6):
        span = slice(j * cols, (j + 1) * cols)
        low = layer[j].astype(BF)
        shaped = dot(dot(left_roots[j].astype(BF), low).astype(BF), right_roots[j].astype(BF))
        layer_out[:, span] = layer[j] * factor
        weights_out[:, span] = weights[:, span] - RATE_LAYER * (shaped * factor + WEIGHT_DECAY * weights[:, span])
    send(0)
    send(1)
    half = grads.shape[1] // 2
    high = FEATS // 8 // nmp
    for m in range(nmp):
        for p in range(high):
            piece = packets[m, p].astype(F32) * factor
            d = m * high + p
            grads[7 * d : 7 * d + 7, :] = jnp.concatenate([piece[0:7, :], piece[8:15, :]], 1)
            if d < 22:
                vector_grads[d // 2 : d // 2 + 1, d % 2 * half : (d % 2 + 1) * half] = piece[7:8, :]
    rows = tables.shape[0]

    def table_rows(t, unused):
        r = pl.ds(pl.multiple_of(t * 8, 8), 8)
        tm_out[r, :], tv_out[r, :], t_out[r, :] = adam(tables[r, :], tables_m[r, :], tables_v[r, :], grads[r, :], RATE_TABLES)
        return 0

    lax.fori_loop(0, rows // 8, table_rows, 0, unroll=4)
    for k in (4, 5, 6):
        send(k)
    nrows = vectors.shape[0]
    vm_out[...], vv_out[...], v_out[...] = adam(vectors[...], vectors_m[...], vectors_v[...], vector_grads[0:nrows, :], RATE_VECTORS)
    for k in (10, 11, 12):
        send(k)
    for copy in started:
        copy.wait()


def exchange(x, axis):
    n = lax.axis_size(axis)
    return [x] + [lax.ppermute(x, axis, [(i, i ^ k) for i in range(n)]) for k in range(1, n)]


def flip(x, k):
    n = lax.axis_size("dp")
    return lax.ppermute(x, "dp", [(i, i ^ k) for i in range(n)])


def after(values, *others):
    return lax.optimization_barrier((tuple(values), tuple(others)))[0]


def spread(x, second=()):
    four, one, two = after([flip(x, 4), flip(x, 1), flip(x, 2)], *second)
    return [x, one, two, flip(two, 1), four, flip(four, 1), flip(four, 2), flip(one, 6)]


def per_device(
    lap_vectors,
    eig_index,
    type_ids,
    seg_ids,
    targets,
    layer_weights,
    left_stats,
    right_stats,
    left_roots,
    right_roots,
    tables,
    tables_m,
    tables_v,
    head_weight,
    head_m,
    head_v,
    vectors,
    vectors_m,
    vectors_v,
):
    dp = lax.axis_size("dp")
    nmp = lax.axis_size("mp")
    length = seg_ids.shape[1]
    mols = targets.shape[1]
    width = vectors.shape[1]
    own, group_cols = layer_weights.shape[0], layer_weights.shape[1]
    cols = group_cols // 6
    heads = cols // HEAD_DIM
    scale = HEAD_DIM ** (-0.5)
    owners = FEATS // nmp // 8

    w = layer_weights.astype(BF)
    sources = [in_hbm(x) for x in (lap_vectors[0].T, eig_index[0].T, type_ids, seg_ids, tables, vectors)]
    at, normed, hats, invs = call(
        functools.partial(embed_kernel, mols),
        [sds((FEATS, length), BF), sds((length, width), BF), sds((length, width), BF), sds((length, 128), F32)],
        sources,
        [pltpu.VMEM(x.shape, x.dtype) for x in sources]
        + [pltpu.VMEM((FEATS, width), BF), pltpu.VMEM((FEATS, width), BF), pltpu.VMEM((8, length), I32), pltpu.SemaphoreType.DMA((6,))],
        flops=4 * length * FEATS * width,
        in_specs=[IN_PLACE] * 6,
    )
    direct = dp == 8 and own == 4 * mols and own % 16 == 0
    if direct:
        ones = spread(w, (normed,))
    else:
        ones = [lax.all_gather(w, "dp", axis=0, tiled=True)]
    np_ = len(ones)
    part, probs, values, ctx, keyed, query, w1, w2 = call(
        functools.partial(attn_kernel, np_, mols, heads, scale),
        [
            sds((mols, width), BF),
            sds((mols * heads, length), BF),
            sds((length, 256), BF),
            sds((mols, 256), BF),
            sds((width, 256), BF),
            sds((8, 256), F32),
            sds((width, 4 * cols), BF),
            sds((width, 2 * cols), BF),
        ],
        [normed, seg_ids, vectors, *ones],
        flops=4 * length * 256 * width,
    )
    part, resid_one, normed_two, hidden, act = call(
        functools.partial(ffn_kernel, nmp, cols),
        [
            sds((mols, width), BF),
            sds((mols, width), F32),
            sds((mols, width), BF),
            sds((mols, 256), F32),
            sds((mols, 256), BF),
        ],
        [*exchange(part, "mp"), vectors, w2],
        flops=4 * mols * width * 256,
    )
    part, pack, grad_two, grad_low, grad_hidden, head_rows = call(
        functools.partial(head_kernel, nmp, cols),
        [
            sds((mols, width), BF),
            sds((mols, 2 * width), BF),
            sds((mols, width), F32),
            sds((mols, width), BF),
            sds((mols, 256), BF),
            sds((8, width), F32),
        ],
        [*exchange(part, "mp"), resid_one, vectors, head_weight, targets, seg_ids, hidden, w2],
        [pltpu.VMEM((width, width), BF)],
        flops=4 * width * width * mols,
    )
    odd = lax.axis_index("dp") & 1
    high = dp // 2
    deep = (own + 15) // 16 * 16
    nlayer = 2 if own == deep else 1

    def halves(parts):
        if nlayer == 2:
            return parts
        both = parts[0].reshape(high, 2, own, -1)
        both = jnp.pad(both, ((0, 0), (0, 0), (0, deep - own), (0, 0)))
        return [lax.dynamic_index_in_dim(both, i, 1, False) for i in (odd, 1 - odd)]

    def half_shapes(lanes, number=1, more=0):
        return [sds((high * number + more, own // number, lanes), BF)] * 2 if nlayer == 2 else [sds((width, lanes), BF)]

    number = 2 if direct else 1
    parts = exchange(part, "mp")
    *ffn_parts, comb = call(
        functools.partial(ffn_grad_kernel, nlayer, high),
        half_shapes(384, number, number - 1) + [sds((256, width), BF)],
        [normed_two, grad_hidden, grad_low, act, pack, keyed],
        [pltpu.VMEM((width, 384), BF)],
        flops=4 * mols * width * 256,
    )
    ffn_keep, ffn_send = halves(ffn_parts)
    ffn_came = flip(ffn_send, 1)
    *layer_halves, side, key_rows, sides, extras = call(
        functools.partial(attn_back_kernel, nmp, nlayer, high, mols, heads, scale),
        half_shapes(384)
        + [sds((8, 256), F32), sds((8, width), F32), sds((256, length), BF), sds((16, width), F32)],
        [*parts, resid_one, grad_two, head_rows, vectors, probs, values, normed, w1, ctx],
        [pltpu.VMEM((width, 384), BF)],
        flops=4 * length * 256 * width,
    )
    layer_keep, layer_send = halves(layer_halves)
    layer_came = flip(layer_send, 1)
    shares = call(
        functools.partial(embed_back_kernel, nmp, mols),
        [sds((FEATS // nmp, width), BF) for _ in range(nmp)],
        [sides, comb, extras, vectors, hats, invs, at, seg_ids],
        [pltpu.VMEM((FEATS, width), F32), pltpu.VMEM((16, width), F32)],
        flops=4 * length * 256 * width,
    )
    moved = [shares[0]] + [lax.ppermute(shares[k], "mp", [(i, i ^ k) for i in range(nmp)]) for k in range(1, nmp)]
    table_keep, table_send = call(
        functools.partial(merge_table_kernel, nmp, owners, own, high),
        [sds((high, 32, 384), BF)] * 2,
        [*moved, side, key_rows],
        [pltpu.VMEM((FEATS // nmp, width), F32), pltpu.VMEM((dp, 8, 384), F32)],
    )
    (ffn_came,) = after([ffn_came], shares[0])
    if direct:
        near_keep, near_send, pair = call(
            ffn_x_kernel,
            [sds((2, own, 384), BF)] * 2 + [sds((2, 2 * mols, width // 2), BF)],
            [ffn_keep, ffn_came],
        )
        far_keep, far_send = call(
            ffn_z_kernel,
            [sds((2, own // 2, 384), BF), sds((4, own // 2, 384), BF)],
            [near_keep, flip(near_send, 2), pair],
        )
        ffn_parts = [far_keep, flip(far_send, 4), pair]
    else:
        ffn_parts = call(ffn_all_kernel, [sds((deep, 384), BF)] * high, [ffn_keep, ffn_came])
        ffn_parts = [ffn_parts[0]] + [flip(ffn_parts[k], 2 * k) for k in range(1, high)]
    merged = call(
        merge_kernel,
        [sds((deep + 32, 384), BF)] * high,
        [layer_keep, layer_came, table_keep, flip(table_send, 1)],
    )
    merged = [merged[0]] + [flip(merged[k], 2 * k) for k in range(1, high)]
    layer, send, scalars, quad = call(
        functools.partial(owner_kernel, own, cols, scale, dp),
        [sds((6, own, cols), F32), sds((dp, 16, 384), BF), sds((8, 128), F32), sds((4, 2 * mols, 384), BF)],
        [*merged, *ffn_parts, query, vectors],
        flops=2 * own * 256 * 1024,
    )
    swap = [(i, i ^ 1) for i in range(nmp)]
    kept = [
        jnp.swapaxes(left_roots, 0, 1), right_roots[0], layer_weights, jnp.swapaxes(left_stats, 0, 1), right_stats[0],
        tables, tables_m, tables_v, head_weight, head_m, head_v, vectors, vectors_m, vectors_v,
    ]
    sums = lax.all_to_all(send, "dp", 0, 0, tiled=True)
    if direct:
        (came,) = after([flip(quad, 2)], sums)
        pieces = [quad, came]
    else:
        packs = lax.all_gather(pack, "dp", axis=0)
        packs = jnp.pad(packs, ((0, 0), (0, 32 - mols), (0, 0))).reshape(dp * 32, -1)
        first = (lax.axis_index("mp") & 1) == 0
        pieces = [jnp.where(first, packs[:, :width], packs[:, width:])]
    (mine,) = call(
        functools.partial(rows_kernel, len(pieces), 0),
        [sds((dp * 32, width), BF)],
        [*pieces],
        [pltpu.SemaphoreType.DMA((1,))],
        vmem=8,
    )
    sums = exchange(sums, "mp")
    token, *kept = call(
        functools.partial(rows_kernel, 1, len(kept)),
        [sds(scalars.shape, F32)] + [pltpu.VMEM(x.shape, F32) for x in kept],
        [scalars, *[in_hbm(x) for x in kept]],
        [pltpu.SemaphoreType.DMA((len(kept),))],
        in_specs=[IN_VMEM] + [IN_PLACE] * len(kept),
        vmem=2,
    )
    other = lax.ppermute(mine, "mp", swap)
    head_grad, head_square = call(
        outer_kernel,
        [sds((width, width), F32), sds((8, 128), F32)],
        [mine, other],
        flops=2 * dp * mols * width * width,
        vmem=16 + dp // 4,
    )
    kept = [in_vmem(x) for x in kept]
    results = [
        sds((own, group_cols), F32),
        sds((own, group_cols), F32),
        sds((6, own, own), F32),
        sds((6, cols, cols), F32),
        *[sds(tables.shape, F32)] * 3,
        *[sds(head_weight.shape, F32)] * 3,
        *[sds(vectors.shape, F32)] * 3,
    ]
    outs = call(
        functools.partial(update_kernel, nmp, cols),
        [sds((1, 1), F32)] * 3 + results,
        [
            *sums, head_square, token, layer, *kept[:11], head_grad, *kept[11:],
        ],
        [pltpu.VMEM(x.shape, x.dtype) for x in results] + [pltpu.VMEM((FEATS, width), F32), pltpu.VMEM((16, width), F32), pltpu.VMEM((nmp, dp, 16, 384), BF), pltpu.SemaphoreType.DMA((34,))],
        flops=20 * width * width,
        vmem=24,
        out_specs=[IN_VMEM] * 3 + [IN_PLACE] * 13,
    )
    loss, count, norm, layer_grad, layer_new, left_new, right_new, tm, tv, tn, hm, hv, hn, vm, vv, vn = outs
    return (
        loss.reshape(()),
        count.reshape(()),
        norm.reshape(()),
        layer_grad,
        layer_new,
        jnp.swapaxes(left_new, 0, 1),
        right_new[None],
        tm,
        tv,
        tn,
        hm,
        hv,
        hn,
        vm,
        vv,
        vn,
    )


def solution(mesh):
    placed = (
        P("dp", None, None),
        P("dp", None, None),
        P("dp", None),
        P("dp", None),
        P("dp", None),
        P("dp", "mp"),
        P("dp", "mp", None),
        P("dp", "mp", None, None),
        P("dp", "mp", None),
        P("dp", "mp", None, None),
        *[P()] * 9,
    )
    return jax.shard_map(
        per_device,
        mesh=mesh,
        in_specs=placed,
        out_specs=(
            P(),
            P(),
            P(),
            P("dp", "mp"),
            P("dp", "mp"),
            P("dp", "mp", None),
            P("dp", "mp", None, None),
            *[P()] * 9,
        ),
        check_vma=False,
    )
```

```python
import functools
import math

import jax
import jax.numpy as jnp
from jax import lax
from jax.experimental import pallas as pl
from jax.experimental.pallas import tpu as pltpu
from jax.sharding import PartitionSpec as P

HEAD_DIM = 24
TYPES = 192
STEP = 10
NORM_EPS = 1e-05
CLIP = 0.25
STATS_DECAY = 0.95
RATE_LAYER = 0.15
RATE_TABLES = 0.15
RATE_HEAD = 0.01
RATE_VECTORS = 0.2
BETA_ONE = 0.9
BETA_TWO = 0.99
ADAM_EPS = 1e-08
WEIGHT_DECAY = 0.01
MASKED = -1000000000.0
GELU_C = 0.7978845608028654
GELU_A = 0.044715

BF = jnp.bfloat16
F32 = jnp.float32
I32 = jnp.int32
HIGHEST = lax.Precision.HIGHEST
NN = ((1,), (0,))
NT = ((1,), (1,))
TN = ((0,), (0,))
BLOCK = 256
FEATS = 256
MIB = 1024 * 1024


def dot(a, b, dims=NN, precision=None):
    return lax.dot_general(a, b, (dims, ((), ())), preferred_element_type=F32, precision=precision)


def iota(shape, dim):
    return lax.broadcasted_iota(I32, shape, dim)


IN_VMEM = pl.BlockSpec(memory_space=pltpu.VMEM)
IN_PLACE = pl.BlockSpec(memory_space=pltpu.HBM)


def call(kernel, outs, ins, scratch=(), flops=0, vmem=16, in_specs=None, out_specs=None):
    moved = sum(math.prod(x.shape) * x.dtype.itemsize for x in list(ins) + list(outs))
    return pl.pallas_call(
        kernel,
        out_shape=tuple(outs),
        in_specs=in_specs or [IN_VMEM] * len(ins),
        out_specs=tuple(out_specs or [IN_VMEM] * len(outs)),
        scratch_shapes=list(scratch),
        compiler_params=pltpu.CompilerParams(vmem_limit_bytes=vmem * MIB),
        cost_estimate=pl.CostEstimate(flops=flops, bytes_accessed=moved, transcendentals=0),
    )(*ins)


def in_hbm(x):
    return pltpu.with_memory_space_constraint(x, pltpu.HBM)


def in_vmem(x):
    return pltpu.with_memory_space_constraint(x, pltpu.VMEM)


def sds(shape, dtype):
    return jax.ShapeDtypeStruct(shape, dtype)


def norm_parts(values):
    center = values - jnp.mean(values, -1, keepdims=True)
    spread = jnp.mean(center * center, -1, keepdims=True)
    inverse = lax.rsqrt(spread + NORM_EPS)
    return center * inverse, inverse


def norm_back(grad, hat, inverse, gain):
    scaled = grad * gain
    mean_one = jnp.mean(scaled, -1, keepdims=True)
    mean_two = jnp.mean(scaled * hat, -1, keepdims=True)
    return inverse * (scaled - mean_one - hat * mean_two)


def gelu_pair(x):
    t = jnp.tanh(GELU_C * (x + GELU_A * x * x * x))
    value = 0.5 * x * (1.0 + t)
    slope = 0.5 * (1.0 + t) + 0.5 * x * (1.0 - t * t) * (GELU_C * (1.0 + 3.0 * GELU_A * x * x))
    return value, slope


def tree(refs):
    parts = [r[...].astype(F32) for r in refs]
    while len(parts) > 1:
        parts = [parts[i] + parts[i + 1] for i in range(0, len(parts), 2)]
    return parts[0]


def three(x):
    high = x.astype(BF).astype(F32)
    mid = (x - high).astype(BF).astype(F32)
    return high, mid, x - high - mid


def assemble(pieces, first, second, owner):
    rows = pieces[0].shape[0]
    split = first.shape[1]
    for k, piece in enumerate(pieces):
        here = pl.ds(0 if len(pieces) == 1 else pl.multiple_of((owner ^ k) * rows, 16), rows)
        first[here, :] = piece[:, 0:split]
        second[here, :] = piece[:, split:]


def spaced(t):
    return t + ((t * 9363) >> 16)


def embed_kernel(mols, *refs):
    sources, (at, normed, hats, invs), held, (high, low, prev, sems) = refs[:6], refs[6:10], refs[10:16], refs[16:]
    copies = [pltpu.make_async_copy(a, b, sems.at[i]) for i, (a, b) in enumerate(zip(sources, held))]
    for copy in copies:
        copy.start()
    normed[...] = jnp.zeros(normed.shape, BF)
    for copy in copies:
        copy.wait()
    lap, eig, kinds, seg, tables, vectors = held
    length = seg.shape[1]
    width = vectors.shape[1]
    rows = tables.shape[0]
    tab = tables[...]
    tab_high = tab.astype(BF)
    rest = jnp.where(iota(tab.shape, 0) < TYPES, tab - tab_high.astype(F32), 0.0).astype(BF)
    place = (iota((FEATS, rows), 0) == spaced(iota((FEATS, rows), 1))).astype(F32).astype(BF)
    r = iota((32, width), 0)
    extra = jnp.where(r == 7, vectors[6:7, :], jnp.where(r == 15, vectors[7:8, :], jnp.where(r == 23, vectors[8:9, :], 0.0)))
    extra_high = extra.astype(BF)
    placed = dot(place, tab_high)
    high[0:32, :] = (placed[0:32, :] + extra_high.astype(F32)).astype(BF)
    high[32:, :] = placed[32:, :].astype(BF)
    placed = dot(place, rest)
    low[0:32, :] = (placed[0:32, :] + extra - extra_high.astype(F32)).astype(BF)
    low[32:, :] = placed[32:, :].astype(BF)
    place = place[:, TYPES:]
    seg_row = seg[...]
    before = pltpu.roll(jnp.broadcast_to(seg_row, (8, length)), 1, 1)
    before = jnp.where(iota((8, length), 1) == 0, -1, before)
    prev[...] = before
    filled = jnp.sum((seg_row != mols).astype(F32)).astype(I32)
    gain = vectors[0:1, :]
    shift = vectors[1:2, :]
    window = 2 * BLOCK

    def one_block(b, unused):
        start = pl.multiple_of(b * BLOCK, BLOCK)
        here = pl.ds(start, BLOCK)
        first = pl.multiple_of(jnp.clip(start - 128, 0, length - window), 128)
        source = iota((window, BLOCK), 0) + first
        one = eig[0:1, here]
        two = eig[1:2, here]
        near = lap[:, pl.ds(first, window)].astype(BF)
        pair_one = dot(near, (source == one).astype(F32).astype(BF))
        pair_two = dot(near, (source == two).astype(F32).astype(BF))
        seg_here = seg[0:1, here]
        begins = (seg_here != mols) & (seg_here != prev[0:1, here])
        kind = jnp.where(begins, -1, spaced(kinds[0:1, here]))
        keep = jnp.where(begins, 0.0, 1.0)
        which = jnp.where(begins, 23, jnp.where(one == two, 7, 15))
        pair = (jnp.concatenate([pair_one, pair_two], 0) * keep).astype(BF)
        spot = iota((FEATS, BLOCK), 0)
        at[:, here] = (((spot == kind) | (spot == which)).astype(F32) + dot(place, pair)).astype(BF)
        picks = at[:, here]
        resid = dot(picks, high[...], TN) + dot(picks, low[...], TN)
        hat, inverse = norm_parts(resid)
        normed[here, :] = (hat * gain + shift).astype(BF)
        hats[here, :] = hat.astype(BF)
        invs[here, :] = jnp.broadcast_to(inverse, (BLOCK, 128))
        return 0

    lax.fori_loop(0, (filled + BLOCK - 1) // BLOCK, one_block, 0)


def attn_kernel(npiece, mols, heads, scale, *refs):
    normed, seg, vectors = refs[:3]
    ones = refs[3 : 3 + npiece]
    part, probs, values, ctx_out, keyed, query_out, w1, w2 = refs[3 + npiece :]
    assemble(ones, w1, w2, lax.axis_index("dp"))
    width = vectors.shape[1]
    cols = heads * HEAD_DIM
    hat, _ = norm_parts(vectors[8:9, :])
    start_row = (hat * vectors[0:1, :] + vectors[1:2, :]).astype(BF)
    q = dot(jnp.broadcast_to(start_row, (16, width)), w1[:, 0:256])
    q = q.astype(BF).astype(F32)
    q = jnp.where(iota((16, 256), 1) < cols, q, 0.0)
    r = iota((16, 256), 0)
    head_of = iota((16, 256), 1) // HEAD_DIM
    query_out[...] = jnp.where(r == head_of, q, 0.0)[0:8, :]
    shifted = pltpu.roll(q, 64, 1)[0:1, :]
    r = iota((128, 256), 0)
    lane = iota((128, 256), 1) - 64
    pick = (lane >= 0) & ((r & 7) == lane // HEAD_DIM) & (r >= 64) & (r < 80)
    q_keys = jnp.where(pick, shifted, 0.0).astype(BF)
    u = dot(w1[:, 128:384], q_keys, NT)
    u_high = u.astype(BF)
    lane = iota(u.shape, 1)
    u_both = jnp.where(lane < 72, u_high.astype(F32), u - u_high.astype(F32))
    last = w1[:, 512:640].astype(F32)
    side = jnp.where(lane < 64, last, u_both).astype(BF)
    keyed[:, 0:128] = w1[:, 384:512]
    keyed[:, 128:256] = jnp.where(lane < 64, last, jnp.where(lane < 72, u * scale, 0.0)).astype(BF)
    normed_all = normed[...]
    values[:, 0:128] = dot(normed_all, w1[:, 384:512]).astype(BF)
    second = dot(normed_all, side)
    values[:, 128:256] = jnp.where(iota(second.shape, 1) < 64, second, 0.0).astype(BF)
    turned = second.T
    scores = (turned[64:72, :] + turned[72:80, :]) * scale
    seg_row = seg[...]
    length = seg_row.shape[1]
    mine = iota((mols, 1, length), 0) == seg_row[None]
    masked = jnp.where(mine, scores[None], MASKED)
    peak = jnp.max(masked, -1, keepdims=True)
    grown = jnp.exp(masked - peak)
    total = jnp.sum(grown, -1, keepdims=True)
    prob = (grown * (1.0 / total)).reshape(mols * heads, length).astype(BF)
    probs[...] = prob
    wide = dot(prob, values[...])
    r = iota(wide.shape, 0) & (heads - 1)
    wide = jnp.where(r == iota(wide.shape, 1) // HEAD_DIM, wide, 0.0)
    ctx = jnp.sum(wide.reshape(mols, heads, 256), 1)
    ctx_out[...] = ctx.astype(BF)
    turned_ctx = pltpu.roll(ctx, 64, 1).astype(BF)
    part[...] = dot(turned_ctx, w1[:, 512:768], NT).astype(BF)


def ffn_kernel(nmp, cols, *refs):
    terms = refs[:nmp]
    vectors, w2, part, resid_out, normed_out, hidden_out, act_out = refs[nmp:]
    resid = vectors[8:9, :] + tree(terms)
    resid_out[...] = resid
    hat, _ = norm_parts(resid)
    low = (hat * vectors[2:3, :] + vectors[3:4, :]).astype(BF)
    normed_out[...] = low
    hidden = dot(low, w2[:, 0:256])
    hidden = jnp.where(iota(hidden.shape, 1) < cols, hidden, 0.0)
    hidden_out[...] = hidden
    act, _ = gelu_pair(hidden)
    act_out[...] = act.astype(BF)
    turned = pltpu.roll(act, 64, 1).astype(BF)
    part[...] = dot(turned, w2[:, 128:384], NT).astype(BF)


def head_kernel(nmp, cols, *refs):
    terms = refs[:nmp]
    resid_one, vectors, head, targets, seg, hidden, w2 = refs[nmp : nmp + 7]
    part, pack, pred_out, grad_out, low_out, hidden_out, rows_out, head_low = refs[nmp + 7 :]
    width = vectors.shape[1]
    mols = targets.shape[1]
    head_low[...] = head[...].astype(BF)
    resid = resid_one[...] + tree(terms)
    hat, inverse = norm_parts(resid)
    gain = vectors[4:5, :]
    low = (hat * gain + vectors[5:6, :]).astype(BF)
    mid = dot(low, head_low[...]) + vectors[9:10, :]
    act_head, slope = gelu_pair(mid)
    act_head = act_head.astype(BF).astype(F32)
    readout = vectors[10:11, :].astype(BF).astype(F32)
    predicted = jnp.sum(act_head * readout, -1, keepdims=True)
    spot = iota((mols, mols), 0) == iota((mols, mols), 1)
    goal = jnp.sum(jnp.where(spot, targets[...], 0.0), -1, keepdims=True)
    seg_row = seg[...]
    there = iota((mols, seg_row.shape[1]), 0) == seg_row
    present = jnp.max(there.astype(F32), -1, keepdims=True)
    error = predicted - goal
    root = jnp.sqrt(error * error + 1.0)
    loss = jnp.sum(present * (root - 1.0), 0, keepdims=True)
    count = jnp.sum(present, 0, keepdims=True)
    grad_pred = present * error / root
    grad_readout = jnp.sum(grad_pred * act_head, 0, keepdims=True)
    grad_mid = (grad_pred * readout * slope).astype(BF)
    grad_bias = jnp.sum(grad_mid.astype(F32), 0, keepdims=True)
    grad_rows = dot(grad_mid, head_low[...], NT)
    grad_gain = jnp.sum(grad_rows * hat, 0, keepdims=True)
    grad_shift = jnp.sum(grad_rows, 0, keepdims=True)
    grad_two = norm_back(grad_rows, hat, inverse, gain)
    grad_out[...] = grad_two
    grad_low = grad_two.astype(BF)
    grad_act = dot(grad_low, w2[:, 128:384])
    grad_act = pltpu.roll(grad_act, 192, 1)
    _, slope_hidden = gelu_pair(hidden[...])
    grad_hidden = jnp.where(iota(grad_act.shape, 1) < cols, grad_act * slope_hidden, 0.0).astype(BF)
    part[...] = dot(grad_hidden, w2[:, 0:256], NT).astype(BF)
    pack[...] = low
    pred_out[...] = jnp.broadcast_to(grad_pred, pred_out.shape)
    low_out[...] = grad_low
    hidden_out[...] = grad_hidden
    r = iota((8, width), 0)
    lane = iota((8, width), 1)
    scalars = jnp.where(lane == 0, loss, jnp.where(lane == 1, count, 0.0))
    rows_out[...] = jnp.where(
        r == 0,
        grad_gain,
        jnp.where(r == 1, grad_shift, jnp.where(r == 2, grad_bias, jnp.where(r == 3, grad_readout, jnp.where(r == 4, scalars, 0.0)))),
    )


def parts_for(rows, keep, send, each, odd, high, number=1):
    for z in range(high):
        for i in range(number):
            keep[z * number + i] = rows[pl.ds(pl.multiple_of(((2 * z + odd) * number + i) * each, 16), each), :]
            send[z * number + i] = rows[pl.ds(pl.multiple_of(((2 * z + 1 - odd) * number + i) * each, 16), each), :]


def ffn_grad_kernel(nlayer, high, normed, grad_hidden, grad_low, act, pack, keyed, *refs):
    outs, (comb, rows) = refs[:nlayer], refs[nlayer:]
    comb[...] = keyed[...].astype(F32).T.astype(BF)
    up = dot(normed[...], grad_hidden[...], TN)
    turned = pltpu.roll(act[...].astype(F32), 64, 1).astype(BF)
    down = dot(grad_low[...], turned, TN)
    target = rows if nlayer == 2 else outs[0]
    target[:, 0:128] = up[:, 0:128].astype(BF)
    target[:, 128:256] = (up[:, 128:256] + down[:, 0:128]).astype(BF)
    target[:, 256:384] = down[:, 128:256].astype(BF)
    if nlayer == 2:
        half = outs[0].shape[1]
        parts_for(rows, *outs, half, lax.axis_index("dp") & 1, high, 2)
        if outs[0].shape[0] > 2 * high:
            lanes = pack[...].astype(F32)
            lanes = jnp.concatenate([lanes[:, 0:384], lanes[:, 384:768]], 0).astype(BF)
            outs[0][2 * high] = lanes
            outs[1][2 * high] = lanes


def attn_back_kernel(nmp, nlayer, high, mols, heads, scale, *refs):
    terms = refs[:nmp]
    resid_one, grad_two, head_rows, vectors, probs, values, normed, w1, ctx = refs[nmp : nmp + 9]
    layer_outs = refs[nmp + 9 : nmp + 9 + nlayer]
    side, key_rows, sides, extras, turned_lay = refs[nmp + 9 + nlayer :]
    group = lax.axis_index("mp")
    width = vectors.shape[1]
    length = probs.shape[1]
    cols = heads * HEAD_DIM
    grad_normed = tree(terms)
    hat, inverse = norm_parts(resid_one[...])
    grad_gain = jnp.sum(grad_normed * hat, 0, keepdims=True)
    grad_shift = jnp.sum(grad_normed, 0, keepdims=True)
    grad_one = grad_two[...] + norm_back(grad_normed, hat, inverse, vectors[2:3, :])
    low = grad_one.astype(BF)
    grad_start = jnp.sum(low.astype(F32), 0, keepdims=True)
    grad_ctx = pltpu.roll(dot(low, w1[:, 512:768]), 192, 1).astype(BF).astype(F32)
    spread_ctx = jnp.broadcast_to(grad_ctx[:, None, :], (mols, heads, 256)).reshape(mols * heads, 256)
    r = iota(spread_ctx.shape, 0) & (heads - 1)
    spread_ctx = jnp.where(r == iota(spread_ctx.shape, 1) // HEAD_DIM, spread_ctx, 0.0).astype(BF)
    grad_probs = dot(spread_ctx, values[...], NT)
    prob = probs[...].astype(F32)
    inner = jnp.sum(prob * grad_probs, -1, keepdims=True)
    grad_scores = (prob * (grad_probs - inner)).astype(BF).astype(F32)
    grad_scores = jnp.sum(grad_scores.reshape(mols, heads, length), 0)
    grad_values = dot(spread_ctx, probs[...], TN)
    sides[0:cols, :] = grad_values[0:cols, :].astype(BF)
    sides[cols:256, :] = jnp.concatenate([grad_scores, jnp.zeros((256 - cols - heads, length), F32)], 0).astype(BF)
    sums = dot(sides[...], normed[...])
    turned_ctx = pltpu.roll(ctx[...].astype(F32), 64, 1).astype(BF)
    out_grad = dot(low, turned_ctx, TN)
    r = iota(sums.shape, 0)
    value_grad = jnp.where(r < cols, sums, 0.0).T
    lay = layer_outs[0] if nlayer == 1 else turned_lay
    lay[:, 0:128] = value_grad[:, 0:128].astype(BF)
    lay[:, 128:256] = (value_grad[:, 128:256] + out_grad[:, 0:128]).astype(BF)
    lay[:, 256:384] = out_grad[:, 128:256].astype(BF)
    if nlayer == 2:
        parts_for(lay, *layer_outs, layer_outs[0].shape[1], lax.axis_index("dp") & 1, high)
    gain = vectors[0:1, :]
    grad_keys = sums[cols : cols + heads, :]
    key_rows[...] = grad_keys
    turned = dot(grad_keys.astype(BF), w1[:, 128:384])
    lane = iota(turned.shape, 1) - 64
    picked = jnp.where((lane >= 0) & (lane // HEAD_DIM == iota(turned.shape, 0)), turned, 0.0)
    grad_query = jnp.sum(pltpu.roll(picked, 192, 1), 0, keepdims=True) * scale
    r = iota(side.shape, 0)
    side[...] = jnp.where(r == 0, grad_query, jnp.where(r == 1, head_rows[4:5, 0:256], 0.0))
    grad_query = jnp.broadcast_to(grad_query.astype(BF), (16, 256))
    grad_row = dot(grad_query, w1[:, 0:256], NT)[0:1, :]
    hat_start, inverse_start = norm_parts(vectors[8:9, :])
    first = jnp.where(group == 0, 1.0, 0.0)
    row_graph = norm_back(grad_row, hat_start, inverse_start, gain) + first * grad_start
    r = iota(extras.shape, 0)
    extra = jnp.where(r == 0, grad_row * hat_start, 0.0)
    extra = jnp.where(r == 1, grad_row, extra)
    extra = jnp.where(r == 2, first * grad_gain, extra)
    extra = jnp.where(r == 3, first * grad_shift, extra)
    extra = jnp.where(r == 8, row_graph, extra)
    for i, o in enumerate((4, 5, 9, 10)):
        extra = jnp.where(r == o, first * head_rows[i : i + 1, :], extra)
    extras[...] = extra


def embed_back_kernel(nmp, mols, *refs):
    sides, comb, extras, vectors, hats, invs, at, seg = refs[:8]
    outs, (total, gains) = refs[8 : 8 + nmp], refs[8 + nmp :]
    width = vectors.shape[1]
    filled = jnp.sum((seg[...] != mols).astype(F32)).astype(I32)
    total[...] = jnp.zeros(total.shape, F32)
    gains[...] = jnp.zeros(gains.shape, F32)
    gain = vectors[0:1, :]

    def one_block(b, unused):
        here = pl.ds(pl.multiple_of(b * BLOCK, BLOCK), BLOCK)
        grad = dot(sides[:, here], comb[...], TN)
        hat_here = hats[here, :].astype(F32)
        low_grad = norm_back(grad, hat_here, invs[here, 0:1], gain).astype(BF)
        total[...] += dot(at[:, here], low_grad)
        gains[0:8, :] += jnp.sum((grad * hat_here).reshape(BLOCK // 8, 8, width), 0)
        gains[8:16, :] += jnp.sum(grad.reshape(BLOCK // 8, 8, width), 0)
        return 0

    lax.fori_loop(0, (filled + BLOCK - 1) // BLOCK, one_block, 0)
    r = iota(extras.shape, 0)
    extra = extras[...] + jnp.where(r == 0, jnp.sum(gains[0:8, :], 0, keepdims=True), 0.0)
    extra += jnp.where(r == 1, jnp.sum(gains[8:16, :], 0, keepdims=True), 0.0)
    for i in range(3):
        extra += jnp.where(r == 6 + i, total[8 * i + 7 : 8 * i + 8, :], 0.0)
    half = width // 2
    nothing = jnp.zeros((1, half), F32)
    for d in range(FEATS // 8):
        row = extra[d // 2 : d // 2 + 1, d % 2 * half : (d % 2 + 1) * half] if d < 22 else nothing
        total[8 * d + 7 : 8 * d + 8, :] = jnp.concatenate([row, nothing], 1)
    group = lax.axis_index("mp")
    each = FEATS // nmp
    for k in range(nmp):
        start = pl.multiple_of((group ^ k) * each, 16)
        outs[k][...] = total[pl.ds(start, each), :].astype(BF)


def loss_row(value, count, lanes):
    a, b, c = three(value)
    lane = iota((1, lanes), 1)
    return jnp.where(lane == 0, a, jnp.where(lane == 1, b, jnp.where(lane == 2, c, jnp.where(lane == 3, count, 0.0))))


def merge_table_kernel(nmp, owners, own, high, *refs):
    terms = refs[:nmp]
    side, key_rows, preds, table_keep, table_send, table_sum, key_sum = refs[nmp:]
    odd = lax.axis_index("dp") & 1
    table_sum[...] = tree(terms)
    half = table_sum.shape[1] // 2
    query = jnp.concatenate([side[0:1, :], jnp.zeros((1, 128), F32)], 1)
    scal = loss_row(side[1:2, 0:1], side[1:2, 1:2], 384)
    r = iota((8, 384), 0)
    mols = preds.shape[0]
    spot = iota((mols, 384), 1) == iota((mols, 384), 0) + lax.axis_index("dp") * mols
    pred_high, pred_mid, _ = three(jnp.sum(jnp.where(spot, preds[:, 0:1], 0.0), 0, keepdims=True))
    scal = jnp.where(r == 0, query, jnp.where(r == 1, scal, jnp.where(r == 2, pred_high, jnp.where(r == 3, pred_mid, 0.0))))
    fill = jnp.zeros((8, 384 - own), F32)
    for p in range(2 * high):
        key_sum[p] = jnp.concatenate([key_rows[:, p * own : (p + 1) * own], fill], 1)
    for z in range(high):
        for out, x in ((table_keep, odd), (table_send, 1 - odd)):
            p = 2 * z + x
            if 2 * z < owners:
                each = table_sum[pl.ds(pl.multiple_of(p * 8, 8), 8), :]
            else:
                each = jnp.zeros((8, 2 * half), F32)
            out[z] = jnp.concatenate([each[:, 0:half], each[:, half:], key_sum[p], scal], 0).astype(BF)


def merge_kernel(layer_keep, layer_came, table_keep, table_came, *outs):
    deep = layer_keep.shape[1]
    mine = lax.axis_index("dp") >> 1
    r = iota((16, 384), 0)
    for k, out in enumerate(outs):
        z = mine ^ k
        out[0:deep, :] = (layer_keep[z].astype(F32) + layer_came[z].astype(F32)).astype(BF)
        out[deep : deep + 16, :] = (table_keep[z, 0:16].astype(F32) + table_came[z, 0:16].astype(F32)).astype(BF)
        both = table_keep[z, 16:32].astype(F32) + table_came[z, 16:32].astype(F32)
        loss = both[9:10, 0:1] + both[9:10, 1:2] + both[9:10, 2:3]
        out[deep + 16 :, :] = jnp.where(r == 9, loss_row(loss, both[9:10, 3:4], 384), both).astype(BF)


def ffn_all_kernel(keep, came, *outs):
    mine = lax.axis_index("dp") >> 1
    for k, out in enumerate(outs):
        out[...] = (keep[mine ^ k].astype(F32) + came[mine ^ k].astype(F32)).astype(BF)


def ffn_x_kernel(keep, came, near_keep, near_send, pair):
    me = lax.axis_index("dp")
    odd, side = me & 1, (me >> 1) & 1
    for out, s in ((near_keep, side), (near_send, 1 - side)):
        for h in range(2):
            for i in range(2):
                p = (2 * h + s) * 2 + i
                out[h, i * 48 : (i + 1) * 48, :] = (keep[p].astype(F32) + came[p].astype(F32)).astype(BF)
    last = keep.shape[0] - 1
    pair[odd] = keep[last]
    pair[1 - odd] = came[last]


def quad_kernel(pair, far, quad):
    for i in range(2):
        quad[i] = pair[i]
        quad[2 + i] = far[2 + i]


def ffn_z_kernel(keep, came, pair, far_keep, far_send):
    side = lax.axis_index("dp") >> 2
    each = far_send.shape[1]
    for i in range(2):
        rows = slice(i * each, (i + 1) * each)
        far_keep[i] = (keep[side, rows].astype(F32) + came[side, rows].astype(F32)).astype(BF)
        far_send[i] = (keep[1 - side, rows].astype(F32) + came[1 - side, rows].astype(F32)).astype(BF)
        far_send[2 + i] = pair[i]


def sum_squares(value):
    return jnp.sum(jnp.sum(value * value, 0, keepdims=True), 1, keepdims=True)


def outer_kernel(npiece, nkept, head_at, *refs):
    pieces, (preds, vectors), sources = refs[:npiece], refs[npiece : npiece + 2], refs[npiece + 2 : npiece + 2 + nkept]
    head_grad, square = refs[npiece + 2 + nkept : npiece + 4 + nkept]
    kept, (rows, low, sems) = refs[npiece + 4 + nkept : -3], refs[-3:]
    copies = [pltpu.make_async_copy(sources[i], kept[i], sems.at[i]) for i in range(nkept)]
    copies[head_at].start()
    for i, copy in enumerate(copies):
        if i != head_at:
            copy.start()
    slots = rows.shape[0]
    if npiece == 1:
        rows[...] = pieces[0][...]
        column = preds[:, 0:1]
    else:
        mine = lax.axis_index("dp") >> 1
        for k in range(4):
            for x in range(2):
                part = pieces[k & 1][(k & 2) + x].astype(F32)
                mols = part.shape[0] // 2
                part = jnp.concatenate([part[0:mols, :], part[mols:, :]], 1)
                part = jnp.concatenate([part, jnp.zeros((32 - mols, part.shape[1]), F32)], 0).astype(BF)
                rows[pl.ds(pl.multiple_of(((mine ^ k) * 2 + x) * 32, 16), 32), :] = part
        r = iota((slots, 384), 0)
        spot = (iota((slots, 384), 1) == r - (r >> 5) * (32 - mols)) & ((r & 31) < mols)
        column = jnp.sum(jnp.where(spot, preds[2:3, :] + preds[3:4, :], 0.0), -1, keepdims=True)
    copies[head_at].wait()
    low[...] = kept[head_at][...].astype(BF)
    mid = dot(rows[...], low[...]) + vectors[9:10, :]
    _, slope = gelu_pair(mid)
    readout = vectors[10:11, :].astype(BF).astype(F32)
    grad = dot(rows[...], (column * readout * slope).astype(BF), TN)
    head_grad[...] = grad
    square[...] = jnp.broadcast_to(sum_squares(grad), square.shape)
    for i, copy in enumerate(copies):
        if i != head_at:
            copy.wait()


def owner_kernel(own, cols, scale, dp, *refs):
    parts, ffn_parts, (query, vectors, layer, send, scalars, preds) = refs[: dp // 2], refs[dp // 2 : -6], refs[-6:]
    width = vectors.shape[1]
    summed = tree(parts)
    if ffn_parts[0].shape[0] == 2:
        near, far = ffn_parts
        ffn = jnp.concatenate([near[i].astype(F32) + far[i].astype(F32) for i in range(2)], 0)
    else:
        ffn = tree(ffn_parts)
    deep = ffn.shape[0]
    acc, summed = summed[0:deep, :], summed[deep:, :]
    table, keys, side = summed[0:16, :], summed[16:24, 0:128], summed[24:32, :]
    preds[...] = side
    key_grad = dot(keys, query[...], TN, HIGHEST) * scale
    hat, _ = norm_parts(vectors[8:9, :])
    start_row = (hat * vectors[0:1, :] + vectors[1:2, :]).astype(BF).astype(F32)
    here = iota((deep, width), 1) == iota((deep, width), 0) + lax.axis_index("dp") * own
    start_col = jnp.sum(jnp.where(here, start_row, 0.0), -1, keepdims=True)
    square = sum_squares(table)
    grads = [start_col * side[0:1, 0:256], key_grad, acc[:, 0:256], acc[:, 192:384], ffn[:, 0:256], ffn[:, 192:384]]
    for j, grad in enumerate(grads):
        grad = grad[0:own, 0:cols]
        layer[j] = grad
        square += sum_squares(grad)
    a, b, c = three(square)
    lane = iota((16, 384), 1)
    tail = jnp.where(lane == 0, a, jnp.where(lane == 1, b, jnp.where(lane == 2, c, 0.0)))
    packet = jnp.where(iota((16, 384), 0) == 15, tail, table).astype(BF)
    for p in range(send.shape[0]):
        send[p] = packet
    loss = side[1:2, 0:1] + side[1:2, 1:2] + side[1:2, 2:3]
    scalars[...] = jnp.where(iota(scalars.shape, 1) == 0, loss, side[1:2, 3:4])


def adam(weight, first, second, grad, rate):
    first_new = BETA_ONE * first + (1.0 - BETA_ONE) * grad
    second_new = BETA_TWO * second + (1.0 - BETA_TWO) * grad * grad
    fixed_one = 1.0 - BETA_ONE**STEP
    fixed_two = 1.0 - BETA_TWO**STEP
    scaled = second_new * (1.0 / fixed_two)
    root = scaled * lax.rsqrt(jnp.maximum(scaled, 1e-36))
    update = first_new * (1.0 / fixed_one) / (root + ADAM_EPS)
    return first_new, second_new, weight - rate * (update + WEIGHT_DECAY * weight)


def update_kernel(nmp, cols, *refs):
    arrived, refs = refs[:nmp], refs[nmp:]
    (
        head_square, scalars, layer, left_roots, right_roots, weights, left, right,
        tables, tables_m, tables_v, head, head_m, head_v, head_grad, vectors, vectors_m, vectors_v,
    ) = refs[:18]
    loss_out, count_out, norm_out = refs[18:21]
    outs = refs[21:34]
    held = refs[34:47]
    grads, vector_grads, packets, sems = refs[47:]
    layer_out, weights_out, left_out, right_out, tm_out, tv_out, t_out, hm_out, hv_out, h_out, vm_out, vv_out, v_out = held
    started = []

    def send(i, rows=None):
        src, dst = held[i], outs[i]
        if rows is not None:
            src, dst = src.at[rows], dst.at[rows]
        copy = pltpu.make_async_copy(src, dst, sems.at[len(started)])
        copy.start()
        started.append(copy)

    group = lax.axis_index("mp")
    for k in range(nmp):
        packets[group ^ k] = arrived[k][...]
    tails = jnp.zeros((16, 128), F32)
    for m in range(nmp):
        for p in range(packets.shape[1]):
            tails += packets[m, p, :, 0:128].astype(F32)
    square = head_square[0:1, 0:1] + tails[15:16, 0:1] + tails[15:16, 1:2] + tails[15:16, 2:3]
    loss, count = scalars[0:1, 0:1], scalars[0:1, 1:2]
    norm = jnp.sqrt(square) / count
    factor = CLIP / jnp.maximum(norm, CLIP) / count
    loss_out[...] = loss
    count_out[...] = count
    norm_out[...] = norm
    for j in range(6):
        layer_out[:, j * cols : (j + 1) * cols] = layer[j] * factor
    send(0)
    width = head.shape[0]
    parts = 8
    each = width // parts
    for i in range(parts):

        def some_rows(t, unused, i=i):
            rows = pl.ds(pl.multiple_of(i * each + t * 8, 8), 8)
            hm_out[rows, :], hv_out[rows, :], h_out[rows, :] = adam(
                head[rows, :], head_m[rows, :], head_v[rows, :], head_grad[rows, :] * factor, RATE_HEAD
            )
            return 0

        lax.fori_loop(0, each // 8, some_rows, 0, unroll=4)
        for k in (7, 8, 9):
            send(k, pl.ds(i * each, each))
    scale = (1.0 - STATS_DECAY) * factor * factor
    for j in range(6):
        low = layer[j].astype(BF)
        right_out[j] = STATS_DECAY * right[j] + scale * dot(low, low, TN)
        left_out[j] = STATS_DECAY * left[j] + scale * dot(low, low, NT)
    send(3)
    send(2)
    for j in range(6):
        span = slice(j * cols, (j + 1) * cols)
        low = layer[j].astype(BF)
        shaped = dot(dot(left_roots[j].astype(BF), low).astype(BF), right_roots[j].astype(BF))
        weights_out[:, span] = weights[:, span] - RATE_LAYER * (shaped * factor + WEIGHT_DECAY * weights[:, span])
    send(1)
    half = grads.shape[1] // 2
    high = FEATS // 8 // nmp
    for m in range(nmp):
        for p in range(high):
            piece = packets[m, p].astype(F32) * factor
            d = m * high + p
            grads[7 * d : 7 * d + 7, :] = jnp.concatenate([piece[0:7, :], piece[8:15, :]], 1)
            if d < 22:
                vector_grads[d // 2 : d // 2 + 1, d % 2 * half : (d % 2 + 1) * half] = piece[7:8, :]
    rows = tables.shape[0]

    def table_rows(t, unused):
        r = pl.ds(pl.multiple_of(t * 8, 8), 8)
        tm_out[r, :], tv_out[r, :], t_out[r, :] = adam(tables[r, :], tables_m[r, :], tables_v[r, :], grads[r, :], RATE_TABLES)
        return 0

    lax.fori_loop(0, rows // 8, table_rows, 0, unroll=4)
    for k in (4, 5, 6):
        send(k)
    nrows = vectors.shape[0]
    vm_out[...], vv_out[...], v_out[...] = adam(vectors[...], vectors_m[...], vectors_v[...], vector_grads[0:nrows, :], RATE_VECTORS)
    for k in (10, 11, 12):
        send(k)
    for copy in started:
        copy.wait()


def exchange(x, axis):
    n = lax.axis_size(axis)
    return [x] + [lax.ppermute(x, axis, [(i, i ^ k) for i in range(n)]) for k in range(1, n)]


def flip(x, k):
    n = lax.axis_size("dp")
    return lax.ppermute(x, "dp", [(i, i ^ k) for i in range(n)])


def after(values, *others):
    return lax.optimization_barrier((tuple(values), tuple(others)))[0]


def spread(x, second=()):
    four, one, two = after([flip(x, 4), flip(x, 1), flip(x, 2)], *second)
    return [x, one, two, flip(two, 1), four, flip(four, 1), flip(four, 2), flip(one, 6)]


def per_device(
    lap_vectors,
    eig_index,
    type_ids,
    seg_ids,
    targets,
    layer_weights,
    left_stats,
    right_stats,
    left_roots,
    right_roots,
    tables,
    tables_m,
    tables_v,
    head_weight,
    head_m,
    head_v,
    vectors,
    vectors_m,
    vectors_v,
):
    dp = lax.axis_size("dp")
    nmp = lax.axis_size("mp")
    length = seg_ids.shape[1]
    mols = targets.shape[1]
    width = vectors.shape[1]
    own, group_cols = layer_weights.shape[0], layer_weights.shape[1]
    cols = group_cols // 6
    heads = cols // HEAD_DIM
    scale = HEAD_DIM ** (-0.5)
    owners = FEATS // nmp // 8

    w = layer_weights.astype(BF)
    sources = [in_hbm(x) for x in (lap_vectors[0].T, eig_index[0].T, type_ids, seg_ids, tables, vectors)]
    at, normed, hats, invs = call(
        functools.partial(embed_kernel, mols),
        [sds((FEATS, length), BF), sds((length, width), BF), sds((length, width), BF), sds((length, 128), F32)],
        sources,
        [pltpu.VMEM(x.shape, x.dtype) for x in sources]
        + [pltpu.VMEM((FEATS, width), BF), pltpu.VMEM((FEATS, width), BF), pltpu.VMEM((8, length), I32), pltpu.SemaphoreType.DMA((6,))],
        flops=4 * length * FEATS * width,
        in_specs=[IN_PLACE] * 6,
    )
    direct = dp == 8 and own == 4 * mols and own % 16 == 0
    if direct:
        ones = spread(w, (normed,))
    else:
        ones = [lax.all_gather(w, "dp", axis=0, tiled=True)]
    np_ = len(ones)
    part, probs, values, ctx, keyed, query, w1, w2 = call(
        functools.partial(attn_kernel, np_, mols, heads, scale),
        [
            sds((mols, width), BF),
            sds((mols * heads, length), BF),
            sds((length, 256), BF),
            sds((mols, 256), BF),
            sds((width, 256), BF),
            sds((8, 256), F32),
            sds((width, 4 * cols), BF),
            sds((width, 2 * cols), BF),
        ],
        [normed, seg_ids, vectors, *ones],
        flops=4 * length * 256 * width,
    )
    part, resid_one, normed_two, hidden, act = call(
        functools.partial(ffn_kernel, nmp, cols),
        [
            sds((mols, width), BF),
            sds((mols, width), F32),
            sds((mols, width), BF),
            sds((mols, 256), F32),
            sds((mols, 256), BF),
        ],
        [*exchange(part, "mp"), vectors, w2],
        flops=4 * mols * width * 256,
    )
    part, pack, grad_pred, grad_two, grad_low, grad_hidden, head_rows = call(
        functools.partial(head_kernel, nmp, cols),
        [
            sds((mols, width), BF),
            sds((mols, width), BF),
            sds((mols, 128), F32),
            sds((mols, width), F32),
            sds((mols, width), BF),
            sds((mols, 256), BF),
            sds((8, width), F32),
        ],
        [*exchange(part, "mp"), resid_one, vectors, head_weight, targets, seg_ids, hidden, w2],
        [pltpu.VMEM((width, width), BF)],
        flops=4 * width * width * mols,
    )
    odd = lax.axis_index("dp") & 1
    high = dp // 2
    deep = (own + 15) // 16 * 16
    nlayer = 2 if own == deep else 1

    def halves(parts):
        if nlayer == 2:
            return parts
        both = parts[0].reshape(high, 2, own, -1)
        both = jnp.pad(both, ((0, 0), (0, 0), (0, deep - own), (0, 0)))
        return [lax.dynamic_index_in_dim(both, i, 1, False) for i in (odd, 1 - odd)]

    def half_shapes(lanes, number=1, more=0):
        return [sds((high * number + more, own // number, lanes), BF)] * 2 if nlayer == 2 else [sds((width, lanes), BF)]

    number = 2 if direct else 1
    parts = exchange(part, "mp")
    *ffn_parts, comb = call(
        functools.partial(ffn_grad_kernel, nlayer, high),
        half_shapes(384, number, number - 1) + [sds((256, width), BF)],
        [normed_two, grad_hidden, grad_low, act, pack, keyed],
        [pltpu.VMEM((width, 384), BF)],
        flops=4 * mols * width * 256,
    )
    ffn_keep, ffn_send = halves(ffn_parts)
    (ffn_send,) = after([ffn_send], *parts[1:])
    ffn_came = flip(ffn_send, 1)
    *layer_halves, side, key_rows, sides, extras = call(
        functools.partial(attn_back_kernel, nmp, nlayer, high, mols, heads, scale),
        half_shapes(384)
        + [sds((8, 256), F32), sds((8, width), F32), sds((256, length), BF), sds((16, width), F32)],
        [*parts, resid_one, grad_two, head_rows, vectors, probs, values, normed, w1, ctx],
        [pltpu.VMEM((width, 384), BF)],
        flops=4 * length * 256 * width,
    )
    layer_keep, layer_send = halves(layer_halves)
    layer_came = flip(layer_send, 1)
    shares = call(
        functools.partial(embed_back_kernel, nmp, mols),
        [sds((FEATS // nmp, width), BF) for _ in range(nmp)],
        [sides, comb, extras, vectors, hats, invs, at, seg_ids],
        [pltpu.VMEM((FEATS, width), F32), pltpu.VMEM((16, width), F32)],
        flops=4 * length * 256 * width,
    )
    moved = [shares[0]] + [lax.ppermute(shares[k], "mp", [(i, i ^ k) for i in range(nmp)]) for k in range(1, nmp)]
    table_keep, table_send = call(
        functools.partial(merge_table_kernel, nmp, owners, own, high),
        [sds((high, 32, 384), BF)] * 2,
        [*moved, side, key_rows, grad_pred],
        [pltpu.VMEM((FEATS // nmp, width), F32), pltpu.VMEM((dp, 8, 384), F32)],
    )
    (ffn_came,) = after([ffn_came], shares[0])
    if direct:
        near_keep, near_send, pair = call(
            ffn_x_kernel,
            [sds((2, own, 384), BF)] * 2 + [sds((2, 2 * mols, width // 2), BF)],
            [ffn_keep, ffn_came],
        )
        far_keep, far_send = call(
            ffn_z_kernel,
            [sds((2, own // 2, 384), BF), sds((4, own // 2, 384), BF)],
            [near_keep, flip(near_send, 2), pair],
        )
        ffn_parts = [far_keep, flip(far_send, 4)]
    else:
        ffn_parts = call(ffn_all_kernel, [sds((deep, 384), BF)] * high, [ffn_keep, ffn_came])
        ffn_parts = [ffn_parts[0]] + [flip(ffn_parts[k], 2 * k) for k in range(1, high)]
    merged = call(
        merge_kernel,
        [sds((deep + 32, 384), BF)] * high,
        [layer_keep, layer_came, table_keep, flip(table_send, 1)],
    )
    merged = [merged[0]] + [flip(merged[k], 2 * k) for k in range(1, high)]
    layer, send, scalars, preds = call(
        functools.partial(owner_kernel, own, cols, scale, dp),
        [sds((6, own, cols), F32), sds((dp, 16, 384), BF), sds((8, 128), F32), sds((8, 384), F32)],
        [*merged, *ffn_parts, query, vectors],
        flops=2 * own * 256 * 1024,
    )
    kept = [
        jnp.swapaxes(left_roots, 0, 1), right_roots[0], layer_weights, jnp.swapaxes(left_stats, 0, 1), right_stats[0],
        tables, tables_m, tables_v, head_weight, head_m, head_v, vectors, vectors_m, vectors_v,
    ]
    sums = lax.all_to_all(send, "dp", 0, 0, tiled=True)
    if direct:
        (far,) = after([ffn_parts[1]], scalars)
        (quad,) = call(quad_kernel, [sds((4, 2 * mols, 384), BF)], [pair, far])
        (came,) = after([flip(quad, 2)], sums)
        pieces = [quad, came]
    else:
        pieces = [jnp.pad(lax.all_gather(pack, "dp", axis=0), ((0, 0), (0, 32 - mols), (0, 0))).reshape(dp * 32, -1)]
        preds = jnp.pad(lax.all_gather(grad_pred, "dp", axis=0), ((0, 0), (0, 32 - mols), (0, 0))).reshape(dp * 32, -1)
    sums = exchange(sums, "mp")
    head_grad, head_square, *kept = call(
        functools.partial(outer_kernel, len(pieces), len(kept), 8),
        [sds((width, width), F32), sds((8, 128), F32)] + [pltpu.VMEM(x.shape, F32) for x in kept],
        [*pieces, preds, vectors, *[in_hbm(x) for x in kept]],
        [pltpu.VMEM((dp * 32, width), BF), pltpu.VMEM((width, width), BF), pltpu.SemaphoreType.DMA((len(kept),))],
        flops=4 * dp * mols * width * width,
        in_specs=[IN_VMEM] * (len(pieces) + 2) + [IN_PLACE] * len(kept),
        vmem=16 + dp // 4,
    )
    kept = [in_vmem(x) for x in kept]
    results = [
        sds((own, group_cols), F32),
        sds((own, group_cols), F32),
        sds((6, own, own), F32),
        sds((6, cols, cols), F32),
        *[sds(tables.shape, F32)] * 3,
        *[sds(head_weight.shape, F32)] * 3,
        *[sds(vectors.shape, F32)] * 3,
    ]
    outs = call(
        functools.partial(update_kernel, nmp, cols),
        [sds((1, 1), F32)] * 3 + results,
        [
            *sums, head_square, scalars, layer, *kept[:11], head_grad, *kept[11:],
        ],
        [pltpu.VMEM(x.shape, x.dtype) for x in results] + [pltpu.VMEM((FEATS, width), F32), pltpu.VMEM((16, width), F32), pltpu.VMEM((nmp, dp, 16, 384), BF), pltpu.SemaphoreType.DMA((34,))],
        flops=20 * width * width,
        vmem=24,
        out_specs=[IN_VMEM] * 3 + [IN_PLACE] * 13,
    )
    loss, count, norm, layer_grad, layer_new, left_new, right_new, tm, tv, tn, hm, hv, hn, vm, vv, vn = outs
    return (
        loss.reshape(()),
        count.reshape(()),
        norm.reshape(()),
        layer_grad,
        layer_new,
        jnp.swapaxes(left_new, 0, 1),
        right_new[None],
        tm,
        tv,
        tn,
        hm,
        hv,
        hn,
        vm,
        vv,
        vn,
    )


def solution(mesh):
    placed = (
        P("dp", None, None),
        P("dp", None, None),
        P("dp", None),
        P("dp", None),
        P("dp", None),
        P("dp", "mp"),
        P("dp", "mp", None),
        P("dp", "mp", None, None),
        P("dp", "mp", None),
        P("dp", "mp", None, None),
        *[P()] * 9,
    )
    return jax.shard_map(
        per_device,
        mesh=mesh,
        in_specs=placed,
        out_specs=(
            P(),
            P(),
            P(),
            P("dp", "mp"),
            P("dp", "mp"),
            P("dp", "mp", None),
            P("dp", "mp", None, None),
            *[P()] * 9,
        ),
        check_vma=False,
    )
```

```python
import functools
import math

import jax
import jax.numpy as jnp
from jax import lax
from jax.experimental import pallas as pl
from jax.experimental.pallas import tpu as pltpu
from jax.sharding import PartitionSpec as P

HEAD_DIM = 24
TYPES = 192
STEP = 10
NORM_EPS = 1e-05
CLIP = 0.25
STATS_DECAY = 0.95
RATE_LAYER = 0.15
RATE_TABLES = 0.15
RATE_HEAD = 0.01
RATE_VECTORS = 0.2
BETA_ONE = 0.9
BETA_TWO = 0.99
ADAM_EPS = 1e-08
WEIGHT_DECAY = 0.01
MASKED = -1000000000.0
GELU_C = 0.7978845608028654
GELU_A = 0.044715

BF = jnp.bfloat16
F32 = jnp.float32
I32 = jnp.int32
HIGHEST = lax.Precision.HIGHEST
NN = ((1,), (0,))
NT = ((1,), (1,))
TN = ((0,), (0,))
BLOCK = 256
FEATS = 256
MIB = 1024 * 1024


def dot(a, b, dims=NN, precision=None):
    return lax.dot_general(a, b, (dims, ((), ())), preferred_element_type=F32, precision=precision)


def iota(shape, dim):
    return lax.broadcasted_iota(I32, shape, dim)


IN_VMEM = pl.BlockSpec(memory_space=pltpu.VMEM)
IN_PLACE = pl.BlockSpec(memory_space=pltpu.HBM)


def call(kernel, outs, ins, scratch=(), flops=0, vmem=16, in_specs=None, out_specs=None):
    moved = sum(math.prod(x.shape) * x.dtype.itemsize for x in list(ins) + list(outs))
    return pl.pallas_call(
        kernel,
        out_shape=tuple(outs),
        in_specs=in_specs or [IN_VMEM] * len(ins),
        out_specs=tuple(out_specs or [IN_VMEM] * len(outs)),
        scratch_shapes=list(scratch),
        compiler_params=pltpu.CompilerParams(vmem_limit_bytes=vmem * MIB),
        cost_estimate=pl.CostEstimate(flops=flops, bytes_accessed=moved, transcendentals=0),
    )(*ins)


def in_hbm(x):
    return pltpu.with_memory_space_constraint(x, pltpu.HBM)


def in_vmem(x):
    return pltpu.with_memory_space_constraint(x, pltpu.VMEM)


def sds(shape, dtype):
    return jax.ShapeDtypeStruct(shape, dtype)


def norm_parts(values):
    center = values - jnp.mean(values, -1, keepdims=True)
    spread = jnp.mean(center * center, -1, keepdims=True)
    inverse = lax.rsqrt(spread + NORM_EPS)
    return center * inverse, inverse


def norm_back(grad, hat, inverse, gain):
    scaled = grad * gain
    mean_one = jnp.mean(scaled, -1, keepdims=True)
    mean_two = jnp.mean(scaled * hat, -1, keepdims=True)
    return inverse * (scaled - mean_one - hat * mean_two)


def gelu_pair(x):
    t = jnp.tanh(GELU_C * (x + GELU_A * x * x * x))
    value = 0.5 * x * (1.0 + t)
    slope = 0.5 * (1.0 + t) + 0.5 * x * (1.0 - t * t) * (GELU_C * (1.0 + 3.0 * GELU_A * x * x))
    return value, slope


def tree(refs):
    parts = [r[...].astype(F32) for r in refs]
    while len(parts) > 1:
        parts = [parts[i] + parts[i + 1] for i in range(0, len(parts), 2)]
    return parts[0]


def three(x):
    high = x.astype(BF).astype(F32)
    mid = (x - high).astype(BF).astype(F32)
    return high, mid, x - high - mid


def assemble(pieces, first, second, owner):
    rows = pieces[0].shape[0]
    split = first.shape[1]
    for k, piece in enumerate(pieces):
        here = pl.ds(0 if len(pieces) == 1 else pl.multiple_of((owner ^ k) * rows, 16), rows)
        first[here, :] = piece[:, 0:split]
        second[here, :] = piece[:, split:]


def spaced(t):
    return t + ((t * 9363) >> 16)


def embed_kernel(mols, *refs):
    sources, (at, normed, hats, invs), held, (high, low, prev, sems) = refs[:6], refs[6:10], refs[10:16], refs[16:]
    copies = [pltpu.make_async_copy(a, b, sems.at[i]) for i, (a, b) in enumerate(zip(sources, held))]
    for copy in copies:
        copy.start()
    normed[...] = jnp.zeros(normed.shape, BF)
    for copy in copies:
        copy.wait()
    lap, eig, kinds, seg, tables, vectors = held
    length = seg.shape[1]
    width = vectors.shape[1]
    rows = tables.shape[0]
    tab = tables[...]
    tab_high = tab.astype(BF)
    rest = jnp.where(iota(tab.shape, 0) < TYPES, tab - tab_high.astype(F32), 0.0).astype(BF)
    place = (iota((FEATS, rows), 0) == spaced(iota((FEATS, rows), 1))).astype(F32).astype(BF)
    r = iota((32, width), 0)
    extra = jnp.where(r == 7, vectors[6:7, :], jnp.where(r == 15, vectors[7:8, :], jnp.where(r == 23, vectors[8:9, :], 0.0)))
    extra_high = extra.astype(BF)
    placed = dot(place, tab_high)
    high[0:32, :] = (placed[0:32, :] + extra_high.astype(F32)).astype(BF)
    high[32:, :] = placed[32:, :].astype(BF)
    placed = dot(place, rest)
    low[0:32, :] = (placed[0:32, :] + extra - extra_high.astype(F32)).astype(BF)
    low[32:, :] = placed[32:, :].astype(BF)
    place = place[:, TYPES:]
    seg_row = seg[...]
    before = pltpu.roll(jnp.broadcast_to(seg_row, (8, length)), 1, 1)
    before = jnp.where(iota((8, length), 1) == 0, -1, before)
    prev[...] = before
    filled = jnp.sum((seg_row != mols).astype(F32)).astype(I32)
    gain = vectors[0:1, :]
    shift = vectors[1:2, :]
    window = 2 * BLOCK

    def one_block(b, unused):
        start = pl.multiple_of(b * BLOCK, BLOCK)
        here = pl.ds(start, BLOCK)
        first = pl.multiple_of(jnp.clip(start - 128, 0, length - window), 128)
        source = iota((window, BLOCK), 0) + first
        one = eig[0:1, here]
        two = eig[1:2, here]
        near = lap[:, pl.ds(first, window)].astype(BF)
        pair_one = dot(near, (source == one).astype(F32).astype(BF))
        pair_two = dot(near, (source == two).astype(F32).astype(BF))
        seg_here = seg[0:1, here]
        begins = (seg_here != mols) & (seg_here != prev[0:1, here])
        kind = jnp.where(begins, -1, spaced(kinds[0:1, here]))
        keep = jnp.where(begins, 0.0, 1.0)
        which = jnp.where(begins, 23, jnp.where(one == two, 7, 15))
        pair = (jnp.concatenate([pair_one, pair_two], 0) * keep).astype(BF)
        spot = iota((FEATS, BLOCK), 0)
        at[:, here] = (((spot == kind) | (spot == which)).astype(F32) + dot(place, pair)).astype(BF)
        picks = at[:, here]
        resid = dot(picks, high[...], TN) + dot(picks, low[...], TN)
        hat, inverse = norm_parts(resid)
        normed[here, :] = (hat * gain + shift).astype(BF)
        hats[here, :] = hat.astype(BF)
        invs[here, :] = jnp.broadcast_to(inverse, (BLOCK, 128))
        return 0

    lax.fori_loop(0, (filled + BLOCK - 1) // BLOCK, one_block, 0)


def attn_kernel(npiece, mols, heads, scale, *refs):
    normed, seg, vectors = refs[:3]
    ones = refs[3 : 3 + npiece]
    part, probs, values, ctx_out, keyed, query_out, w1, w2 = refs[3 + npiece :]
    assemble(ones, w1, w2, lax.axis_index("dp"))
    width = vectors.shape[1]
    cols = heads * HEAD_DIM
    hat, _ = norm_parts(vectors[8:9, :])
    start_row = (hat * vectors[0:1, :] + vectors[1:2, :]).astype(BF)
    q = dot(jnp.broadcast_to(start_row, (16, width)), w1[:, 0:256])
    q = q.astype(BF).astype(F32)
    q = jnp.where(iota((16, 256), 1) < cols, q, 0.0)
    r = iota((16, 256), 0)
    head_of = iota((16, 256), 1) // HEAD_DIM
    query_out[...] = jnp.where(r == head_of, q, 0.0)[0:8, :]
    shifted = pltpu.roll(q, 64, 1)[0:1, :]
    r = iota((128, 256), 0)
    lane = iota((128, 256), 1) - 64
    pick = (lane >= 0) & ((r & 7) == lane // HEAD_DIM) & (r >= 64) & (r < 80)
    q_keys = jnp.where(pick, shifted, 0.0).astype(BF)
    u = dot(w1[:, 128:384], q_keys, NT)
    u_high = u.astype(BF)
    lane = iota(u.shape, 1)
    u_both = jnp.where(lane < 72, u_high.astype(F32), u - u_high.astype(F32))
    last = w1[:, 512:640].astype(F32)
    side = jnp.where(lane < 64, last, u_both).astype(BF)
    keyed[:, 0:128] = w1[:, 384:512]
    keyed[:, 128:256] = jnp.where(lane < 64, last, jnp.where(lane < 72, u * scale, 0.0)).astype(BF)
    normed_all = normed[...]
    values[:, 0:128] = dot(normed_all, w1[:, 384:512]).astype(BF)
    second = dot(normed_all, side)
    values[:, 128:256] = jnp.where(iota(second.shape, 1) < 64, second, 0.0).astype(BF)
    turned = second.T
    scores = (turned[64:72, :] + turned[72:80, :]) * scale
    seg_row = seg[...]
    length = seg_row.shape[1]
    mine = iota((mols, 1, length), 0) == seg_row[None]
    masked = jnp.where(mine, scores[None], MASKED)
    peak = jnp.max(masked, -1, keepdims=True)
    grown = jnp.exp(masked - peak)
    total = jnp.sum(grown, -1, keepdims=True)
    prob = (grown * (1.0 / total)).reshape(mols * heads, length).astype(BF)
    probs[...] = prob
    wide = dot(prob, values[...])
    r = iota(wide.shape, 0) & (heads - 1)
    wide = jnp.where(r == iota(wide.shape, 1) // HEAD_DIM, wide, 0.0)
    ctx = jnp.sum(wide.reshape(mols, heads, 256), 1)
    ctx_out[...] = ctx.astype(BF)
    turned_ctx = pltpu.roll(ctx, 64, 1).astype(BF)
    part[...] = dot(turned_ctx, w1[:, 512:768], NT).astype(BF)


def ffn_kernel(nmp, cols, *refs):
    terms = refs[:nmp]
    vectors, w2, part, resid_out, normed_out, hidden_out, act_out = refs[nmp:]
    resid = vectors[8:9, :] + tree(terms)
    resid_out[...] = resid
    hat, _ = norm_parts(resid)
    low = (hat * vectors[2:3, :] + vectors[3:4, :]).astype(BF)
    normed_out[...] = low
    hidden = dot(low, w2[:, 0:256])
    hidden = jnp.where(iota(hidden.shape, 1) < cols, hidden, 0.0)
    hidden_out[...] = hidden
    act, _ = gelu_pair(hidden)
    act_out[...] = act.astype(BF)
    turned = pltpu.roll(act, 64, 1).astype(BF)
    part[...] = dot(turned, w2[:, 128:384], NT).astype(BF)


def head_kernel(nmp, cols, *refs):
    terms = refs[:nmp]
    resid_one, vectors, head, targets, seg, hidden, w2 = refs[nmp : nmp + 7]
    part, pack, pred_out, grad_out, low_out, hidden_out, rows_out, head_low = refs[nmp + 7 :]
    width = vectors.shape[1]
    mols = targets.shape[1]
    head_low[...] = head[...].astype(BF)
    resid = resid_one[...] + tree(terms)
    hat, inverse = norm_parts(resid)
    gain = vectors[4:5, :]
    low = (hat * gain + vectors[5:6, :]).astype(BF)
    mid = dot(low, head_low[...]) + vectors[9:10, :]
    act_head, slope = gelu_pair(mid)
    act_head = act_head.astype(BF).astype(F32)
    readout = vectors[10:11, :].astype(BF).astype(F32)
    predicted = jnp.sum(act_head * readout, -1, keepdims=True)
    spot = iota((mols, mols), 0) == iota((mols, mols), 1)
    goal = jnp.sum(jnp.where(spot, targets[...], 0.0), -1, keepdims=True)
    seg_row = seg[...]
    there = iota((mols, seg_row.shape[1]), 0) == seg_row
    present = jnp.max(there.astype(F32), -1, keepdims=True)
    error = predicted - goal
    root = jnp.sqrt(error * error + 1.0)
    loss = jnp.sum(present * (root - 1.0), 0, keepdims=True)
    count = jnp.sum(present, 0, keepdims=True)
    grad_pred = present * error / root
    grad_readout = jnp.sum(grad_pred * act_head, 0, keepdims=True)
    grad_mid = (grad_pred * readout * slope).astype(BF)
    grad_bias = jnp.sum(grad_mid.astype(F32), 0, keepdims=True)
    grad_rows = dot(grad_mid, head_low[...], NT)
    grad_gain = jnp.sum(grad_rows * hat, 0, keepdims=True)
    grad_shift = jnp.sum(grad_rows, 0, keepdims=True)
    grad_two = norm_back(grad_rows, hat, inverse, gain)
    grad_out[...] = grad_two
    grad_low = grad_two.astype(BF)
    grad_act = dot(grad_low, w2[:, 128:384])
    grad_act = pltpu.roll(grad_act, 192, 1)
    _, slope_hidden = gelu_pair(hidden[...])
    grad_hidden = jnp.where(iota(grad_act.shape, 1) < cols, grad_act * slope_hidden, 0.0).astype(BF)
    part[...] = dot(grad_hidden, w2[:, 0:256], NT).astype(BF)
    pack[...] = low
    pred_out[...] = jnp.broadcast_to(grad_pred, pred_out.shape)
    low_out[...] = grad_low
    hidden_out[...] = grad_hidden
    r = iota((8, width), 0)
    lane = iota((8, width), 1)
    scalars = jnp.where(lane == 0, loss, jnp.where(lane == 1, count, 0.0))
    rows_out[...] = jnp.where(
        r == 0,
        grad_gain,
        jnp.where(r == 1, grad_shift, jnp.where(r == 2, grad_bias, jnp.where(r == 3, grad_readout, jnp.where(r == 4, scalars, 0.0)))),
    )


def parts_for(rows, keep, send, each, odd, high, number=1):
    for z in range(high):
        for i in range(number):
            keep[z * number + i] = rows[pl.ds(pl.multiple_of(((2 * z + odd) * number + i) * each, 16), each), :]
            send[z * number + i] = rows[pl.ds(pl.multiple_of(((2 * z + 1 - odd) * number + i) * each, 16), each), :]


def ffn_grad_kernel(nlayer, high, normed, grad_hidden, grad_low, act, pack, keyed, *refs):
    outs, (comb, rows) = refs[:nlayer], refs[nlayer:]
    comb[...] = keyed[...].astype(F32).T.astype(BF)
    up = dot(normed[...], grad_hidden[...], TN)
    turned = pltpu.roll(act[...].astype(F32), 64, 1).astype(BF)
    down = dot(grad_low[...], turned, TN)
    target = rows if nlayer == 2 else outs[0]
    target[:, 0:128] = up[:, 0:128].astype(BF)
    target[:, 128:256] = (up[:, 128:256] + down[:, 0:128]).astype(BF)
    target[:, 256:384] = down[:, 128:256].astype(BF)
    if nlayer == 2:
        half = outs[0].shape[1]
        parts_for(rows, *outs, half, lax.axis_index("dp") & 1, high, 2)
        if outs[0].shape[0] > 2 * high:
            lanes = pack[...].astype(F32)
            lanes = jnp.concatenate([lanes[:, 0:384], lanes[:, 384:768]], 0).astype(BF)
            outs[0][2 * high] = lanes
            outs[1][2 * high] = lanes


def attn_back_kernel(nmp, nlayer, high, mols, heads, scale, *refs):
    terms = refs[:nmp]
    resid_one, grad_two, head_rows, vectors, probs, values, normed, w1, ctx = refs[nmp : nmp + 9]
    layer_outs = refs[nmp + 9 : nmp + 9 + nlayer]
    side, key_rows, sides, extras, turned_lay = refs[nmp + 9 + nlayer :]
    group = lax.axis_index("mp")
    width = vectors.shape[1]
    length = probs.shape[1]
    cols = heads * HEAD_DIM
    grad_normed = tree(terms)
    hat, inverse = norm_parts(resid_one[...])
    grad_gain = jnp.sum(grad_normed * hat, 0, keepdims=True)
    grad_shift = jnp.sum(grad_normed, 0, keepdims=True)
    grad_one = grad_two[...] + norm_back(grad_normed, hat, inverse, vectors[2:3, :])
    low = grad_one.astype(BF)
    grad_start = jnp.sum(low.astype(F32), 0, keepdims=True)
    grad_ctx = pltpu.roll(dot(low, w1[:, 512:768]), 192, 1).astype(BF).astype(F32)
    spread_ctx = jnp.broadcast_to(grad_ctx[:, None, :], (mols, heads, 256)).reshape(mols * heads, 256)
    r = iota(spread_ctx.shape, 0) & (heads - 1)
    spread_ctx = jnp.where(r == iota(spread_ctx.shape, 1) // HEAD_DIM, spread_ctx, 0.0).astype(BF)
    grad_probs = dot(spread_ctx, values[...], NT)
    prob = probs[...].astype(F32)
    inner = jnp.sum(prob * grad_probs, -1, keepdims=True)
    grad_scores = (prob * (grad_probs - inner)).astype(BF).astype(F32)
    grad_scores = jnp.sum(grad_scores.reshape(mols, heads, length), 0)
    grad_values = dot(spread_ctx, probs[...], TN)
    sides[0:cols, :] = grad_values[0:cols, :].astype(BF)
    sides[cols:256, :] = jnp.concatenate([grad_scores, jnp.zeros((256 - cols - heads, length), F32)], 0).astype(BF)
    sums = dot(sides[...], normed[...])
    turned_ctx = pltpu.roll(ctx[...].astype(F32), 64, 1).astype(BF)
    out_grad = dot(low, turned_ctx, TN)
    r = iota(sums.shape, 0)
    value_grad = jnp.where(r < cols, sums, 0.0).T
    lay = layer_outs[0] if nlayer == 1 else turned_lay
    lay[:, 0:128] = value_grad[:, 0:128].astype(BF)
    lay[:, 128:256] = (value_grad[:, 128:256] + out_grad[:, 0:128]).astype(BF)
    lay[:, 256:384] = out_grad[:, 128:256].astype(BF)
    if nlayer == 2:
        parts_for(lay, *layer_outs, layer_outs[0].shape[1], lax.axis_index("dp") & 1, high)
    gain = vectors[0:1, :]
    grad_keys = sums[cols : cols + heads, :]
    key_rows[...] = grad_keys
    turned = dot(grad_keys.astype(BF), w1[:, 128:384])
    lane = iota(turned.shape, 1) - 64
    picked = jnp.where((lane >= 0) & (lane // HEAD_DIM == iota(turned.shape, 0)), turned, 0.0)
    grad_query = jnp.sum(pltpu.roll(picked, 192, 1), 0, keepdims=True) * scale
    r = iota(side.shape, 0)
    side[...] = jnp.where(r == 0, grad_query, jnp.where(r == 1, head_rows[4:5, 0:256], 0.0))
    grad_query = jnp.broadcast_to(grad_query.astype(BF), (16, 256))
    grad_row = dot(grad_query, w1[:, 0:256], NT)[0:1, :]
    hat_start, inverse_start = norm_parts(vectors[8:9, :])
    first = jnp.where(group == 0, 1.0, 0.0)
    row_graph = norm_back(grad_row, hat_start, inverse_start, gain) + first * grad_start
    r = iota(extras.shape, 0)
    extra = jnp.where(r == 0, grad_row * hat_start, 0.0)
    extra = jnp.where(r == 1, grad_row, extra)
    extra = jnp.where(r == 2, first * grad_gain, extra)
    extra = jnp.where(r == 3, first * grad_shift, extra)
    extra = jnp.where(r == 8, row_graph, extra)
    for i, o in enumerate((4, 5, 9, 10)):
        extra = jnp.where(r == o, first * head_rows[i : i + 1, :], extra)
    extras[...] = extra


def embed_back_kernel(nmp, mols, *refs):
    sides, comb, extras, vectors, hats, invs, at, seg = refs[:8]
    outs, (total, gains) = refs[8 : 8 + nmp], refs[8 + nmp :]
    width = vectors.shape[1]
    filled = jnp.sum((seg[...] != mols).astype(F32)).astype(I32)
    total[...] = jnp.zeros(total.shape, F32)
    gains[...] = jnp.zeros(gains.shape, F32)
    gain = vectors[0:1, :]

    def one_block(b, unused):
        here = pl.ds(pl.multiple_of(b * BLOCK, BLOCK), BLOCK)
        grad = dot(sides[:, here], comb[...], TN)
        hat_here = hats[here, :].astype(F32)
        low_grad = norm_back(grad, hat_here, invs[here, 0:1], gain).astype(BF)
        total[...] += dot(at[:, here], low_grad)
        gains[0:8, :] += jnp.sum((grad * hat_here).reshape(BLOCK // 8, 8, width), 0)
        gains[8:16, :] += jnp.sum(grad.reshape(BLOCK // 8, 8, width), 0)
        return 0

    lax.fori_loop(0, (filled + BLOCK - 1) // BLOCK, one_block, 0)
    r = iota(extras.shape, 0)
    extra = extras[...] + jnp.where(r == 0, jnp.sum(gains[0:8, :], 0, keepdims=True), 0.0)
    extra += jnp.where(r == 1, jnp.sum(gains[8:16, :], 0, keepdims=True), 0.0)
    for i in range(3):
        extra += jnp.where(r == 6 + i, total[8 * i + 7 : 8 * i + 8, :], 0.0)
    half = width // 2
    nothing = jnp.zeros((1, half), F32)
    for d in range(FEATS // 8):
        row = extra[d // 2 : d // 2 + 1, d % 2 * half : (d % 2 + 1) * half] if d < 22 else nothing
        total[8 * d + 7 : 8 * d + 8, :] = jnp.concatenate([row, nothing], 1)
    group = lax.axis_index("mp")
    each = FEATS // nmp
    for k in range(nmp):
        start = pl.multiple_of((group ^ k) * each, 16)
        outs[k][...] = total[pl.ds(start, each), :].astype(BF)


def loss_row(value, count, lanes):
    a, b, c = three(value)
    lane = iota((1, lanes), 1)
    return jnp.where(lane == 0, a, jnp.where(lane == 1, b, jnp.where(lane == 2, c, jnp.where(lane == 3, count, 0.0))))


def merge_table_kernel(nmp, owners, own, high, *refs):
    terms = refs[:nmp]
    side, key_rows, preds, table_keep, table_send, table_sum, key_sum = refs[nmp:]
    odd = lax.axis_index("dp") & 1
    table_sum[...] = tree(terms)
    half = table_sum.shape[1] // 2
    query = jnp.concatenate([side[0:1, :], jnp.zeros((1, 128), F32)], 1)
    scal = loss_row(side[1:2, 0:1], side[1:2, 1:2], 384)
    r = iota((8, 384), 0)
    mols = preds.shape[0]
    spot = iota((mols, 384), 1) == iota((mols, 384), 0) + lax.axis_index("dp") * mols
    pred_high, pred_mid, _ = three(jnp.sum(jnp.where(spot, preds[:, 0:1], 0.0), 0, keepdims=True))
    scal = jnp.where(r == 0, query, jnp.where(r == 1, scal, jnp.where(r == 2, pred_high, jnp.where(r == 3, pred_mid, 0.0))))
    fill = jnp.zeros((8, 384 - own), F32)
    for p in range(2 * high):
        key_sum[p] = jnp.concatenate([key_rows[:, p * own : (p + 1) * own], fill], 1)
    for z in range(high):
        for out, x in ((table_keep, odd), (table_send, 1 - odd)):
            p = 2 * z + x
            if 2 * z < owners:
                each = table_sum[pl.ds(pl.multiple_of(p * 8, 8), 8), :]
            else:
                each = jnp.zeros((8, 2 * half), F32)
            out[z] = jnp.concatenate([each[:, 0:half], each[:, half:], key_sum[p], scal], 0).astype(BF)


def merge_kernel(layer_keep, layer_came, table_keep, table_came, *outs):
    deep = layer_keep.shape[1]
    mine = lax.axis_index("dp") >> 1
    r = iota((16, 384), 0)
    for k, out in enumerate(outs):
        z = mine ^ k
        out[0:deep, :] = (layer_keep[z].astype(F32) + layer_came[z].astype(F32)).astype(BF)
        out[deep : deep + 16, :] = (table_keep[z, 0:16].astype(F32) + table_came[z, 0:16].astype(F32)).astype(BF)
        both = table_keep[z, 16:32].astype(F32) + table_came[z, 16:32].astype(F32)
        loss = both[9:10, 0:1] + both[9:10, 1:2] + both[9:10, 2:3]
        out[deep + 16 :, :] = jnp.where(r == 9, loss_row(loss, both[9:10, 3:4], 384), both).astype(BF)


def ffn_all_kernel(keep, came, *outs):
    mine = lax.axis_index("dp") >> 1
    for k, out in enumerate(outs):
        out[...] = (keep[mine ^ k].astype(F32) + came[mine ^ k].astype(F32)).astype(BF)


def ffn_x_kernel(keep, came, near_keep, near_send, pair):
    me = lax.axis_index("dp")
    odd, side = me & 1, (me >> 1) & 1
    for out, s in ((near_keep, side), (near_send, 1 - side)):
        for h in range(2):
            for i in range(2):
                p = (2 * h + s) * 2 + i
                out[h, i * 48 : (i + 1) * 48, :] = (keep[p].astype(F32) + came[p].astype(F32)).astype(BF)
    last = keep.shape[0] - 1
    pair[odd] = keep[last]
    pair[1 - odd] = came[last]


def quad_kernel(pair, far, quad):
    for i in range(2):
        quad[i] = pair[i]
        quad[2 + i] = far[2 + i]


def ffn_z_kernel(keep, came, pair, far_keep, far_send):
    side = lax.axis_index("dp") >> 2
    each = far_send.shape[1]
    for i in range(2):
        rows = slice(i * each, (i + 1) * each)
        far_keep[i] = (keep[side, rows].astype(F32) + came[side, rows].astype(F32)).astype(BF)
        far_send[i] = (keep[1 - side, rows].astype(F32) + came[1 - side, rows].astype(F32)).astype(BF)
        far_send[2 + i] = pair[i]


def sum_squares(value):
    return jnp.sum(jnp.sum(value * value, 0, keepdims=True), 1, keepdims=True)


def outer_kernel(npiece, nkept, head_at, *refs):
    pieces, (preds, vectors), sources = refs[:npiece], refs[npiece : npiece + 2], refs[npiece + 2 : npiece + 2 + nkept]
    head_grad, square = refs[npiece + 2 + nkept : npiece + 4 + nkept]
    kept, (rows, low, sems) = refs[npiece + 4 + nkept : -3], refs[-3:]
    copies = [pltpu.make_async_copy(sources[i], kept[i], sems.at[i]) for i in range(nkept)]
    copies[head_at].start()
    for i, copy in enumerate(copies):
        if i != head_at:
            copy.start()
    slots = rows.shape[0]
    if npiece == 1:
        rows[...] = pieces[0][...]
        column = preds[:, 0:1]
    else:
        mine = lax.axis_index("dp") >> 1
        for k in range(4):
            for x in range(2):
                part = pieces[k & 1][(k & 2) + x].astype(F32)
                mols = part.shape[0] // 2
                part = jnp.concatenate([part[0:mols, :], part[mols:, :]], 1)
                part = jnp.concatenate([part, jnp.zeros((32 - mols, part.shape[1]), F32)], 0).astype(BF)
                rows[pl.ds(pl.multiple_of(((mine ^ k) * 2 + x) * 32, 16), 32), :] = part
        r = iota((slots, 384), 0)
        spot = (iota((slots, 384), 1) == r - (r >> 5) * (32 - mols)) & ((r & 31) < mols)
        column = jnp.sum(jnp.where(spot, preds[2:3, :] + preds[3:4, :], 0.0), -1, keepdims=True)
    copies[head_at].wait()
    low[...] = kept[head_at][...].astype(BF)
    mid = dot(rows[...], low[...]) + vectors[9:10, :]
    _, slope = gelu_pair(mid)
    readout = vectors[10:11, :].astype(BF).astype(F32)
    grad = dot(rows[...], (column * readout * slope).astype(BF), TN)
    head_grad[...] = grad
    square[...] = jnp.broadcast_to(sum_squares(grad), square.shape)
    for i, copy in enumerate(copies):
        if i != head_at:
            copy.wait()


def owner_kernel(own, cols, scale, dp, *refs):
    parts, ffn_parts, (query, vectors, layer, send, scalars, preds) = refs[: dp // 2], refs[dp // 2 : -6], refs[-6:]
    width = vectors.shape[1]
    summed = tree(parts)
    if ffn_parts[0].shape[0] == 2:
        near, far = ffn_parts
        ffn = jnp.concatenate([near[i].astype(F32) + far[i].astype(F32) for i in range(2)], 0)
    else:
        ffn = tree(ffn_parts)
    deep = ffn.shape[0]
    acc, summed = summed[0:deep, :], summed[deep:, :]
    table, keys, side = summed[0:16, :], summed[16:24, 0:128], summed[24:32, :]
    preds[...] = side
    key_grad = dot(keys, query[...], TN, HIGHEST) * scale
    hat, _ = norm_parts(vectors[8:9, :])
    start_row = (hat * vectors[0:1, :] + vectors[1:2, :]).astype(BF).astype(F32)
    here = iota((deep, width), 1) == iota((deep, width), 0) + lax.axis_index("dp") * own
    start_col = jnp.sum(jnp.where(here, start_row, 0.0), -1, keepdims=True)
    square = sum_squares(table)
    grads = [start_col * side[0:1, 0:256], key_grad, acc[:, 0:256], acc[:, 192:384], ffn[:, 0:256], ffn[:, 192:384]]
    for j, grad in enumerate(grads):
        grad = grad[0:own, 0:cols]
        layer[j] = grad
        square += sum_squares(grad)
    a, b, c = three(square)
    lane = iota((16, 384), 1)
    tail = jnp.where(lane == 0, a, jnp.where(lane == 1, b, jnp.where(lane == 2, c, 0.0)))
    packet = jnp.where(iota((16, 384), 0) == 15, tail, table).astype(BF)
    for p in range(send.shape[0]):
        send[p] = packet
    loss = side[1:2, 0:1] + side[1:2, 1:2] + side[1:2, 2:3]
    scalars[...] = jnp.where(iota(scalars.shape, 1) == 0, loss, side[1:2, 3:4])


def adam(weight, first, second, grad, rate):
    first_new = BETA_ONE * first + (1.0 - BETA_ONE) * grad
    second_new = BETA_TWO * second + (1.0 - BETA_TWO) * grad * grad
    fixed_one = 1.0 - BETA_ONE**STEP
    fixed_two = 1.0 - BETA_TWO**STEP
    scaled = second_new * (1.0 / fixed_two)
    root = scaled * lax.rsqrt(jnp.maximum(scaled, 1e-36))
    update = first_new * (1.0 / fixed_one) / (root + ADAM_EPS)
    return first_new, second_new, weight - rate * (update + WEIGHT_DECAY * weight)


def update_kernel(nmp, cols, *refs):
    arrived, refs = refs[:nmp], refs[nmp:]
    (
        head_square, scalars, layer, left_roots, right_roots, weights, left, right,
        tables, tables_m, tables_v, head, head_m, head_v, head_grad, vectors, vectors_m, vectors_v,
    ) = refs[:18]
    loss_out, count_out, norm_out = refs[18:21]
    outs = refs[21:34]
    held = refs[34:47]
    grads, vector_grads, packets, sems = refs[47:]
    layer_out, weights_out, left_out, right_out, tm_out, tv_out, t_out, hm_out, hv_out, h_out, vm_out, vv_out, v_out = held
    started = []

    def send(i, rows=None):
        src, dst = held[i], outs[i]
        if rows is not None:
            src, dst = src.at[rows], dst.at[rows]
        copy = pltpu.make_async_copy(src, dst, sems.at[len(started)])
        copy.start()
        started.append(copy)

    group = lax.axis_index("mp")
    for k in range(nmp):
        packets[group ^ k] = arrived[k][...]
    tails = jnp.zeros((16, 128), F32)
    for m in range(nmp):
        for p in range(packets.shape[1]):
            tails += packets[m, p, :, 0:128].astype(F32)
    square = head_square[0:1, 0:1] + tails[15:16, 0:1] + tails[15:16, 1:2] + tails[15:16, 2:3]
    loss, count = scalars[0:1, 0:1], scalars[0:1, 1:2]
    norm = jnp.sqrt(square) / count
    factor = CLIP / jnp.maximum(norm, CLIP) / count
    loss_out[...] = loss
    count_out[...] = count
    norm_out[...] = norm
    for j in range(6):
        layer_out[:, j * cols : (j + 1) * cols] = layer[j] * factor
    send(0)
    width = head.shape[0]
    parts = 8
    each = width // parts
    for i in range(parts):

        def some_rows(t, unused, i=i):
            rows = pl.ds(pl.multiple_of(i * each + t * 8, 8), 8)
            hm_out[rows, :], hv_out[rows, :], h_out[rows, :] = adam(
                head[rows, :], head_m[rows, :], head_v[rows, :], head_grad[rows, :] * factor, RATE_HEAD
            )
            return 0

        lax.fori_loop(0, each // 8, some_rows, 0, unroll=4)
        for k in (7, 8, 9):
            send(k, pl.ds(i * each, each))
    scale = (1.0 - STATS_DECAY) * factor * factor
    for j in range(6):
        low = layer[j].astype(BF)
        right_out[j] = STATS_DECAY * right[j] + scale * dot(low, low, TN)
        left_out[j] = STATS_DECAY * left[j] + scale * dot(low, low, NT)
    send(3)
    send(2)
    for j in range(6):
        span = slice(j * cols, (j + 1) * cols)
        low = layer[j].astype(BF)
        shaped = dot(dot(left_roots[j].astype(BF), low).astype(BF), right_roots[j].astype(BF))
        weights_out[:, span] = weights[:, span] - RATE_LAYER * (shaped * factor + WEIGHT_DECAY * weights[:, span])
    send(1)
    half = grads.shape[1] // 2
    high = FEATS // 8 // nmp
    for m in range(nmp):
        for p in range(high):
            piece = packets[m, p].astype(F32) * factor
            d = m * high + p
            grads[7 * d : 7 * d + 7, :] = jnp.concatenate([piece[0:7, :], piece[8:15, :]], 1)
            if d < 22:
                vector_grads[d // 2 : d // 2 + 1, d % 2 * half : (d % 2 + 1) * half] = piece[7:8, :]
    rows = tables.shape[0]

    def table_rows(t, unused):
        r = pl.ds(pl.multiple_of(t * 8, 8), 8)
        tm_out[r, :], tv_out[r, :], t_out[r, :] = adam(tables[r, :], tables_m[r, :], tables_v[r, :], grads[r, :], RATE_TABLES)
        return 0

    lax.fori_loop(0, rows // 8, table_rows, 0, unroll=4)
    for k in (4, 5, 6):
        send(k)
    nrows = vectors.shape[0]
    vm_out[...], vv_out[...], v_out[...] = adam(vectors[...], vectors_m[...], vectors_v[...], vector_grads[0:nrows, :], RATE_VECTORS)
    for k in (10, 11, 12):
        send(k)
    for copy in started:
        copy.wait()


def exchange(x, axis):
    n = lax.axis_size(axis)
    return [x] + [lax.ppermute(x, axis, [(i, i ^ k) for i in range(n)]) for k in range(1, n)]


def flip(x, k):
    n = lax.axis_size("dp")
    return lax.ppermute(x, "dp", [(i, i ^ k) for i in range(n)])


def after(values, *others):
    return lax.optimization_barrier((tuple(values), tuple(others)))[0]


def spread(x, second=()):
    four, one, two = flip(x, 4), flip(x, 1), flip(x, 2)
    (one,) = after([one], *second)
    (two,) = after([two], *second)
    (four,) = after([four], *second)
    return [x, one, two, flip(two, 1), four, flip(four, 1), flip(four, 2), flip(one, 6)]


def per_device(
    lap_vectors,
    eig_index,
    type_ids,
    seg_ids,
    targets,
    layer_weights,
    left_stats,
    right_stats,
    left_roots,
    right_roots,
    tables,
    tables_m,
    tables_v,
    head_weight,
    head_m,
    head_v,
    vectors,
    vectors_m,
    vectors_v,
):
    dp = lax.axis_size("dp")
    nmp = lax.axis_size("mp")
    length = seg_ids.shape[1]
    mols = targets.shape[1]
    width = vectors.shape[1]
    own, group_cols = layer_weights.shape[0], layer_weights.shape[1]
    cols = group_cols // 6
    heads = cols // HEAD_DIM
    scale = HEAD_DIM ** (-0.5)
    owners = FEATS // nmp // 8

    w = layer_weights.astype(BF)
    sources = [in_hbm(x) for x in (lap_vectors[0].T, eig_index[0].T, type_ids, seg_ids, tables, vectors)]
    at, normed, hats, invs = call(
        functools.partial(embed_kernel, mols),
        [sds((FEATS, length), BF), sds((length, width), BF), sds((length, width), BF), sds((length, 128), F32)],
        sources,
        [pltpu.VMEM(x.shape, x.dtype) for x in sources]
        + [pltpu.VMEM((FEATS, width), BF), pltpu.VMEM((FEATS, width), BF), pltpu.VMEM((8, length), I32), pltpu.SemaphoreType.DMA((6,))],
        flops=4 * length * FEATS * width,
        in_specs=[IN_PLACE] * 6,
    )
    direct = dp == 8 and own == 4 * mols and own % 16 == 0
    if direct:
        ones = spread(w, (normed,))
    else:
        ones = [lax.all_gather(w, "dp", axis=0, tiled=True)]
    np_ = len(ones)
    part, probs, values, ctx, keyed, query, w1, w2 = call(
        functools.partial(attn_kernel, np_, mols, heads, scale),
        [
            sds((mols, width), BF),
            sds((mols * heads, length), BF),
            sds((length, 256), BF),
            sds((mols, 256), BF),
            sds((width, 256), BF),
            sds((8, 256), F32),
            sds((width, 4 * cols), BF),
            sds((width, 2 * cols), BF),
        ],
        [normed, seg_ids, vectors, *ones],
        flops=4 * length * 256 * width,
    )
    part, resid_one, normed_two, hidden, act = call(
        functools.partial(ffn_kernel, nmp, cols),
        [
            sds((mols, width), BF),
            sds((mols, width), F32),
            sds((mols, width), BF),
            sds((mols, 256), F32),
            sds((mols, 256), BF),
        ],
        [*exchange(part, "mp"), vectors, w2],
        flops=4 * mols * width * 256,
    )
    part, pack, grad_pred, grad_two, grad_low, grad_hidden, head_rows = call(
        functools.partial(head_kernel, nmp, cols),
        [
            sds((mols, width), BF),
            sds((mols, width), BF),
            sds((mols, 128), F32),
            sds((mols, width), F32),
            sds((mols, width), BF),
            sds((mols, 256), BF),
            sds((8, width), F32),
        ],
        [*exchange(part, "mp"), resid_one, vectors, head_weight, targets, seg_ids, hidden, w2],
        [pltpu.VMEM((width, width), BF)],
        flops=4 * width * width * mols,
    )
    odd = lax.axis_index("dp") & 1
    high = dp // 2
    deep = (own + 15) // 16 * 16
    nlayer = 2 if own == deep else 1

    def halves(parts):
        if nlayer == 2:
            return parts
        both = parts[0].reshape(high, 2, own, -1)
        both = jnp.pad(both, ((0, 0), (0, 0), (0, deep - own), (0, 0)))
        return [lax.dynamic_index_in_dim(both, i, 1, False) for i in (odd, 1 - odd)]

    def half_shapes(lanes, number=1, more=0):
        return [sds((high * number + more, own // number, lanes), BF)] * 2 if nlayer == 2 else [sds((width, lanes), BF)]

    number = 2 if direct else 1
    parts = exchange(part, "mp")
    *ffn_parts, comb = call(
        functools.partial(ffn_grad_kernel, nlayer, high),
        half_shapes(384, number, number - 1) + [sds((256, width), BF)],
        [normed_two, grad_hidden, grad_low, act, pack, keyed],
        [pltpu.VMEM((width, 384), BF)],
        flops=4 * mols * width * 256,
    )
    ffn_keep, ffn_send = halves(ffn_parts)
    (ffn_send,) = after([ffn_send], *parts[1:])
    ffn_came = flip(ffn_send, 1)
    *layer_halves, side, key_rows, sides, extras = call(
        functools.partial(attn_back_kernel, nmp, nlayer, high, mols, heads, scale),
        half_shapes(384)
        + [sds((8, 256), F32), sds((8, width), F32), sds((256, length), BF), sds((16, width), F32)],
        [*parts, resid_one, grad_two, head_rows, vectors, probs, values, normed, w1, ctx],
        [pltpu.VMEM((width, 384), BF)],
        flops=4 * length * 256 * width,
    )
    layer_keep, layer_send = halves(layer_halves)
    layer_came = flip(layer_send, 1)
    shares = call(
        functools.partial(embed_back_kernel, nmp, mols),
        [sds((FEATS // nmp, width), BF) for _ in range(nmp)],
        [sides, comb, extras, vectors, hats, invs, at, seg_ids],
        [pltpu.VMEM((FEATS, width), F32), pltpu.VMEM((16, width), F32)],
        flops=4 * length * 256 * width,
    )
    moved = [shares[0]] + [lax.ppermute(shares[k], "mp", [(i, i ^ k) for i in range(nmp)]) for k in range(1, nmp)]
    table_keep, table_send = call(
        functools.partial(merge_table_kernel, nmp, owners, own, high),
        [sds((high, 32, 384), BF)] * 2,
        [*moved, side, key_rows, grad_pred],
        [pltpu.VMEM((FEATS // nmp, width), F32), pltpu.VMEM((dp, 8, 384), F32)],
    )
    (ffn_came,) = after([ffn_came], shares[0])
    if direct:
        near_keep, near_send, pair = call(
            ffn_x_kernel,
            [sds((2, own, 384), BF)] * 2 + [sds((2, 2 * mols, width // 2), BF)],
            [ffn_keep, ffn_came],
        )
        far_keep, far_send = call(
            ffn_z_kernel,
            [sds((2, own // 2, 384), BF), sds((4, own // 2, 384), BF)],
            [near_keep, flip(near_send, 2), pair],
        )
        ffn_parts = [far_keep, flip(far_send, 4)]
    else:
        ffn_parts = call(ffn_all_kernel, [sds((deep, 384), BF)] * high, [ffn_keep, ffn_came])
        ffn_parts = [ffn_parts[0]] + [flip(ffn_parts[k], 2 * k) for k in range(1, high)]
    merged = call(
        merge_kernel,
        [sds((deep + 32, 384), BF)] * high,
        [layer_keep, layer_came, table_keep, flip(table_send, 1)],
    )
    merged = [merged[0]] + [flip(merged[k], 2 * k) for k in range(1, high)]
    layer, send, scalars, preds = call(
        functools.partial(owner_kernel, own, cols, scale, dp),
        [sds((6, own, cols), F32), sds((dp, 16, 384), BF), sds((8, 128), F32), sds((8, 384), F32)],
        [*merged, *ffn_parts, query, vectors],
        flops=2 * own * 256 * 1024,
    )
    kept = [
        jnp.swapaxes(left_roots, 0, 1), right_roots[0], layer_weights, jnp.swapaxes(left_stats, 0, 1), right_stats[0],
        tables, tables_m, tables_v, head_weight, head_m, head_v, vectors, vectors_m, vectors_v,
    ]
    sums = lax.all_to_all(send, "dp", 0, 0, tiled=True)
    if direct:
        (far,) = after([ffn_parts[1]], scalars)
        (quad,) = call(quad_kernel, [sds((4, 2 * mols, 384), BF)], [pair, far])
        (came,) = after([flip(quad, 2)], sums)
        pieces = [quad, came]
    else:
        pieces = [jnp.pad(lax.all_gather(pack, "dp", axis=0), ((0, 0), (0, 32 - mols), (0, 0))).reshape(dp * 32, -1)]
        preds = jnp.pad(lax.all_gather(grad_pred, "dp", axis=0), ((0, 0), (0, 32 - mols), (0, 0))).reshape(dp * 32, -1)
    sums = exchange(sums, "mp")
    head_grad, head_square, *kept = call(
        functools.partial(outer_kernel, len(pieces), len(kept), 8),
        [sds((width, width), F32), sds((8, 128), F32)] + [pltpu.VMEM(x.shape, F32) for x in kept],
        [*pieces, preds, vectors, *[in_hbm(x) for x in kept]],
        [pltpu.VMEM((dp * 32, width), BF), pltpu.VMEM((width, width), BF), pltpu.SemaphoreType.DMA((len(kept),))],
        flops=4 * dp * mols * width * width,
        in_specs=[IN_VMEM] * (len(pieces) + 2) + [IN_PLACE] * len(kept),
        vmem=16 + dp // 4,
    )
    kept = [in_vmem(x) for x in kept]
    results = [
        sds((own, group_cols), F32),
        sds((own, group_cols), F32),
        sds((6, own, own), F32),
        sds((6, cols, cols), F32),
        *[sds(tables.shape, F32)] * 3,
        *[sds(head_weight.shape, F32)] * 3,
        *[sds(vectors.shape, F32)] * 3,
    ]
    outs = call(
        functools.partial(update_kernel, nmp, cols),
        [sds((1, 1), F32)] * 3 + results,
        [
            *sums, head_square, scalars, layer, *kept[:11], head_grad, *kept[11:],
        ],
        [pltpu.VMEM(x.shape, x.dtype) for x in results] + [pltpu.VMEM((FEATS, width), F32), pltpu.VMEM((16, width), F32), pltpu.VMEM((nmp, dp, 16, 384), BF), pltpu.SemaphoreType.DMA((34,))],
        flops=20 * width * width,
        vmem=24,
        out_specs=[IN_VMEM] * 3 + [IN_PLACE] * 13,
    )
    loss, count, norm, layer_grad, layer_new, left_new, right_new, tm, tv, tn, hm, hv, hn, vm, vv, vn = outs
    return (
        loss.reshape(()),
        count.reshape(()),
        norm.reshape(()),
        layer_grad,
        layer_new,
        jnp.swapaxes(left_new, 0, 1),
        right_new[None],
        tm,
        tv,
        tn,
        hm,
        hv,
        hn,
        vm,
        vv,
        vn,
    )


def solution(mesh):
    placed = (
        P("dp", None, None),
        P("dp", None, None),
        P("dp", None),
        P("dp", None),
        P("dp", None),
        P("dp", "mp"),
        P("dp", "mp", None),
        P("dp", "mp", None, None),
        P("dp", "mp", None),
        P("dp", "mp", None, None),
        *[P()] * 9,
    )
    return jax.shard_map(
        per_device,
        mesh=mesh,
        in_specs=placed,
        out_specs=(
            P(),
            P(),
            P(),
            P("dp", "mp"),
            P("dp", "mp"),
            P("dp", "mp", None),
            P("dp", "mp", None, None),
            *[P()] * 9,
        ),
        check_vma=False,
    )
```

```python
import functools
import math

import jax
import jax.numpy as jnp
from jax import lax
from jax.experimental import pallas as pl
from jax.experimental.pallas import tpu as pltpu
from jax.sharding import PartitionSpec as P

HEAD_DIM = 24
TYPES = 192
STEP = 10
NORM_EPS = 1e-05
CLIP = 0.25
STATS_DECAY = 0.95
RATE_LAYER = 0.15
RATE_TABLES = 0.15
RATE_HEAD = 0.01
RATE_VECTORS = 0.2
BETA_ONE = 0.9
BETA_TWO = 0.99
ADAM_EPS = 1e-08
WEIGHT_DECAY = 0.01
MASKED = -1000000000.0
GELU_C = 0.7978845608028654
GELU_A = 0.044715

BF = jnp.bfloat16
F32 = jnp.float32
I32 = jnp.int32
HIGHEST = lax.Precision.HIGHEST
NN = ((1,), (0,))
NT = ((1,), (1,))
TN = ((0,), (0,))
BLOCK = 256
FEATS = 256
MIB = 1024 * 1024


def dot(a, b, dims=NN, precision=None):
    return lax.dot_general(a, b, (dims, ((), ())), preferred_element_type=F32, precision=precision)


def iota(shape, dim):
    return lax.broadcasted_iota(I32, shape, dim)


IN_VMEM = pl.BlockSpec(memory_space=pltpu.VMEM)
IN_PLACE = pl.BlockSpec(memory_space=pltpu.HBM)


def call(kernel, outs, ins, scratch=(), flops=0, vmem=16, in_specs=None, out_specs=None):
    moved = sum(math.prod(x.shape) * x.dtype.itemsize for x in list(ins) + list(outs))
    return pl.pallas_call(
        kernel,
        out_shape=tuple(outs),
        in_specs=in_specs or [IN_VMEM] * len(ins),
        out_specs=tuple(out_specs or [IN_VMEM] * len(outs)),
        scratch_shapes=list(scratch),
        compiler_params=pltpu.CompilerParams(vmem_limit_bytes=vmem * MIB),
        cost_estimate=pl.CostEstimate(flops=flops, bytes_accessed=moved, transcendentals=0),
    )(*ins)


def in_hbm(x):
    return pltpu.with_memory_space_constraint(x, pltpu.HBM)


def in_vmem(x):
    return pltpu.with_memory_space_constraint(x, pltpu.VMEM)


def sds(shape, dtype):
    return jax.ShapeDtypeStruct(shape, dtype)


def norm_parts(values):
    center = values - jnp.mean(values, -1, keepdims=True)
    spread = jnp.mean(center * center, -1, keepdims=True)
    inverse = lax.rsqrt(spread + NORM_EPS)
    return center * inverse, inverse


def norm_back(grad, hat, inverse, gain):
    scaled = grad * gain
    mean_one = jnp.mean(scaled, -1, keepdims=True)
    mean_two = jnp.mean(scaled * hat, -1, keepdims=True)
    return inverse * (scaled - mean_one - hat * mean_two)


def gelu_pair(x):
    t = jnp.tanh(GELU_C * (x + GELU_A * x * x * x))
    value = 0.5 * x * (1.0 + t)
    slope = 0.5 * (1.0 + t) + 0.5 * x * (1.0 - t * t) * (GELU_C * (1.0 + 3.0 * GELU_A * x * x))
    return value, slope


def tree(refs):
    parts = [r[...].astype(F32) for r in refs]
    while len(parts) > 1:
        parts = [parts[i] + parts[i + 1] for i in range(0, len(parts), 2)]
    return parts[0]


def three(x):
    high = x.astype(BF).astype(F32)
    mid = (x - high).astype(BF).astype(F32)
    return high, mid, x - high - mid


def assemble(pieces, first, second, owner):
    rows = pieces[0].shape[0]
    split = first.shape[1]
    for k, piece in enumerate(pieces):
        here = pl.ds(0 if len(pieces) == 1 else pl.multiple_of((owner ^ k) * rows, 16), rows)
        first[here, :] = piece[:, 0:split]
        second[here, :] = piece[:, split:]


def spaced(t):
    return t + ((t * 9363) >> 16)


def embed_kernel(mols, *refs):
    sources, (at, normed, hats, invs), held, (high, low, prev, sems) = refs[:6], refs[6:10], refs[10:16], refs[16:]
    copies = [pltpu.make_async_copy(a, b, sems.at[i]) for i, (a, b) in enumerate(zip(sources, held))]
    for copy in copies:
        copy.start()
    normed[...] = jnp.zeros(normed.shape, BF)
    for copy in copies:
        copy.wait()
    lap, eig, kinds, seg, tables, vectors = held
    length = seg.shape[1]
    width = vectors.shape[1]
    rows = tables.shape[0]
    tab = tables[...]
    tab_high = tab.astype(BF)
    rest = jnp.where(iota(tab.shape, 0) < TYPES, tab - tab_high.astype(F32), 0.0).astype(BF)
    place = (iota((FEATS, rows), 0) == spaced(iota((FEATS, rows), 1))).astype(F32).astype(BF)
    r = iota((32, width), 0)
    extra = jnp.where(r == 7, vectors[6:7, :], jnp.where(r == 15, vectors[7:8, :], jnp.where(r == 23, vectors[8:9, :], 0.0)))
    extra_high = extra.astype(BF)
    placed = dot(place, tab_high)
    high[0:32, :] = (placed[0:32, :] + extra_high.astype(F32)).astype(BF)
    high[32:, :] = placed[32:, :].astype(BF)
    placed = dot(place, rest)
    low[0:32, :] = (placed[0:32, :] + extra - extra_high.astype(F32)).astype(BF)
    low[32:, :] = placed[32:, :].astype(BF)
    place = place[:, TYPES:]
    seg_row = seg[...]
    before = pltpu.roll(jnp.broadcast_to(seg_row, (8, length)), 1, 1)
    before = jnp.where(iota((8, length), 1) == 0, -1, before)
    prev[...] = before
    filled = jnp.sum((seg_row != mols).astype(F32)).astype(I32)
    gain = vectors[0:1, :]
    shift = vectors[1:2, :]
    window = 2 * BLOCK

    def one_block(b, unused):
        start = pl.multiple_of(b * BLOCK, BLOCK)
        here = pl.ds(start, BLOCK)
        first = pl.multiple_of(jnp.clip(start - 128, 0, length - window), 128)
        source = iota((window, BLOCK), 0) + first
        one = eig[0:1, here]
        two = eig[1:2, here]
        near = lap[:, pl.ds(first, window)].astype(BF)
        pair_one = dot(near, (source == one).astype(F32).astype(BF))
        pair_two = dot(near, (source == two).astype(F32).astype(BF))
        seg_here = seg[0:1, here]
        begins = (seg_here != mols) & (seg_here != prev[0:1, here])
        kind = jnp.where(begins, -1, spaced(kinds[0:1, here]))
        keep = jnp.where(begins, 0.0, 1.0)
        which = jnp.where(begins, 23, jnp.where(one == two, 7, 15))
        pair = (jnp.concatenate([pair_one, pair_two], 0) * keep).astype(BF)
        spot = iota((FEATS, BLOCK), 0)
        at[:, here] = (((spot == kind) | (spot == which)).astype(F32) + dot(place, pair)).astype(BF)
        picks = at[:, here]
        resid = dot(picks, high[...], TN) + dot(picks, low[...], TN)
        hat, inverse = norm_parts(resid)
        normed[here, :] = (hat * gain + shift).astype(BF)
        hats[here, :] = hat.astype(BF)
        invs[here, :] = jnp.broadcast_to(inverse, (BLOCK, 128))
        return 0

    lax.fori_loop(0, (filled + BLOCK - 1) // BLOCK, one_block, 0)


def attn_kernel(npiece, mols, heads, scale, *refs):
    normed, seg, vectors = refs[:3]
    ones = refs[3 : 3 + npiece]
    part, probs, values, ctx_out, keyed, query_out, w1, w2 = refs[3 + npiece :]
    assemble(ones, w1, w2, lax.axis_index("dp"))
    width = vectors.shape[1]
    cols = heads * HEAD_DIM
    hat, _ = norm_parts(vectors[8:9, :])
    start_row = (hat * vectors[0:1, :] + vectors[1:2, :]).astype(BF)
    q = dot(jnp.broadcast_to(start_row, (16, width)), w1[:, 0:256])
    q = q.astype(BF).astype(F32)
    q = jnp.where(iota((16, 256), 1) < cols, q, 0.0)
    r = iota((16, 256), 0)
    head_of = iota((16, 256), 1) // HEAD_DIM
    query_out[...] = jnp.where(r == head_of, q, 0.0)[0:8, :]
    shifted = pltpu.roll(q, 64, 1)[0:1, :]
    r = iota((128, 256), 0)
    lane = iota((128, 256), 1) - 64
    pick = (lane >= 0) & ((r & 7) == lane // HEAD_DIM) & (r >= 64) & (r < 80)
    q_keys = jnp.where(pick, shifted, 0.0).astype(BF)
    u = dot(w1[:, 128:384], q_keys, NT)
    u_high = u.astype(BF)
    lane = iota(u.shape, 1)
    u_both = jnp.where(lane < 72, u_high.astype(F32), u - u_high.astype(F32))
    last = w1[:, 512:640].astype(F32)
    side = jnp.where(lane < 64, last, u_both).astype(BF)
    keyed[:, 0:128] = w1[:, 384:512]
    keyed[:, 128:256] = jnp.where(lane < 64, last, jnp.where(lane < 72, u * scale, 0.0)).astype(BF)
    normed_all = normed[...]
    values[:, 0:128] = dot(normed_all, w1[:, 384:512]).astype(BF)
    second = dot(normed_all, side)
    values[:, 128:256] = jnp.where(iota(second.shape, 1) < 64, second, 0.0).astype(BF)
    turned = second.T
    scores = (turned[64:72, :] + turned[72:80, :]) * scale
    seg_row = seg[...]
    length = seg_row.shape[1]
    mine = iota((mols, 1, length), 0) == seg_row[None]
    masked = jnp.where(mine, scores[None], MASKED)
    peak = jnp.max(masked, -1, keepdims=True)
    grown = jnp.exp(masked - peak)
    total = jnp.sum(grown, -1, keepdims=True)
    prob = (grown * (1.0 / total)).reshape(mols * heads, length).astype(BF)
    probs[...] = prob
    wide = dot(prob, values[...])
    r = iota(wide.shape, 0) & (heads - 1)
    wide = jnp.where(r == iota(wide.shape, 1) // HEAD_DIM, wide, 0.0)
    ctx = jnp.sum(wide.reshape(mols, heads, 256), 1)
    ctx_out[...] = ctx.astype(BF)
    turned_ctx = pltpu.roll(ctx, 64, 1).astype(BF)
    part[...] = dot(turned_ctx, w1[:, 512:768], NT).astype(BF)


def ffn_kernel(nmp, cols, *refs):
    terms = refs[:nmp]
    vectors, w2, part, resid_out, normed_out, hidden_out, act_out = refs[nmp:]
    resid = vectors[8:9, :] + tree(terms)
    resid_out[...] = resid
    hat, _ = norm_parts(resid)
    low = (hat * vectors[2:3, :] + vectors[3:4, :]).astype(BF)
    normed_out[...] = low
    hidden = dot(low, w2[:, 0:256])
    hidden = jnp.where(iota(hidden.shape, 1) < cols, hidden, 0.0)
    hidden_out[...] = hidden
    act, _ = gelu_pair(hidden)
    act_out[...] = act.astype(BF)
    turned = pltpu.roll(act, 64, 1).astype(BF)
    part[...] = dot(turned, w2[:, 128:384], NT).astype(BF)


def head_kernel(nmp, cols, *refs):
    terms = refs[:nmp]
    resid_one, vectors, head, targets, seg, hidden, w2 = refs[nmp : nmp + 7]
    part, pack, pred_out, grad_out, low_out, hidden_out, rows_out, head_low = refs[nmp + 7 :]
    width = vectors.shape[1]
    mols = targets.shape[1]
    head_low[...] = head[...].astype(BF)
    resid = resid_one[...] + tree(terms)
    hat, inverse = norm_parts(resid)
    gain = vectors[4:5, :]
    low = (hat * gain + vectors[5:6, :]).astype(BF)
    mid = dot(low, head_low[...]) + vectors[9:10, :]
    act_head, slope = gelu_pair(mid)
    act_head = act_head.astype(BF).astype(F32)
    readout = vectors[10:11, :].astype(BF).astype(F32)
    predicted = jnp.sum(act_head * readout, -1, keepdims=True)
    spot = iota((mols, mols), 0) == iota((mols, mols), 1)
    goal = jnp.sum(jnp.where(spot, targets[...], 0.0), -1, keepdims=True)
    seg_row = seg[...]
    there = iota((mols, seg_row.shape[1]), 0) == seg_row
    present = jnp.max(there.astype(F32), -1, keepdims=True)
    error = predicted - goal
    root = jnp.sqrt(error * error + 1.0)
    loss = jnp.sum(present * (root - 1.0), 0, keepdims=True)
    count = jnp.sum(present, 0, keepdims=True)
    grad_pred = present * error / root
    grad_readout = jnp.sum(grad_pred * act_head, 0, keepdims=True)
    grad_mid = (grad_pred * readout * slope).astype(BF)
    grad_bias = jnp.sum(grad_mid.astype(F32), 0, keepdims=True)
    grad_rows = dot(grad_mid, head_low[...], NT)
    grad_gain = jnp.sum(grad_rows * hat, 0, keepdims=True)
    grad_shift = jnp.sum(grad_rows, 0, keepdims=True)
    grad_two = norm_back(grad_rows, hat, inverse, gain)
    grad_out[...] = grad_two
    grad_low = grad_two.astype(BF)
    grad_act = dot(grad_low, w2[:, 128:384])
    grad_act = pltpu.roll(grad_act, 192, 1)
    _, slope_hidden = gelu_pair(hidden[...])
    grad_hidden = jnp.where(iota(grad_act.shape, 1) < cols, grad_act * slope_hidden, 0.0).astype(BF)
    part[...] = dot(grad_hidden, w2[:, 0:256], NT).astype(BF)
    pack[...] = low
    pred_out[...] = jnp.broadcast_to(grad_pred, pred_out.shape)
    low_out[...] = grad_low
    hidden_out[...] = grad_hidden
    r = iota((8, width), 0)
    lane = iota((8, width), 1)
    scalars = jnp.where(lane == 0, loss, jnp.where(lane == 1, count, 0.0))
    rows_out[...] = jnp.where(
        r == 0,
        grad_gain,
        jnp.where(r == 1, grad_shift, jnp.where(r == 2, grad_bias, jnp.where(r == 3, grad_readout, jnp.where(r == 4, scalars, 0.0)))),
    )


def parts_for(rows, keep, send, each, odd, high, number=1):
    for z in range(high):
        for i in range(number):
            keep[z * number + i] = rows[pl.ds(pl.multiple_of(((2 * z + odd) * number + i) * each, 16), each), :]
            send[z * number + i] = rows[pl.ds(pl.multiple_of(((2 * z + 1 - odd) * number + i) * each, 16), each), :]


def ffn_grad_kernel(nlayer, high, normed, grad_hidden, grad_low, act, pack, keyed, *refs):
    outs, (comb, rows) = refs[:nlayer], refs[nlayer:]
    comb[...] = keyed[...].astype(F32).T.astype(BF)
    up = dot(normed[...], grad_hidden[...], TN)
    turned = pltpu.roll(act[...].astype(F32), 64, 1).astype(BF)
    down = dot(grad_low[...], turned, TN)
    target = rows if nlayer == 2 else outs[0]
    target[:, 0:128] = up[:, 0:128].astype(BF)
    target[:, 128:256] = (up[:, 128:256] + down[:, 0:128]).astype(BF)
    target[:, 256:384] = down[:, 128:256].astype(BF)
    if nlayer == 2:
        half = outs[0].shape[1]
        parts_for(rows, *outs, half, lax.axis_index("dp") & 1, high, 2)
        if outs[0].shape[0] > 2 * high:
            lanes = pack[...].astype(F32)
            lanes = jnp.concatenate([lanes[:, 0:384], lanes[:, 384:768]], 0).astype(BF)
            outs[0][2 * high] = lanes
            outs[1][2 * high] = lanes


def attn_back_kernel(nmp, nlayer, high, mols, heads, scale, *refs):
    terms = refs[:nmp]
    resid_one, grad_two, head_rows, vectors, probs, values, normed, w1, ctx = refs[nmp : nmp + 9]
    layer_outs = refs[nmp + 9 : nmp + 9 + nlayer]
    side, key_rows, sides, extras, turned_lay = refs[nmp + 9 + nlayer :]
    group = lax.axis_index("mp")
    width = vectors.shape[1]
    length = probs.shape[1]
    cols = heads * HEAD_DIM
    grad_normed = tree(terms)
    hat, inverse = norm_parts(resid_one[...])
    grad_gain = jnp.sum(grad_normed * hat, 0, keepdims=True)
    grad_shift = jnp.sum(grad_normed, 0, keepdims=True)
    grad_one = grad_two[...] + norm_back(grad_normed, hat, inverse, vectors[2:3, :])
    low = grad_one.astype(BF)
    grad_start = jnp.sum(low.astype(F32), 0, keepdims=True)
    grad_ctx = pltpu.roll(dot(low, w1[:, 512:768]), 192, 1).astype(BF).astype(F32)
    spread_ctx = jnp.broadcast_to(grad_ctx[:, None, :], (mols, heads, 256)).reshape(mols * heads, 256)
    r = iota(spread_ctx.shape, 0) & (heads - 1)
    spread_ctx = jnp.where(r == iota(spread_ctx.shape, 1) // HEAD_DIM, spread_ctx, 0.0).astype(BF)
    grad_probs = dot(spread_ctx, values[...], NT)
    prob = probs[...].astype(F32)
    inner = jnp.sum(prob * grad_probs, -1, keepdims=True)
    grad_scores = (prob * (grad_probs - inner)).astype(BF).astype(F32)
    grad_scores = jnp.sum(grad_scores.reshape(mols, heads, length), 0)
    grad_values = dot(spread_ctx, probs[...], TN)
    sides[0:cols, :] = grad_values[0:cols, :].astype(BF)
    sides[cols:256, :] = jnp.concatenate([grad_scores, jnp.zeros((256 - cols - heads, length), F32)], 0).astype(BF)
    sums = dot(sides[...], normed[...])
    turned_ctx = pltpu.roll(ctx[...].astype(F32), 64, 1).astype(BF)
    out_grad = dot(low, turned_ctx, TN)
    r = iota(sums.shape, 0)
    value_grad = jnp.where(r < cols, sums, 0.0).T
    lay = layer_outs[0] if nlayer == 1 else turned_lay
    lay[:, 0:128] = value_grad[:, 0:128].astype(BF)
    lay[:, 128:256] = (value_grad[:, 128:256] + out_grad[:, 0:128]).astype(BF)
    lay[:, 256:384] = out_grad[:, 128:256].astype(BF)
    if nlayer == 2:
        parts_for(lay, *layer_outs, layer_outs[0].shape[1], lax.axis_index("dp") & 1, high)
    gain = vectors[0:1, :]
    grad_keys = sums[cols : cols + heads, :]
    key_rows[...] = grad_keys
    turned = dot(grad_keys.astype(BF), w1[:, 128:384])
    lane = iota(turned.shape, 1) - 64
    picked = jnp.where((lane >= 0) & (lane // HEAD_DIM == iota(turned.shape, 0)), turned, 0.0)
    grad_query = jnp.sum(pltpu.roll(picked, 192, 1), 0, keepdims=True) * scale
    r = iota(side.shape, 0)
    side[...] = jnp.where(r == 0, grad_query, jnp.where(r == 1, head_rows[4:5, 0:256], 0.0))
    grad_query = jnp.broadcast_to(grad_query.astype(BF), (16, 256))
    grad_row = dot(grad_query, w1[:, 0:256], NT)[0:1, :]
    hat_start, inverse_start = norm_parts(vectors[8:9, :])
    first = jnp.where(group == 0, 1.0, 0.0)
    row_graph = norm_back(grad_row, hat_start, inverse_start, gain) + first * grad_start
    r = iota(extras.shape, 0)
    extra = jnp.where(r == 0, grad_row * hat_start, 0.0)
    extra = jnp.where(r == 1, grad_row, extra)
    extra = jnp.where(r == 2, first * grad_gain, extra)
    extra = jnp.where(r == 3, first * grad_shift, extra)
    extra = jnp.where(r == 8, row_graph, extra)
    for i, o in enumerate((4, 5, 9, 10)):
        extra = jnp.where(r == o, first * head_rows[i : i + 1, :], extra)
    extras[...] = extra


def embed_back_kernel(nmp, mols, *refs):
    sides, comb, extras, vectors, hats, invs, at, seg = refs[:8]
    outs, (total, gains) = refs[8 : 8 + nmp], refs[8 + nmp :]
    width = vectors.shape[1]
    filled = jnp.sum((seg[...] != mols).astype(F32)).astype(I32)
    total[...] = jnp.zeros(total.shape, F32)
    gains[...] = jnp.zeros(gains.shape, F32)
    gain = vectors[0:1, :]

    def one_block(b, unused):
        here = pl.ds(pl.multiple_of(b * BLOCK, BLOCK), BLOCK)
        grad = dot(sides[:, here], comb[...], TN)
        hat_here = hats[here, :].astype(F32)
        low_grad = norm_back(grad, hat_here, invs[here, 0:1], gain).astype(BF)
        total[...] += dot(at[:, here], low_grad)
        gains[0:8, :] += jnp.sum((grad * hat_here).reshape(BLOCK // 8, 8, width), 0)
        gains[8:16, :] += jnp.sum(grad.reshape(BLOCK // 8, 8, width), 0)
        return 0

    lax.fori_loop(0, (filled + BLOCK - 1) // BLOCK, one_block, 0)
    r = iota(extras.shape, 0)
    extra = extras[...] + jnp.where(r == 0, jnp.sum(gains[0:8, :], 0, keepdims=True), 0.0)
    extra += jnp.where(r == 1, jnp.sum(gains[8:16, :], 0, keepdims=True), 0.0)
    for i in range(3):
        extra += jnp.where(r == 6 + i, total[8 * i + 7 : 8 * i + 8, :], 0.0)
    half = width // 2
    nothing = jnp.zeros((1, half), F32)
    for d in range(FEATS // 8):
        row = extra[d // 2 : d // 2 + 1, d % 2 * half : (d % 2 + 1) * half] if d < 22 else nothing
        total[8 * d + 7 : 8 * d + 8, :] = jnp.concatenate([row, nothing], 1)
    group = lax.axis_index("mp")
    each = FEATS // nmp
    for k in range(nmp):
        start = pl.multiple_of((group ^ k) * each, 16)
        outs[k][...] = total[pl.ds(start, each), :].astype(BF)


def loss_row(value, count, lanes):
    a, b, c = three(value)
    lane = iota((1, lanes), 1)
    return jnp.where(lane == 0, a, jnp.where(lane == 1, b, jnp.where(lane == 2, c, jnp.where(lane == 3, count, 0.0))))


def merge_table_kernel(nmp, owners, own, high, *refs):
    terms = refs[:nmp]
    side, key_rows, preds, table_keep, table_send, table_sum, key_sum = refs[nmp:]
    odd = lax.axis_index("dp") & 1
    table_sum[...] = tree(terms)
    half = table_sum.shape[1] // 2
    query = jnp.concatenate([side[0:1, :], jnp.zeros((1, 128), F32)], 1)
    scal = loss_row(side[1:2, 0:1], side[1:2, 1:2], 384)
    r = iota((8, 384), 0)
    mols = preds.shape[0]
    spot = iota((mols, 384), 1) == iota((mols, 384), 0) + lax.axis_index("dp") * mols
    pred_high, pred_mid, _ = three(jnp.sum(jnp.where(spot, preds[:, 0:1], 0.0), 0, keepdims=True))
    scal = jnp.where(r == 0, query, jnp.where(r == 1, scal, jnp.where(r == 2, pred_high, jnp.where(r == 3, pred_mid, 0.0))))
    fill = jnp.zeros((8, 384 - own), F32)
    for p in range(2 * high):
        key_sum[p] = jnp.concatenate([key_rows[:, p * own : (p + 1) * own], fill], 1)
    for z in range(high):
        for out, x in ((table_keep, odd), (table_send, 1 - odd)):
            p = 2 * z + x
            if 2 * z < owners:
                each = table_sum[pl.ds(pl.multiple_of(p * 8, 8), 8), :]
            else:
                each = jnp.zeros((8, 2 * half), F32)
            out[z] = jnp.concatenate([each[:, 0:half], each[:, half:], key_sum[p], scal], 0).astype(BF)


def merge_kernel(layer_keep, layer_came, table_keep, table_came, *outs):
    deep = layer_keep.shape[1]
    mine = lax.axis_index("dp") >> 1
    r = iota((16, 384), 0)
    for k, out in enumerate(outs):
        z = mine ^ k
        out[0:deep, :] = (layer_keep[z].astype(F32) + layer_came[z].astype(F32)).astype(BF)
        out[deep : deep + 16, :] = (table_keep[z, 0:16].astype(F32) + table_came[z, 0:16].astype(F32)).astype(BF)
        both = table_keep[z, 16:32].astype(F32) + table_came[z, 16:32].astype(F32)
        loss = both[9:10, 0:1] + both[9:10, 1:2] + both[9:10, 2:3]
        out[deep + 16 :, :] = jnp.where(r == 9, loss_row(loss, both[9:10, 3:4], 384), both).astype(BF)


def ffn_all_kernel(keep, came, *outs):
    mine = lax.axis_index("dp") >> 1
    for k, out in enumerate(outs):
        out[...] = (keep[mine ^ k].astype(F32) + came[mine ^ k].astype(F32)).astype(BF)


def ffn_x_kernel(keep, came, near_keep, near_send, pair):
    me = lax.axis_index("dp")
    odd, side = me & 1, (me >> 1) & 1
    for out, s in ((near_keep, side), (near_send, 1 - side)):
        for h in range(2):
            for i in range(2):
                p = (2 * h + s) * 2 + i
                out[h, i * 48 : (i + 1) * 48, :] = (keep[p].astype(F32) + came[p].astype(F32)).astype(BF)
    last = keep.shape[0] - 1
    pair[odd] = keep[last]
    pair[1 - odd] = came[last]


def quad_kernel(pair, far, quad):
    for i in range(2):
        quad[i] = pair[i]
        quad[2 + i] = far[2 + i]


def ffn_z_kernel(keep, came, pair, far_keep, far_send):
    side = lax.axis_index("dp") >> 2
    each = far_send.shape[1]
    for i in range(2):
        rows = slice(i * each, (i + 1) * each)
        far_keep[i] = (keep[side, rows].astype(F32) + came[side, rows].astype(F32)).astype(BF)
        far_send[i] = (keep[1 - side, rows].astype(F32) + came[1 - side, rows].astype(F32)).astype(BF)
        far_send[2 + i] = pair[i]


def sum_squares(value):
    return jnp.sum(jnp.sum(value * value, 0, keepdims=True), 1, keepdims=True)


def outer_kernel(npiece, nkept, head_at, *refs):
    pieces, (preds, vectors), sources = refs[:npiece], refs[npiece : npiece + 2], refs[npiece + 2 : npiece + 2 + nkept]
    head_grad, square = refs[npiece + 2 + nkept : npiece + 4 + nkept]
    kept, (rows, low, sems) = refs[npiece + 4 + nkept : -3], refs[-3:]
    copies = [pltpu.make_async_copy(sources[i], kept[i], sems.at[i]) for i in range(nkept)]
    copies[head_at].start()
    for i, copy in enumerate(copies):
        if i != head_at:
            copy.start()
    slots = rows.shape[0]
    if npiece == 1:
        rows[...] = pieces[0][...]
        column = preds[:, 0:1]
    else:
        mine = lax.axis_index("dp") >> 1
        for k in range(4):
            for x in range(2):
                part = pieces[k & 1][(k & 2) + x].astype(F32)
                mols = part.shape[0] // 2
                part = jnp.concatenate([part[0:mols, :], part[mols:, :]], 1)
                part = jnp.concatenate([part, jnp.zeros((32 - mols, part.shape[1]), F32)], 0).astype(BF)
                rows[pl.ds(pl.multiple_of(((mine ^ k) * 2 + x) * 32, 16), 32), :] = part
        r = iota((slots, 384), 0)
        spot = (iota((slots, 384), 1) == r - (r >> 5) * (32 - mols)) & ((r & 31) < mols)
        column = jnp.sum(jnp.where(spot, preds[2:3, :] + preds[3:4, :], 0.0), -1, keepdims=True)
    copies[head_at].wait()
    low[...] = kept[head_at][...].astype(BF)
    mid = dot(rows[...], low[...]) + vectors[9:10, :]
    _, slope = gelu_pair(mid)
    readout = vectors[10:11, :].astype(BF).astype(F32)
    grad = dot(rows[...], (column * readout * slope).astype(BF), TN)
    head_grad[...] = grad
    square[...] = jnp.broadcast_to(sum_squares(grad), square.shape)
    for i, copy in enumerate(copies):
        if i != head_at:
            copy.wait()


def owner_kernel(own, cols, scale, dp, *refs):
    parts, ffn_parts, (query, vectors, layer, send, scalars, preds) = refs[: dp // 2], refs[dp // 2 : -6], refs[-6:]
    width = vectors.shape[1]
    summed = tree(parts)
    if ffn_parts[0].shape[0] == 2:
        near, far = ffn_parts
        ffn = jnp.concatenate([near[i].astype(F32) + far[i].astype(F32) for i in range(2)], 0)
    else:
        ffn = tree(ffn_parts)
    deep = ffn.shape[0]
    acc, summed = summed[0:deep, :], summed[deep:, :]
    table, keys, side = summed[0:16, :], summed[16:24, 0:128], summed[24:32, :]
    preds[...] = side
    key_grad = dot(keys, query[...], TN, HIGHEST) * scale
    hat, _ = norm_parts(vectors[8:9, :])
    start_row = (hat * vectors[0:1, :] + vectors[1:2, :]).astype(BF).astype(F32)
    here = iota((deep, width), 1) == iota((deep, width), 0) + lax.axis_index("dp") * own
    start_col = jnp.sum(jnp.where(here, start_row, 0.0), -1, keepdims=True)
    square = sum_squares(table)
    grads = [start_col * side[0:1, 0:256], key_grad, acc[:, 0:256], acc[:, 192:384], ffn[:, 0:256], ffn[:, 192:384]]
    for j, grad in enumerate(grads):
        grad = grad[0:own, 0:cols]
        layer[j] = grad
        square += sum_squares(grad)
    a, b, c = three(square)
    lane = iota((16, 384), 1)
    tail = jnp.where(lane == 0, a, jnp.where(lane == 1, b, jnp.where(lane == 2, c, 0.0)))
    packet = jnp.where(iota((16, 384), 0) == 15, tail, table).astype(BF)
    for p in range(send.shape[0]):
        send[p] = packet
    loss = side[1:2, 0:1] + side[1:2, 1:2] + side[1:2, 2:3]
    scalars[...] = jnp.where(iota(scalars.shape, 1) == 0, loss, side[1:2, 3:4])


def adam(weight, first, second, grad, rate):
    first_new = BETA_ONE * first + (1.0 - BETA_ONE) * grad
    second_new = BETA_TWO * second + (1.0 - BETA_TWO) * grad * grad
    fixed_one = 1.0 - BETA_ONE**STEP
    fixed_two = 1.0 - BETA_TWO**STEP
    scaled = second_new * (1.0 / fixed_two)
    root = scaled * lax.rsqrt(jnp.maximum(scaled, 1e-36))
    update = first_new * (1.0 / fixed_one) / (root + ADAM_EPS)
    return first_new, second_new, weight - rate * (update + WEIGHT_DECAY * weight)


def update_kernel(nmp, cols, *refs):
    arrived, refs = refs[:nmp], refs[nmp:]
    (
        head_square, scalars, layer, left_roots, right_roots, weights, left, right,
        tables, tables_m, tables_v, head, head_m, head_v, head_grad, vectors, vectors_m, vectors_v,
    ) = refs[:18]
    loss_out, count_out, norm_out = refs[18:21]
    outs = refs[21:34]
    held = refs[34:47]
    grads, vector_grads, packets, sems = refs[47:]
    layer_out, weights_out, left_out, right_out, tm_out, tv_out, t_out, hm_out, hv_out, h_out, vm_out, vv_out, v_out = held
    started = []

    def send(i, rows=None):
        src, dst = held[i], outs[i]
        if rows is not None:
            src, dst = src.at[rows], dst.at[rows]
        copy = pltpu.make_async_copy(src, dst, sems.at[len(started)])
        copy.start()
        started.append(copy)

    group = lax.axis_index("mp")
    for k in range(nmp):
        packets[group ^ k] = arrived[k][...]
    tails = jnp.zeros((16, 128), F32)
    for m in range(nmp):
        for p in range(packets.shape[1]):
            tails += packets[m, p, :, 0:128].astype(F32)
    square = head_square[0:1, 0:1] + tails[15:16, 0:1] + tails[15:16, 1:2] + tails[15:16, 2:3]
    loss, count = scalars[0:1, 0:1], scalars[0:1, 1:2]
    norm = jnp.sqrt(square) / count
    factor = CLIP / jnp.maximum(norm, CLIP) / count
    loss_out[...] = loss
    count_out[...] = count
    norm_out[...] = norm
    for j in range(6):
        layer_out[:, j * cols : (j + 1) * cols] = layer[j] * factor
    send(0)
    width = head.shape[0]
    parts = 8
    each = width // parts
    for i in range(parts):

        def some_rows(t, unused, i=i):
            rows = pl.ds(pl.multiple_of(i * each + t * 8, 8), 8)
            hm_out[rows, :], hv_out[rows, :], h_out[rows, :] = adam(
                head[rows, :], head_m[rows, :], head_v[rows, :], head_grad[rows, :] * factor, RATE_HEAD
            )
            return 0

        lax.fori_loop(0, each // 8, some_rows, 0, unroll=12)
        for k in (7, 8, 9):
            send(k, pl.ds(i * each, each))
    scale = (1.0 - STATS_DECAY) * factor * factor
    for j in range(6):
        low = layer[j].astype(BF)
        right_out[j] = STATS_DECAY * right[j] + scale * dot(low, low, TN)
        left_out[j] = STATS_DECAY * left[j] + scale * dot(low, low, NT)
    send(3)
    send(2)
    for j in range(6):
        span = slice(j * cols, (j + 1) * cols)
        low = layer[j].astype(BF)
        shaped = dot(dot(left_roots[j].astype(BF), low).astype(BF), right_roots[j].astype(BF))
        weights_out[:, span] = weights[:, span] - RATE_LAYER * (shaped * factor + WEIGHT_DECAY * weights[:, span])
    send(1)
    half = grads.shape[1] // 2
    high = FEATS // 8 // nmp
    for m in range(nmp):
        for p in range(high):
            piece = packets[m, p].astype(F32) * factor
            d = m * high + p
            grads[7 * d : 7 * d + 7, :] = jnp.concatenate([piece[0:7, :], piece[8:15, :]], 1)
            if d < 22:
                vector_grads[d // 2 : d // 2 + 1, d % 2 * half : (d % 2 + 1) * half] = piece[7:8, :]
    rows = tables.shape[0]

    def table_rows(t, unused):
        r = pl.ds(pl.multiple_of(t * 8, 8), 8)
        tm_out[r, :], tv_out[r, :], t_out[r, :] = adam(tables[r, :], tables_m[r, :], tables_v[r, :], grads[r, :], RATE_TABLES)
        return 0

    lax.fori_loop(0, rows // 8, table_rows, 0, unroll=7)
    for k in (4, 5, 6):
        send(k)
    nrows = vectors.shape[0]
    vm_out[...], vv_out[...], v_out[...] = adam(vectors[...], vectors_m[...], vectors_v[...], vector_grads[0:nrows, :], RATE_VECTORS)
    for k in (10, 11, 12):
        send(k)
    for copy in started:
        copy.wait()


def exchange(x, axis):
    n = lax.axis_size(axis)
    return [x] + [lax.ppermute(x, axis, [(i, i ^ k) for i in range(n)]) for k in range(1, n)]


def flip(x, k):
    n = lax.axis_size("dp")
    return lax.ppermute(x, "dp", [(i, i ^ k) for i in range(n)])


def after(values, *others):
    return lax.optimization_barrier((tuple(values), tuple(others)))[0]


def spread(x, second=()):
    four, one, two = flip(x, 4), flip(x, 1), flip(x, 2)
    (one,) = after([one], *second)
    (two,) = after([two], *second)
    (four,) = after([four], *second)
    return [x, one, two, flip(two, 1), four, flip(four, 1), flip(four, 2), flip(one, 6)]


def per_device(
    lap_vectors,
    eig_index,
    type_ids,
    seg_ids,
    targets,
    layer_weights,
    left_stats,
    right_stats,
    left_roots,
    right_roots,
    tables,
    tables_m,
    tables_v,
    head_weight,
    head_m,
    head_v,
    vectors,
    vectors_m,
    vectors_v,
):
    dp = lax.axis_size("dp")
    nmp = lax.axis_size("mp")
    length = seg_ids.shape[1]
    mols = targets.shape[1]
    width = vectors.shape[1]
    own, group_cols = layer_weights.shape[0], layer_weights.shape[1]
    cols = group_cols // 6
    heads = cols // HEAD_DIM
    scale = HEAD_DIM ** (-0.5)
    owners = FEATS // nmp // 8

    w = layer_weights.astype(BF)
    sources = [in_hbm(x) for x in (lap_vectors[0].T, eig_index[0].T, type_ids, seg_ids, tables, vectors)]
    at, normed, hats, invs = call(
        functools.partial(embed_kernel, mols),
        [sds((FEATS, length), BF), sds((length, width), BF), sds((length, width), BF), sds((length, 128), F32)],
        sources,
        [pltpu.VMEM(x.shape, x.dtype) for x in sources]
        + [pltpu.VMEM((FEATS, width), BF), pltpu.VMEM((FEATS, width), BF), pltpu.VMEM((8, length), I32), pltpu.SemaphoreType.DMA((6,))],
        flops=4 * length * FEATS * width,
        in_specs=[IN_PLACE] * 6,
    )
    direct = dp == 8 and own == 4 * mols and own % 16 == 0
    if direct:
        ones = spread(w, (normed,))
    else:
        ones = [lax.all_gather(w, "dp", axis=0, tiled=True)]
    np_ = len(ones)
    part, probs, values, ctx, keyed, query, w1, w2 = call(
        functools.partial(attn_kernel, np_, mols, heads, scale),
        [
            sds((mols, width), BF),
            sds((mols * heads, length), BF),
            sds((length, 256), BF),
            sds((mols, 256), BF),
            sds((width, 256), BF),
            sds((8, 256), F32),
            sds((width, 4 * cols), BF),
            sds((width, 2 * cols), BF),
        ],
        [normed, seg_ids, vectors, *ones],
        flops=4 * length * 256 * width,
    )
    part, resid_one, normed_two, hidden, act = call(
        functools.partial(ffn_kernel, nmp, cols),
        [
            sds((mols, width), BF),
            sds((mols, width), F32),
            sds((mols, width), BF),
            sds((mols, 256), F32),
            sds((mols, 256), BF),
        ],
        [*exchange(part, "mp"), vectors, w2],
        flops=4 * mols * width * 256,
    )
    part, pack, grad_pred, grad_two, grad_low, grad_hidden, head_rows = call(
        functools.partial(head_kernel, nmp, cols),
        [
            sds((mols, width), BF),
            sds((mols, width), BF),
            sds((mols, 128), F32),
            sds((mols, width), F32),
            sds((mols, width), BF),
            sds((mols, 256), BF),
            sds((8, width), F32),
        ],
        [*exchange(part, "mp"), resid_one, vectors, head_weight, targets, seg_ids, hidden, w2],
        [pltpu.VMEM((width, width), BF)],
        flops=4 * width * width * mols,
    )
    odd = lax.axis_index("dp") & 1
    high = dp // 2
    deep = (own + 15) // 16 * 16
    nlayer = 2 if own == deep else 1

    def halves(parts):
        if nlayer == 2:
            return parts
        both = parts[0].reshape(high, 2, own, -1)
        both = jnp.pad(both, ((0, 0), (0, 0), (0, deep - own), (0, 0)))
        return [lax.dynamic_index_in_dim(both, i, 1, False) for i in (odd, 1 - odd)]

    def half_shapes(lanes, number=1, more=0):
        return [sds((high * number + more, own // number, lanes), BF)] * 2 if nlayer == 2 else [sds((width, lanes), BF)]

    number = 2 if direct else 1
    parts = exchange(part, "mp")
    *ffn_parts, comb = call(
        functools.partial(ffn_grad_kernel, nlayer, high),
        half_shapes(384, number, number - 1) + [sds((256, width), BF)],
        [normed_two, grad_hidden, grad_low, act, pack, keyed],
        [pltpu.VMEM((width, 384), BF)],
        flops=4 * mols * width * 256,
    )
    ffn_keep, ffn_send = halves(ffn_parts)
    (ffn_send,) = after([ffn_send], *parts[1:])
    ffn_came = flip(ffn_send, 1)
    *layer_halves, side, key_rows, sides, extras = call(
        functools.partial(attn_back_kernel, nmp, nlayer, high, mols, heads, scale),
        half_shapes(384)
        + [sds((8, 256), F32), sds((8, width), F32), sds((256, length), BF), sds((16, width), F32)],
        [*parts, resid_one, grad_two, head_rows, vectors, probs, values, normed, w1, ctx],
        [pltpu.VMEM((width, 384), BF)],
        flops=4 * length * 256 * width,
    )
    layer_keep, layer_send = halves(layer_halves)
    layer_came = flip(layer_send, 1)
    shares = call(
        functools.partial(embed_back_kernel, nmp, mols),
        [sds((FEATS // nmp, width), BF) for _ in range(nmp)],
        [sides, comb, extras, vectors, hats, invs, at, seg_ids],
        [pltpu.VMEM((FEATS, width), F32), pltpu.VMEM((16, width), F32)],
        flops=4 * length * 256 * width,
    )
    moved = [shares[0]] + [lax.ppermute(shares[k], "mp", [(i, i ^ k) for i in range(nmp)]) for k in range(1, nmp)]
    table_keep, table_send = call(
        functools.partial(merge_table_kernel, nmp, owners, own, high),
        [sds((high, 32, 384), BF)] * 2,
        [*moved, side, key_rows, grad_pred],
        [pltpu.VMEM((FEATS // nmp, width), F32), pltpu.VMEM((dp, 8, 384), F32)],
    )
    (ffn_came,) = after([ffn_came], shares[0])
    if direct:
        near_keep, near_send, pair = call(
            ffn_x_kernel,
            [sds((2, own, 384), BF)] * 2 + [sds((2, 2 * mols, width // 2), BF)],
            [ffn_keep, ffn_came],
        )
        far_keep, far_send = call(
            ffn_z_kernel,
            [sds((2, own // 2, 384), BF), sds((4, own // 2, 384), BF)],
            [near_keep, flip(near_send, 2), pair],
        )
        ffn_parts = [far_keep, flip(far_send, 4)]
    else:
        ffn_parts = call(ffn_all_kernel, [sds((deep, 384), BF)] * high, [ffn_keep, ffn_came])
        ffn_parts = [ffn_parts[0]] + [flip(ffn_parts[k], 2 * k) for k in range(1, high)]
    merged = call(
        merge_kernel,
        [sds((deep + 32, 384), BF)] * high,
        [layer_keep, layer_came, table_keep, flip(table_send, 1)],
    )
    merged = [merged[0]] + [flip(merged[k], 2 * k) for k in range(1, high)]
    layer, send, scalars, preds = call(
        functools.partial(owner_kernel, own, cols, scale, dp),
        [sds((6, own, cols), F32), sds((dp, 16, 384), BF), sds((8, 128), F32), sds((8, 384), F32)],
        [*merged, *ffn_parts, query, vectors],
        flops=2 * own * 256 * 1024,
    )
    kept = [
        jnp.swapaxes(left_roots, 0, 1), right_roots[0], layer_weights, jnp.swapaxes(left_stats, 0, 1), right_stats[0],
        tables, tables_m, tables_v, head_weight, head_m, head_v, vectors, vectors_m, vectors_v,
    ]
    sums = lax.all_to_all(send, "dp", 0, 0, tiled=True)
    if direct:
        (far,) = after([ffn_parts[1]], scalars)
        (quad,) = call(quad_kernel, [sds((4, 2 * mols, 384), BF)], [pair, far])
        (came,) = after([flip(quad, 2)], sums)
        pieces = [quad, came]
    else:
        pieces = [jnp.pad(lax.all_gather(pack, "dp", axis=0), ((0, 0), (0, 32 - mols), (0, 0))).reshape(dp * 32, -1)]
        preds = jnp.pad(lax.all_gather(grad_pred, "dp", axis=0), ((0, 0), (0, 32 - mols), (0, 0))).reshape(dp * 32, -1)
    sums = exchange(sums, "mp")
    head_grad, head_square, *kept = call(
        functools.partial(outer_kernel, len(pieces), len(kept), 8),
        [sds((width, width), F32), sds((8, 128), F32)] + [pltpu.VMEM(x.shape, F32) for x in kept],
        [*pieces, preds, vectors, *[in_hbm(x) for x in kept]],
        [pltpu.VMEM((dp * 32, width), BF), pltpu.VMEM((width, width), BF), pltpu.SemaphoreType.DMA((len(kept),))],
        flops=4 * dp * mols * width * width,
        in_specs=[IN_VMEM] * (len(pieces) + 2) + [IN_PLACE] * len(kept),
        vmem=16 + dp // 4,
    )
    kept = [in_vmem(x) for x in kept]
    results = [
        sds((own, group_cols), F32),
        sds((own, group_cols), F32),
        sds((6, own, own), F32),
        sds((6, cols, cols), F32),
        *[sds(tables.shape, F32)] * 3,
        *[sds(head_weight.shape, F32)] * 3,
        *[sds(vectors.shape, F32)] * 3,
    ]
    outs = call(
        functools.partial(update_kernel, nmp, cols),
        [sds((1, 1), F32)] * 3 + results,
        [
            *sums, head_square, scalars, layer, *kept[:11], head_grad, *kept[11:],
        ],
        [pltpu.VMEM(x.shape, x.dtype) for x in results] + [pltpu.VMEM((FEATS, width), F32), pltpu.VMEM((16, width), F32), pltpu.VMEM((nmp, dp, 16, 384), BF), pltpu.SemaphoreType.DMA((34,))],
        flops=20 * width * width,
        vmem=24,
        out_specs=[IN_VMEM] * 3 + [IN_PLACE] * 13,
    )
    loss, count, norm, layer_grad, layer_new, left_new, right_new, tm, tv, tn, hm, hv, hn, vm, vv, vn = outs
    return (
        loss.reshape(()),
        count.reshape(()),
        norm.reshape(()),
        layer_grad,
        layer_new,
        jnp.swapaxes(left_new, 0, 1),
        right_new[None],
        tm,
        tv,
        tn,
        hm,
        hv,
        hn,
        vm,
        vv,
        vn,
    )


def solution(mesh):
    placed = (
        P("dp", None, None),
        P("dp", None, None),
        P("dp", None),
        P("dp", None),
        P("dp", None),
        P("dp", "mp"),
        P("dp", "mp", None),
        P("dp", "mp", None, None),
        P("dp", "mp", None),
        P("dp", "mp", None, None),
        *[P()] * 9,
    )
    return jax.shard_map(
        per_device,
        mesh=mesh,
        in_specs=placed,
        out_specs=(
            P(),
            P(),
            P(),
            P("dp", "mp"),
            P("dp", "mp"),
            P("dp", "mp", None),
            P("dp", "mp", None, None),
            *[P()] * 9,
        ),
        check_vma=False,
    )
```
